32 devices in a mesh: section: 4 (over y, x), expert: 4 (over z), mp: 2 (over core).
Axes of the slice: x: 2, y: 2, z: 4, core: 2. Of those that a mesh axis runs over, the one named last changes fastest.
Arguments:
- out_grad: bfloat16 [4, 512, 4096], P('section', 'expert', 'mp'), may hold values from -6 to 6
- expert_ids: int32 [4, 512, 2], P('section', 'expert'), may hold values from 0 to 3, all different within a row; in each aligned block of 128 rows (0 to 127, 128 to 255, ..., all dimensions but the last counted through in order) at most 128 rows name the same one
- gate_codes: int32 [4, 512, 2], P('section', 'expert'), may hold values from 1 to 255
- up_weight: bfloat16 [4, 4, 4096, 1024], P('section', 'expert', None, 'mp'), may hold values from -0.09375 to 0.09375
- down_weight: bfloat16 [4, 4, 1024, 4096], P('section', 'expert', 'mp'), may hold values from -0.1875 to 0.1875
- pre_act: bfloat16 [4, 4, 512, 1024], P('section', 'expert', None, 'mp'), may hold values from -6 to 6
- conv_grad: bfloat16 [4, 512, 4096], P('section', 'expert', 'mp'), may hold values from -6 to 6
- conv_input: bfloat16 [4, 512, 4096], P('section', 'expert', 'mp'), may hold values from -0.26367188 to 0.26367188
- conv_weight: float32 [4, 4, 4096], P('section', None, 'mp'), may hold values from -3 to 3
- in_proj: bfloat16 [4, 4096, 4096], P('section', 'expert', 'mp'), may hold values from -0.09375 to 0.09375
Outputs:
- residual_to_previous: bfloat16 [4, 512, 4096], P('section', 'expert', 'mp')
- kernel_grad: float32 [4, 4, 4096], P('section', None, 'mp')
The draws below stay inside these ranges and needn't reach their ends.
Inputs may be any that keep to these rules, and one draw needn't show every extreme that they name: `expert_ids`: each token names two different experts; in every section, the tokens of one block of 128 name no expert more than 128 times, a bound that some block reaches.
All inputs are finite; a program needn't handle non-finite values.
Results may differ from the reference program's by a relative error of at most 0.0044.
Values may be sent and summed in bfloat16 or wider, within the bound.
No kernel may reach another device: no remote copies, remote signals or barrier semaphores. Data moves between devices by JAX's collectives and lax.ppermute only.
A program may use at most 128 MiB of HBM per device.

```python
import math
import jax
import jax.numpy as jnp
import numpy as np
from jax import lax

D = 4096
FF = 1024
CH = 4096
KERNEL = 4
TOK_DEV = 128
TOKENS = 512
EXPERTS = 4
CAP = 128
SLOTS = 512
N_SECTION = 4
N_EXPERT = 4


def place_ends(array, rng, least, high):
    shape = array.shape
    spot = [jax.random.randint(jax.random.fold_in(rng, axis), (), 0, shape[axis]) for axis in range(len(shape))]
    array = array.at[tuple(spot)].set(least)
    longest = shape.index(max(shape))
    spot[longest] = (spot[longest] + 1) % shape[longest]
    return array.at[tuple(spot)].set(high)


def steps_of(key, dims, cuts, smallest, high):
    level, own = 1.0, jax.random.fold_in(key, 6)
    for position, shards_of in cuts:
        draws = jnp.exp(jax.random.uniform(jax.random.fold_in(own, position), (shards_of,), jnp.float32, smallest / len(cuts), high / len(cuts)))
        level = level * jnp.repeat(draws, dims[position] // shards_of).reshape([-1 if axis == position else 1 for axis in range(len(dims))])
    return level


def shared_out(own_key, own, number, rows, amount, top, reach, slope):
    order = jax.random.permutation(own_key, amount)
    crowded, common = shares(amount, rows * top, reach, slope, True), shares(amount, rows * top, reach, slope, False)
    places = jnp.arange(amount)

    def named(tallies, offset_by):
        used = int((tallies > 0).sum())
        fixed = max(1, used // 4)
        passed = fixed + (places - fixed + offset_by * (used - fixed)) % max(1, amount - fixed)
        return jnp.zeros((amount,), jnp.int32).at[order[jnp.where(places < fixed, places, passed)]].set(jnp.asarray(tallies, jnp.int32))

    tallies = jnp.where(number % 4 == 0, named(crowded, number // 4), named(common, number - number // 4 - 1))
    mixed = jax.random.permutation(jax.random.fold_in(own, 3), amount)
    source_of, receiver = mixed[0:amount // 2 * 2:2], mixed[1:amount // 2 * 2:2]
    room = jnp.minimum(tallies[source_of] - 1, reach - tallies[receiver]) // 2
    room = jnp.where((source_of == order[0]) | (receiver == order[0]) | (tallies[receiver] == 0), 0, jnp.maximum(room, 0))
    passed = jax.random.randint(jax.random.fold_in(own, 4), (amount // 2,), 0, 1 << 20) % (room + 1)
    tallies = tallies.at[source_of].add(-passed).at[receiver].add(passed)
    labels = jnp.searchsorted(jnp.cumsum(tallies), jnp.arange(rows * top), side="right").astype(jnp.int32)
    table = labels.reshape(top, rows).T
    table = table[jax.random.permutation(jax.random.fold_in(own, 1), rows)]
    offset_by = jax.random.randint(jax.random.fold_in(own, 2), (rows, 1), 0, top)
    return jnp.take_along_axis(table, (jnp.arange(top)[None, :] + offset_by) % top, axis=1)


def shares(amount, total, limit, skew, full):
    weights = [(1 << 20) // math.isqrt(grade ** skew) + 1 for grade in range(1, amount + 1)]
    largest = limit if full else min(limit, max(-(-total // amount), total * weights[0] // sum(weights)))
    least = 1 if total - largest >= amount - 1 else 0
    holding, surplus = [largest] + [least] * (amount - 1), total - largest - least * (amount - 1)
    while surplus > 0:
        free = [i for i in range(1, amount) if holding[i] < largest] or [i for i in range(1, amount) if holding[i] < limit]
        pool, left = sum([weights[i] for i in free]), surplus
        for i in free:
            addition = min(limit - holding[i], max(1, left * weights[i] // pool), surplus)
            holding[i] = holding[i] + addition
            surplus = surplus - addition
    return np.array(holding)


def normal_values(key, shape, deviation, reach, cuts=(), held_as=jnp.bfloat16):
    array = deviation * jax.random.normal(key, shape, jnp.float32)
    if cuts:
        array = array * steps_of(key, shape, cuts, -0.22, 0.18)
    return jnp.clip(array, -reach, reach).astype(held_as)


def setup_inputs(seed: int = 0) -> dict:
    arg_keys = jax.random.split(jax.random.key(seed), 11)
    out_grad = normal_values(arg_keys[0], (N_SECTION, TOKENS, D), 1.0, 6.0, ((0, 4), (1, 4), (2, 2)))
    expert_ids_keys = jax.random.split(jax.random.fold_in(arg_keys[1], 1), N_SECTION * TOKENS // TOK_DEV)
    expert_ids_turns = jax.random.permutation(jax.random.fold_in(arg_keys[1], 3), N_SECTION * TOKENS // TOK_DEV)
    expert_ids = jax.vmap(lambda own, number: shared_out(jax.random.fold_in(arg_keys[1], 2), own, number, TOK_DEV, EXPERTS, 2, CAP, 2))(expert_ids_keys, expert_ids_turns).reshape((N_SECTION, TOKENS, 2))
    gate_codes = place_ends(jax.random.randint(arg_keys[2], (N_SECTION, TOKENS, 2), 1, 256), jax.random.fold_in(arg_keys[2], 1), 1, 255).astype(jnp.int32)
    up_weight = normal_values(arg_keys[3], (N_SECTION, EXPERTS, D, FF), D ** -0.5, 0.09375, ((0, 4), (1, 4), (3, 2)))
    down_weight = normal_values(arg_keys[4], (N_SECTION, EXPERTS, FF, D), FF ** -0.5, 0.1875, ((0, 4), (1, 4), (2, 2)))
    pre_act = normal_values(arg_keys[5], (N_SECTION, EXPERTS, SLOTS, FF), 1.0, 6.0, ((0, 4), (1, 4), (3, 2)))
    conv_grad = normal_values(arg_keys[6], (N_SECTION, TOKENS, CH), 1.0, 6.0, ((0, 4), (1, 4), (2, 2)))
    conv_input = normal_values(arg_keys[7], (N_SECTION, TOKENS, CH), (1.0 / TOKENS ** 0.5), 0.26367188, ((0, 4), (1, 4), (2, 2)))
    conv_weight = normal_values(arg_keys[8], (N_SECTION, KERNEL, CH), 0.5, 3.0, ((0, 4), (2, 2)), jnp.float32)
    in_proj = normal_values(arg_keys[9], (N_SECTION, D, CH), CH ** -0.5, 0.09375, ((0, 4), (1, 4), (2, 2)))
    return {"out_grad": out_grad, "expert_ids": expert_ids, "gate_codes": gate_codes, "up_weight": up_weight, "down_weight": down_weight, "pre_act": pre_act, "conv_grad": conv_grad, "conv_input": conv_input, "conv_weight": conv_weight, "in_proj": in_proj}


def silu_slope(pre_value):
    sig = jax.nn.sigmoid(pre_value)
    return sig * (1.0 + pre_value * (1.0 - sig))


def slot_targets(route_ids):
    blocks = route_ids.reshape(N_EXPERT, TOK_DEV * 2)
    onehot = (blocks[:, :, None] == jnp.arange(EXPERTS, dtype=jnp.int32)[None, None, :]).astype(jnp.int32)
    before = jnp.cumsum(onehot, axis=1) - onehot
    rank = jnp.sum(before * onehot, axis=2)
    source = jnp.arange(N_EXPERT, dtype=jnp.int32)[:, None]
    return (source * CAP + rank).reshape(TOKENS * 2).astype(jnp.int32)


def section_moe(grad_rows, route_ids, codes, up_section, down_section, pre_section):
    gates = codes.astype(jnp.float32) / 256.0
    slots = slot_targets(route_ids)
    owners = route_ids.reshape(TOKENS * 2).astype(jnp.int32)
    scaled = (gates[:, :, None] * grad_rows.astype(jnp.float32)[:, None, :]).astype(jnp.bfloat16)
    scaled = scaled.reshape(TOKENS * 2, D)

    def one_expert(items):
        number, up_one, down_one, pre_one = items
        places = jnp.where(owners == number, slots, SLOTS)
        rows = jnp.zeros((SLOTS, D), jnp.bfloat16).at[places].set(scaled, mode="drop")
        hidden = jnp.dot(rows, down_one.T, preferred_element_type=jnp.float32)
        pre_grad = (hidden * silu_slope(pre_one.astype(jnp.float32))).astype(jnp.bfloat16)
        return jnp.dot(pre_grad, up_one.T, preferred_element_type=jnp.float32).astype(jnp.bfloat16)

    slot_grad = lax.map(one_expert, (jnp.arange(EXPERTS, dtype=jnp.int32), up_section, down_section, pre_section))
    picked = slot_grad[owners, slots].astype(jnp.float32).reshape(TOKENS, 2, D)
    return grad_rows.astype(jnp.float32) + picked[:, 0, :] + picked[:, 1, :]


def section_conv(grad_conv, input_conv, taps):
    grad_full = grad_conv.astype(jnp.float32)
    input_full = input_conv.astype(jnp.float32)
    padded_grad = jnp.pad(grad_full, ((0, KERNEL - 1), (0, 0)))
    result = jnp.zeros((TOKENS, CH), jnp.float32)
    for tap in range(KERNEL):
        start = KERNEL - 1 - tap
        result = result + taps[tap][None, :] * padded_grad[start:start + TOKENS]
    padded_input = jnp.pad(input_full, ((KERNEL - 1, 0), (0, 0)))
    tap_grads = jnp.stack([jnp.sum(grad_full * padded_input[tap:tap + TOKENS], axis=0) for tap in range(KERNEL)])
    return result.astype(jnp.bfloat16), tap_grads


def reference(out_grad, expert_ids, gate_codes, up_weight, down_weight, pre_act, conv_grad, conv_input, conv_weight, in_proj):
    residuals = []
    kernels = []
    for section_index in range(N_SECTION):
        moe_total = section_moe(out_grad[section_index], expert_ids[section_index], gate_codes[section_index], up_weight[section_index], down_weight[section_index], pre_act[section_index])
        input_grad, tap_grads = section_conv(conv_grad[section_index], conv_input[section_index], conv_weight[section_index])
        proj_grad = jnp.dot(input_grad, in_proj[section_index].T, preferred_element_type=jnp.float32)
        residuals.append((moe_total + proj_grad).astype(jnp.bfloat16))
        kernels.append(tap_grads)
    residuals = residuals[1:] + [jnp.zeros((TOKENS, D), jnp.bfloat16)]
    return jnp.stack(residuals), jnp.stack(kernels)
```

```python
import jax
import jax.numpy as jnp
from jax import lax
from jax.sharding import PartitionSpec as P


def shifted(array, axis, by):
    size = lax.axis_size(axis)
    pairs = [(i, i + by) for i in range(size) if 0 <= i + by < size]
    return lax.ppermute(array, axis, pairs)


def silu_slope(pre_value):
    sig = jax.nn.sigmoid(pre_value)
    return sig * (1.0 + pre_value * (1.0 - sig))


def gated_rows(gates, rows, tok_rows):
    scaled = (gates[:, :, None] * rows.astype(jnp.float32)[:, None, :]).astype(jnp.bfloat16)
    return scaled.reshape(tok_rows * 2, rows.shape[1])


def fill_buffer(scaled, target, experts, capacity):
    width = scaled.shape[1]
    buffer = jnp.zeros((experts * capacity, width), jnp.bfloat16).at[target].set(scaled)
    return buffer.reshape(experts, capacity, width)


def slot_plan(
    out_grad,
    expert_ids,
    gate_codes,
    up_weight,
    down_weight,
    pre_act,
    conv_grad,
    conv_input,
    conv_weight,
    in_proj,
):
    grad_rows = out_grad[0]
    route_ids = expert_ids[0]
    tok_rows = grad_rows.shape[0]
    experts = lax.axis_size("expert")
    capacity = pre_act.shape[2] // experts
    gates = gate_codes[0].astype(jnp.float32) / 256.0
    flat_ids = route_ids.reshape(tok_rows * 2)
    onehot = (flat_ids[:, None] == jnp.arange(experts, dtype=jnp.int32)[None, :]).astype(jnp.int32)
    before = jnp.cumsum(onehot, axis=0) - onehot
    position = jnp.sum(before * onehot, axis=1)
    target = flat_ids * capacity + position
    whole_rows = lax.all_gather(grad_rows, "mp", axis=1, tiled=True)
    buffer = fill_buffer(gated_rows(gates, whole_rows, tok_rows), target, experts, capacity)
    arrived = lax.all_to_all(buffer, "expert", split_axis=0, concat_axis=0, tiled=True)
    slot_rows = arrived.reshape(experts * capacity, whole_rows.shape[1])
    w_down = down_weight[0, 0]
    w_up = up_weight[0, 0]
    pre_slots = pre_act[0, 0].astype(jnp.float32)
    hidden = lax.dot_general(
        slot_rows, w_down, (((1,), (1,)), ((), ())), preferred_element_type=jnp.float32
    )
    pre_grad = (hidden * silu_slope(pre_slots)).astype(jnp.bfloat16)
    partial_value = lax.dot_general(
        pre_grad, w_up, (((1,), (1,)), ((), ())), preferred_element_type=jnp.float32
    )
    share = lax.psum_scatter(partial_value, "mp", scatter_dimension=1, tiled=True).astype(
        jnp.bfloat16
    )
    returned = lax.all_to_all(
        share.reshape(experts, capacity, share.shape[1]),
        "expert",
        split_axis=0,
        concat_axis=0,
        tiled=True,
    )
    picked = returned.reshape(experts * capacity, grad_rows.shape[1])[target]
    picked = picked.astype(jnp.float32).reshape(tok_rows, 2, grad_rows.shape[1])
    moe_total = grad_rows.astype(jnp.float32) + picked[:, 0, :] + picked[:, 1, :]
    grads_here = conv_grad[0]
    inputs_here = conv_input[0]
    taps = conv_weight[0]
    kernel_size = taps.shape[0]
    next_rows = shifted(grads_here[: kernel_size - 1], "expert", -1)
    prev_rows = shifted(inputs_here[tok_rows - kernel_size + 1 :], "expert", 1)
    grad_ext = jnp.concatenate([grads_here, next_rows], axis=0).astype(jnp.float32)
    input_ext = jnp.concatenate([prev_rows, inputs_here], axis=0).astype(jnp.float32)
    grad_local = grads_here.astype(jnp.float32)
    conv_result = jnp.zeros(grads_here.shape, jnp.float32)
    tap_terms = []
    for tap in range(kernel_size):
        start = kernel_size - 1 - tap
        conv_result = conv_result + taps[tap][None, :] * grad_ext[start : start + tok_rows]
        tap_terms.append(jnp.sum(grad_local * input_ext[tap : tap + tok_rows], axis=0))
    input_grad = conv_result.astype(jnp.bfloat16)
    tap_grads = lax.psum(jnp.stack(tap_terms), "expert")
    w_proj = in_proj[0]
    proj_partial = lax.dot_general(
        input_grad,
        lax.all_gather(w_proj, "expert", axis=0, tiled=True),
        (((1,), (1,)), ((), ())),
        preferred_element_type=jnp.float32,
    )
    proj_share = lax.psum_scatter(proj_partial, "mp", scatter_dimension=1, tiled=True)
    residual = (moe_total + proj_share).astype(jnp.bfloat16)
    sent_residual = shifted(residual, "section", -1)
    return (sent_residual[None], tap_grads[None])


def token_plan(
    out_grad,
    expert_ids,
    gate_codes,
    up_weight,
    down_weight,
    pre_act,
    conv_grad,
    conv_input,
    conv_weight,
    in_proj,
):
    experts = lax.axis_size("expert")
    halves = lax.axis_size("mp")
    me = lax.axis_index("expert")
    grad_rows = out_grad[0]
    tok_rows, half_width = grad_rows.shape
    tokens = experts * tok_rows
    width = halves * half_width

    pairs = (expert_ids[0] * 256 + gate_codes[0]).T
    rows_here = lax.all_gather(grad_rows, "expert", axis=0, tiled=True)
    all_rows = lax.all_gather(rows_here, "mp", axis=1, tiled=True)
    all_pairs = lax.all_gather(pairs, "expert", axis=0)
    all_conv = lax.all_gather(conv_grad[0], "expert", axis=0, tiled=True)

    named = (all_pairs // 256 == me).astype(jnp.int32)
    codes = jnp.sum(named * (all_pairs % 256), axis=1)
    named = jnp.sum(named, axis=1)
    gates = codes.reshape(tokens).astype(jnp.float32) / 256.0
    earlier = jnp.triu(jnp.ones((tok_rows, tok_rows), jnp.bfloat16), 1)
    rank = jnp.dot(named.astype(jnp.bfloat16), earlier, preferred_element_type=jnp.float32)
    rank = jnp.where(named == 1, rank.astype(jnp.int32), -1)
    pick = (rank[:, :, None] == jnp.arange(tok_rows, dtype=jnp.int32)).astype(jnp.bfloat16)
    pre_blocks = pre_act[0, 0].reshape(experts, tok_rows, pre_act.shape[3])
    pre_tokens = jnp.einsum("bts,bsf->btf", pick, pre_blocks, preferred_element_type=jnp.float32)
    slope = silu_slope(pre_tokens.reshape(tokens, pre_act.shape[3]))

    dispatched = (gates[:, None] * all_rows.astype(jnp.float32)).astype(jnp.bfloat16)
    hidden = lax.dot_general(
        dispatched, down_weight[0, 0], (((1,), (1,)), ((), ())), preferred_element_type=jnp.float32
    )
    pre_grad = (hidden * slope).astype(jnp.bfloat16)
    partial = lax.dot_general(
        pre_grad, up_weight[0, 0], (((1,), (1,)), ((), ())), preferred_element_type=jnp.float32
    )

    taps = conv_weight[0]
    kernel_size = taps.shape[0]
    padded = jnp.pad(all_conv, ((0, kernel_size - 1), (0, 0)))
    window = lax.dynamic_slice_in_dim(padded, me * tok_rows, tok_rows + kernel_size - 1, 0)
    window = window.astype(jnp.float32)
    inputs_here = conv_input[0].astype(jnp.float32)
    conv_result = jnp.zeros((tokens, half_width), jnp.float32)
    tap_terms = []
    for tap in range(kernel_size):
        start = kernel_size - 1 - tap
        conv_result = conv_result + taps[tap][None, :] * padded[start : start + tokens].astype(jnp.float32)
        tap_terms.append(jnp.sum(inputs_here * window[start : start + tok_rows], axis=0))
    tap_grads = lax.psum(jnp.stack(tap_terms), "expert")
    proj = lax.dot_general(
        conv_result.astype(jnp.bfloat16),
        in_proj[0],
        (((1,), (1,)), ((), ())),
        preferred_element_type=jnp.float32,
    )
    block = width // experts
    columns = partial.reshape(tokens, experts, block)
    mine = (jnp.arange(experts) == me)[None, :, None]
    total = columns + jnp.where(mine, proj[:, None, :], 0.0)
    total = total.reshape(experts, tok_rows, halves, half_width).transpose(0, 2, 1, 3)
    total = total.reshape(experts * halves, tok_rows, half_width).astype(jnp.bfloat16)
    share = lax.psum_scatter(total, ("expert", "mp"), scatter_dimension=0, tiled=False)
    residual = (grad_rows.astype(jnp.float32) + share.astype(jnp.float32)).astype(jnp.bfloat16)
    return (shifted(residual, "section", -1)[None], tap_grads[None])


def shards(*arrays):
    tok_rows, capacity = arrays[0].shape[1], arrays[5].shape[2] // lax.axis_size("expert")
    return (token_plan if capacity == tok_rows else slot_plan)(*arrays)


def solution(mesh):
    in_specs = (
        P("section", "expert", "mp"),
        P("section", "expert", None),
        P("section", "expert", None),
        P("section", "expert", None, "mp"),
        P("section", "expert", "mp", None),
        P("section", "expert", None, "mp"),
        P("section", "expert", "mp"),
        P("section", "expert", "mp"),
        P("section", None, "mp"),
        P("section", "expert", "mp"),
    )
    out_specs = (P("section", "expert", "mp"), P("section", None, "mp"))
    return jax.shard_map(shards, mesh=mesh, in_specs=in_specs, out_specs=out_specs, check_vma=False)
```

```python
import functools

import jax
import jax.numpy as jnp
from jax import lax
from jax.experimental import pallas as pl
from jax.experimental.pallas import tpu as pltpu
from jax.sharding import PartitionSpec as P


def shifted(array, axis, by):
    size = lax.axis_size(axis)
    pairs = [(i, i + by) for i in range(size) if 0 <= i + by < size]
    return lax.ppermute(array, axis, pairs)


def silu_slope(pre_value):
    sig = jax.nn.sigmoid(pre_value)
    return sig * (1.0 + pre_value * (1.0 - sig))


def gated_rows(gates, rows, tok_rows):
    scaled = (gates[:, :, None] * rows.astype(jnp.float32)[:, None, :]).astype(jnp.bfloat16)
    return scaled.reshape(tok_rows * 2, rows.shape[1])


def fill_buffer(scaled, target, experts, capacity):
    width = scaled.shape[1]
    buffer = jnp.zeros((experts * capacity, width), jnp.bfloat16).at[target].set(scaled)
    return buffer.reshape(experts, capacity, width)


def slot_plan(
    out_grad,
    expert_ids,
    gate_codes,
    up_weight,
    down_weight,
    pre_act,
    conv_grad,
    conv_input,
    conv_weight,
    in_proj,
):
    grad_rows = out_grad[0]
    route_ids = expert_ids[0]
    tok_rows = grad_rows.shape[0]
    experts = lax.axis_size("expert")
    capacity = pre_act.shape[2] // experts
    gates = gate_codes[0].astype(jnp.float32) / 256.0
    flat_ids = route_ids.reshape(tok_rows * 2)
    onehot = (flat_ids[:, None] == jnp.arange(experts, dtype=jnp.int32)[None, :]).astype(jnp.int32)
    before = jnp.cumsum(onehot, axis=0) - onehot
    position = jnp.sum(before * onehot, axis=1)
    target = flat_ids * capacity + position
    whole_rows = lax.all_gather(grad_rows, "mp", axis=1, tiled=True)
    buffer = fill_buffer(gated_rows(gates, whole_rows, tok_rows), target, experts, capacity)
    arrived = lax.all_to_all(buffer, "expert", split_axis=0, concat_axis=0, tiled=True)
    slot_rows = arrived.reshape(experts * capacity, whole_rows.shape[1])
    w_down = down_weight[0, 0]
    w_up = up_weight[0, 0]
    pre_slots = pre_act[0, 0].astype(jnp.float32)
    hidden = lax.dot_general(
        slot_rows, w_down, (((1,), (1,)), ((), ())), preferred_element_type=jnp.float32
    )
    pre_grad = (hidden * silu_slope(pre_slots)).astype(jnp.bfloat16)
    partial_value = lax.dot_general(
        pre_grad, w_up, (((1,), (1,)), ((), ())), preferred_element_type=jnp.float32
    )
    share = lax.psum_scatter(partial_value, "mp", scatter_dimension=1, tiled=True).astype(
        jnp.bfloat16
    )
    returned = lax.all_to_all(
        share.reshape(experts, capacity, share.shape[1]),
        "expert",
        split_axis=0,
        concat_axis=0,
        tiled=True,
    )
    picked = returned.reshape(experts * capacity, grad_rows.shape[1])[target]
    picked = picked.astype(jnp.float32).reshape(tok_rows, 2, grad_rows.shape[1])
    moe_total = grad_rows.astype(jnp.float32) + picked[:, 0, :] + picked[:, 1, :]
    grads_here = conv_grad[0]
    inputs_here = conv_input[0]
    taps = conv_weight[0]
    kernel_size = taps.shape[0]
    next_rows = shifted(grads_here[: kernel_size - 1], "expert", -1)
    prev_rows = shifted(inputs_here[tok_rows - kernel_size + 1 :], "expert", 1)
    grad_ext = jnp.concatenate([grads_here, next_rows], axis=0).astype(jnp.float32)
    input_ext = jnp.concatenate([prev_rows, inputs_here], axis=0).astype(jnp.float32)
    grad_local = grads_here.astype(jnp.float32)
    conv_result = jnp.zeros(grads_here.shape, jnp.float32)
    tap_terms = []
    for tap in range(kernel_size):
        start = kernel_size - 1 - tap
        conv_result = conv_result + taps[tap][None, :] * grad_ext[start : start + tok_rows]
        tap_terms.append(jnp.sum(grad_local * input_ext[tap : tap + tok_rows], axis=0))
    input_grad = conv_result.astype(jnp.bfloat16)
    tap_grads = lax.psum(jnp.stack(tap_terms), "expert")
    w_proj = in_proj[0]
    proj_partial = lax.dot_general(
        input_grad,
        lax.all_gather(w_proj, "expert", axis=0, tiled=True),
        (((1,), (1,)), ((), ())),
        preferred_element_type=jnp.float32,
    )
    proj_share = lax.psum_scatter(proj_partial, "mp", scatter_dimension=1, tiled=True)
    residual = (moe_total + proj_share).astype(jnp.bfloat16)
    sent_residual = shifted(residual, "section", -1)
    return (sent_residual[None], tap_grads[None])


F32, BF16 = jnp.float32, jnp.bfloat16
VMEM_LIMIT = 40 * 1024 * 1024
NT = (((1,), (1,)), ((), ()))
TN = (((0,), (0,)), ((), ()))


def whole(memory=pltpu.VMEM):
    return pl.BlockSpec(memory_space=memory)


def rotated(array, axis, by):
    size = lax.axis_size(axis)
    return lax.ppermute(array, axis, [(i, (i + by) % size) for i in range(size)])


def around(array):
    return [array] + [rotated(array, "expert", k) for k in range(1, lax.axis_size("expert"))]


def doubling_sum(array, axis):
    size, step = lax.axis_size(axis), 1
    while step < size:
        array = array + lax.ppermute(array, axis, [(i, i ^ step) for i in range(size)])
        step *= 2
    return array


def expert_kernel(steps, place, *refs):
    experts = len(refs) - 8
    pairs = refs[:experts]
    rows, down, up, pre, out, gates, slope, hidden = refs[experts:]
    tok_rows = pre.shape[0] // experts
    me, step = place[0], pl.program_id(0)

    @pl.when(step == 0)
    def _():
        row = lax.broadcasted_iota(jnp.int32, (tok_rows, tok_rows), 0)
        column = lax.broadcasted_iota(jnp.int32, (tok_rows, tok_rows), 1)

        def upright(line):
            return jnp.sum(jnp.where(row == column, line, 0.0), axis=1, keepdims=True)

        for k in range(experts):
            at = pl.ds(pl.multiple_of(lax.rem(me - k + experts, experts) * tok_rows, tok_rows), tok_rows)
            pair = pairs[k][...]
            named = (pair // 256) == me
            code = jnp.sum(jnp.where(named, (pair % 256).astype(F32), 0.0), axis=0, keepdims=True)
            named = jnp.sum(jnp.where(named, 1.0, 0.0), axis=0, keepdims=True)
            gates[at, :] = upright(code) / 256.0
            rank = jnp.sum(jnp.where(row < column, upright(named), 0.0), axis=0, keepdims=True)
            pick = jnp.where(rank.astype(jnp.int32) == row, named, 0.0).astype(BF16)
            p = lax.dot_general(pick, pre[at, :], TN, preferred_element_type=F32)
            q = 1.0 / (1.0 + jnp.exp(-p))
            slope[at, :] = q * (1.0 + p * (1.0 - q))
        hidden[...] = jnp.zeros_like(hidden)

    @pl.when(step < steps)
    def _():
        values = rows[...].reshape(experts * tok_rows, rows.shape[-1]).astype(F32)
        scaled = (gates[...] * values).astype(BF16)
        hidden[...] += lax.dot_general(scaled, down[...], NT, preferred_element_type=F32)

    @pl.when(step >= steps)
    def _():
        pre_grad = (hidden[...] * slope[...]).astype(BF16)
        result = lax.dot_general(pre_grad, up[...], NT, preferred_element_type=F32)
        out[...] = result.astype(BF16).reshape(out.shape)


def expert_sums(place, pairs, rows, down, up, pre):
    experts, halves, tok_rows, half_width = rows.shape
    units, width = down.shape
    tokens = experts * tok_rows
    chunk = half_width // 2
    per_half = half_width // chunk
    steps = width // chunk

    def first(i):
        return jnp.minimum(i, steps - 1)

    def second(i):
        return jnp.maximum(i - steps, 0)

    block = (experts, 1, tok_rows, chunk)
    return pl.pallas_call(
        functools.partial(expert_kernel, steps),
        grid=(2 * steps,),
        in_specs=[whole(pltpu.SMEM)]
        + [whole()] * experts
        + [
            pl.BlockSpec(block, lambda i: (0, first(i) // per_half, 0, first(i) % per_half)),
            pl.BlockSpec((units, chunk), lambda i: (0, first(i))),
            pl.BlockSpec((chunk, units), lambda i: (second(i), 0)),
            whole(),
        ],
        out_specs=pl.BlockSpec(block, lambda i: (0, second(i) // per_half, 0, second(i) % per_half)),
        out_shape=jax.ShapeDtypeStruct(rows.shape, BF16),
        scratch_shapes=[
            pltpu.VMEM((tokens, 1), F32),
            pltpu.VMEM((tokens, units), F32),
            pltpu.VMEM((tokens, units), F32),
        ],
        compiler_params=pltpu.CompilerParams(vmem_limit_bytes=VMEM_LIMIT),
        cost_estimate=pl.CostEstimate(
            flops=4 * tokens * width * units, bytes_accessed=8 * width * units + 4 * tokens * width, transcendentals=0
        ),
        name="experts",
    )(place, *pairs, rows, down, up, pre)


def proj_kernel(place, *refs):
    experts = len(refs) - 8
    grads = refs[:experts]
    inputs, taps, weight, keep, send, tap_out, ext, total = refs[experts:]
    tok_rows, chunk = inputs.shape
    tokens = experts * tok_rows
    kernel_size = taps.shape[0]
    me, half, step = place[0], place[1], pl.program_id(0)

    for k in range(experts):
        at = pl.ds(pl.multiple_of(lax.rem(me - k + experts, experts) * tok_rows, tok_rows), tok_rows)
        ext[at, :] = grads[k][...].astype(F32)
    ext[tokens:, :] = jnp.zeros((ext.shape[0] - tokens, chunk), F32)

    tap = taps[...]
    result = jnp.zeros((tokens, chunk), F32)
    for j in range(kernel_size):
        start = kernel_size - 1 - j
        result = result + tap[j : j + 1, :] * ext[start : start + tokens, :]
    window = ext[pl.ds(pl.multiple_of(me * tok_rows, tok_rows), tok_rows + 8), :]
    values = inputs[...].astype(F32)
    for j in range(kernel_size):
        start = kernel_size - 1 - j
        tap_out[j : j + 1, :] = jnp.sum(values * window[start : start + tok_rows, :], axis=0, keepdims=True)

    product = lax.dot_general(result.astype(BF16), weight[...], NT, preferred_element_type=F32)

    @pl.when(step == 0)
    def _():
        total[...] = product

    @pl.when(step > 0)
    def _():
        total[...] += product

    @pl.when(step == pl.num_programs(0) - 1)
    def _():
        part = keep.shape[1]
        keep[...] = total[:, pl.ds(pl.multiple_of(half * part, part), part)]
        send[...] = total[:, pl.ds(pl.multiple_of((1 - half) * part, part), part)].astype(BF16)


def proj_sums(place, grads, inputs, taps, weight):
    experts = len(grads)
    tok_rows, half_width = inputs.shape
    block = weight.shape[0]
    part = block // 2
    tokens = experts * tok_rows
    chunk = half_width // 4

    def wide(rows):
        return pl.BlockSpec((rows, chunk), lambda i: (0, i))

    return pl.pallas_call(
        proj_kernel,
        grid=(half_width // chunk,),
        in_specs=[whole(pltpu.SMEM)]
        + [wide(tok_rows)] * (experts + 1)
        + [wide(taps.shape[0]), wide(block)],
        out_specs=[
            pl.BlockSpec((tokens, part), lambda i: (0, 0)),
            pl.BlockSpec((tokens, part), lambda i: (0, 0)),
            wide(taps.shape[0]),
        ],
        out_shape=[
            jax.ShapeDtypeStruct((tokens, part), F32),
            jax.ShapeDtypeStruct((tokens, part), BF16),
            jax.ShapeDtypeStruct(taps.shape, F32),
        ],
        scratch_shapes=[pltpu.VMEM((tokens + 8, chunk), F32), pltpu.VMEM((tokens, block), F32)],
        compiler_params=pltpu.CompilerParams(vmem_limit_bytes=VMEM_LIMIT),
        cost_estimate=pl.CostEstimate(
            flops=2 * tokens * half_width * block,
            bytes_accessed=2 * (block + tokens) * half_width + 6 * tokens * part,
            transcendentals=0,
        ),
        name="projection",
    )(place, *grads, inputs, taps, weight)


def final_kernel(place, grad, share, *refs):
    pieces, out = refs[:-1], refs[-1]
    count, part = len(pieces), pieces[0].shape[1]
    for r in range(count):
        at = pl.ds(pl.multiple_of(lax.rem(place[0] - r + count, count) * part, part), part)
        value = grad[:, at].astype(F32) + share[:, at].astype(F32) + pieces[r][...].astype(F32)
        out[:, at] = value.astype(BF16)


def final_sum(place, grad, share, pieces):
    return pl.pallas_call(
        final_kernel,
        in_specs=[whole(pltpu.SMEM)] + [whole()] * (2 + len(pieces)),
        out_specs=whole(),
        out_shape=jax.ShapeDtypeStruct(grad.shape, BF16),
        compiler_params=pltpu.CompilerParams(vmem_limit_bytes=VMEM_LIMIT),
        cost_estimate=pl.CostEstimate(flops=2 * grad.size, bytes_accessed=8 * grad.size, transcendentals=0),
        name="residual",
    )(place, grad, share, *pieces)


def returned_pieces(keep, received, me, half):
    experts, halves = lax.axis_size("expert"), lax.axis_size("mp")
    tok_rows = keep.shape[0] // experts
    pieces = []
    for r in range(experts):
        owner = (2 * (me % 2) + half + r) % experts
        at = owner * tok_rows
        piece = lax.dynamic_slice_in_dim(keep, at, tok_rows, 0)
        piece = piece + lax.dynamic_slice_in_dim(received, at, tok_rows, 0).astype(F32)
        pairs = []
        for e in range(experts):
            for m in range(halves):
                pairs.append((e * halves + m, (2 * (e % 2) + m + r) % experts * halves + e // 2))
        pieces.append(lax.ppermute(piece.astype(BF16), ("expert", "mp"), pairs))
    return pieces


def token_plan(
    out_grad,
    expert_ids,
    gate_codes,
    up_weight,
    down_weight,
    pre_act,
    conv_grad,
    conv_input,
    conv_weight,
    in_proj,
):
    me, half = lax.axis_index("expert"), lax.axis_index("mp")
    place = jnp.stack([me, half]).astype(jnp.int32)
    grad_rows = out_grad[0]
    experts, halves = lax.axis_size("expert"), lax.axis_size("mp")
    tok_rows, half_width = grad_rows.shape

    rows = lax.all_gather(grad_rows, ("expert", "mp"), axis=0)
    rows = rows.reshape(experts, halves, tok_rows, half_width)
    pairs = around((expert_ids[0] * 256 + gate_codes[0]).T)
    grads = around(conv_grad[0])
    sums = expert_sums(place, pairs, rows, down_weight[0, 0], up_weight[0, 0], pre_act[0, 0])
    sums = sums.reshape(experts * halves, tok_rows, half_width)
    share = lax.psum_scatter(sums, ("expert", "mp"), scatter_dimension=0, tiled=False)

    keep, send, tap_terms = proj_sums(place, grads, conv_input[0], conv_weight[0], in_proj[0])
    received = rotated(send, "mp", 1)
    pieces = returned_pieces(keep, received, me, half)
    tap_grads = doubling_sum(tap_terms, "expert")
    residual = final_sum(place, grad_rows, share, pieces)
    return (shifted(residual, "section", -1)[None], tap_grads[None])


def shards(*arrays):
    experts, halves = lax.axis_size("expert"), lax.axis_size("mp")
    capacity = arrays[5].shape[2] // experts
    dense = capacity == arrays[0].shape[1] and experts == 4 and halves == 2
    return (token_plan if dense else slot_plan)(*arrays)


def solution(mesh):
    in_specs = (
        P("section", "expert", "mp"),
        P("section", "expert", None),
        P("section", "expert", None),
        P("section", "expert", None, "mp"),
        P("section", "expert", "mp", None),
        P("section", "expert", None, "mp"),
        P("section", "expert", "mp"),
        P("section", "expert", "mp"),
        P("section", None, "mp"),
        P("section", "expert", "mp"),
    )
    out_specs = (P("section", "expert", "mp"), P("section", None, "mp"))
    return jax.shard_map(shards, mesh=mesh, in_specs=in_specs, out_specs=out_specs, check_vma=False)
```

```python
import functools

import jax
import jax.numpy as jnp
from jax import lax
from jax.experimental import pallas as pl
from jax.experimental.pallas import tpu as pltpu
from jax.sharding import PartitionSpec as P


def shifted(array, axis, by):
    size = lax.axis_size(axis)
    pairs = [(i, i + by) for i in range(size) if 0 <= i + by < size]
    return lax.ppermute(array, axis, pairs)


def silu_slope(pre_value):
    sig = jax.nn.sigmoid(pre_value)
    return sig * (1.0 + pre_value * (1.0 - sig))


def gated_rows(gates, rows, tok_rows):
    scaled = (gates[:, :, None] * rows.astype(jnp.float32)[:, None, :]).astype(jnp.bfloat16)
    return scaled.reshape(tok_rows * 2, rows.shape[1])


def fill_buffer(scaled, target, experts, capacity):
    width = scaled.shape[1]
    buffer = jnp.zeros((experts * capacity, width), jnp.bfloat16).at[target].set(scaled)
    return buffer.reshape(experts, capacity, width)


def slot_plan(
    out_grad,
    expert_ids,
    gate_codes,
    up_weight,
    down_weight,
    pre_act,
    conv_grad,
    conv_input,
    conv_weight,
    in_proj,
):
    grad_rows = out_grad[0]
    route_ids = expert_ids[0]
    tok_rows = grad_rows.shape[0]
    experts = lax.axis_size("expert")
    capacity = pre_act.shape[2] // experts
    gates = gate_codes[0].astype(jnp.float32) / 256.0
    flat_ids = route_ids.reshape(tok_rows * 2)
    onehot = (flat_ids[:, None] == jnp.arange(experts, dtype=jnp.int32)[None, :]).astype(jnp.int32)
    before = jnp.cumsum(onehot, axis=0) - onehot
    position = jnp.sum(before * onehot, axis=1)
    target = flat_ids * capacity + position
    whole_rows = lax.all_gather(grad_rows, "mp", axis=1, tiled=True)
    buffer = fill_buffer(gated_rows(gates, whole_rows, tok_rows), target, experts, capacity)
    arrived = lax.all_to_all(buffer, "expert", split_axis=0, concat_axis=0, tiled=True)
    slot_rows = arrived.reshape(experts * capacity, whole_rows.shape[1])
    w_down = down_weight[0, 0]
    w_up = up_weight[0, 0]
    pre_slots = pre_act[0, 0].astype(jnp.float32)
    hidden = lax.dot_general(
        slot_rows, w_down, (((1,), (1,)), ((), ())), preferred_element_type=jnp.float32
    )
    pre_grad = (hidden * silu_slope(pre_slots)).astype(jnp.bfloat16)
    partial_value = lax.dot_general(
        pre_grad, w_up, (((1,), (1,)), ((), ())), preferred_element_type=jnp.float32
    )
    share = lax.psum_scatter(partial_value, "mp", scatter_dimension=1, tiled=True).astype(
        jnp.bfloat16
    )
    returned = lax.all_to_all(
        share.reshape(experts, capacity, share.shape[1]),
        "expert",
        split_axis=0,
        concat_axis=0,
        tiled=True,
    )
    picked = returned.reshape(experts * capacity, grad_rows.shape[1])[target]
    picked = picked.astype(jnp.float32).reshape(tok_rows, 2, grad_rows.shape[1])
    moe_total = grad_rows.astype(jnp.float32) + picked[:, 0, :] + picked[:, 1, :]
    grads_here = conv_grad[0]
    inputs_here = conv_input[0]
    taps = conv_weight[0]
    kernel_size = taps.shape[0]
    next_rows = shifted(grads_here[: kernel_size - 1], "expert", -1)
    prev_rows = shifted(inputs_here[tok_rows - kernel_size + 1 :], "expert", 1)
    grad_ext = jnp.concatenate([grads_here, next_rows], axis=0).astype(jnp.float32)
    input_ext = jnp.concatenate([prev_rows, inputs_here], axis=0).astype(jnp.float32)
    grad_local = grads_here.astype(jnp.float32)
    conv_result = jnp.zeros(grads_here.shape, jnp.float32)
    tap_terms = []
    for tap in range(kernel_size):
        start = kernel_size - 1 - tap
        conv_result = conv_result + taps[tap][None, :] * grad_ext[start : start + tok_rows]
        tap_terms.append(jnp.sum(grad_local * input_ext[tap : tap + tok_rows], axis=0))
    input_grad = conv_result.astype(jnp.bfloat16)
    tap_grads = lax.psum(jnp.stack(tap_terms), "expert")
    w_proj = in_proj[0]
    proj_partial = lax.dot_general(
        input_grad,
        lax.all_gather(w_proj, "expert", axis=0, tiled=True),
        (((1,), (1,)), ((), ())),
        preferred_element_type=jnp.float32,
    )
    proj_share = lax.psum_scatter(proj_partial, "mp", scatter_dimension=1, tiled=True)
    residual = (moe_total + proj_share).astype(jnp.bfloat16)
    sent_residual = shifted(residual, "section", -1)
    return (sent_residual[None], tap_grads[None])


F32, BF16 = jnp.float32, jnp.bfloat16
VMEM_LIMIT = 40 * 1024 * 1024
HEAD = 16
NT = (((1,), (1,)), ((), ()))
TN = (((0,), (0,)), ((), ()))


def whole(memory=pltpu.VMEM):
    return pl.BlockSpec(memory_space=memory)


def rotated(array, axis, by):
    size = lax.axis_size(axis)
    return lax.ppermute(array, axis, [(i, (i + by) % size) for i in range(size)])


def around(array):
    return [array] + [rotated(array, "expert", k) for k in range(1, lax.axis_size("expert"))]


def doubling_sum(array, axis):
    size, step = lax.axis_size(axis), 1
    while step < size:
        array = array + lax.ppermute(array, axis, [(i, i ^ step) for i in range(size)])
        step *= 2
    return array


def expert_kernel(count, place, *refs):
    pairs, mine, other = refs[:count], refs[count : 2 * count], refs[2 * count : 3 * count]
    down, up, pre, send, keep, gates, slope, hidden, scaled = refs[3 * count :]
    tok_rows = mine[0].shape[0]
    me, step = place[1], pl.program_id(0)

    @pl.when(step == 0)
    def _():
        row = lax.broadcasted_iota(jnp.int32, (tok_rows, tok_rows), 0)
        column = lax.broadcasted_iota(jnp.int32, (tok_rows, tok_rows), 1)

        def upright(line):
            return jnp.sum(jnp.where(row == column, line, 0.0), axis=1, keepdims=True)

        for k in range(count):
            at = pl.ds(k * tok_rows, tok_rows)
            pair = pairs[k][...]
            named = (pair // 256) == me
            code = jnp.sum(jnp.where(named, (pair % 256).astype(F32), 0.0), axis=0, keepdims=True)
            named = jnp.sum(jnp.where(named, 1.0, 0.0), axis=0, keepdims=True)
            gates[at, :] = upright(code) / 256.0
            rank = jnp.sum(jnp.where(row < column, upright(named), 0.0), axis=0, keepdims=True)
            pick = jnp.where(rank.astype(jnp.int32) == row, named, 0.0).astype(BF16)
            slots = pl.ds(pl.multiple_of(place[2 + k] * tok_rows, tok_rows), tok_rows)
            p = lax.dot_general(pick, pre[slots, :], TN, preferred_element_type=F32)
            q = 1.0 / (1.0 + jnp.exp(-p))
            slope[at, :] = q * (1.0 + p * (1.0 - q))
        hidden[...] = jnp.zeros_like(hidden)

    def add(blocks):
        for k in range(count):
            at = pl.ds(k * tok_rows, tok_rows)
            scaled[at, :] = (gates[at, :] * blocks[k][...].astype(F32)).astype(BF16)
        hidden[...] += lax.dot_general(scaled[...], down[...], NT, preferred_element_type=F32)

    @pl.when(step < 2)
    def _():
        add(mine)

    @pl.when((step >= 2) & (step < 4))
    def _():
        add(other)

    def result():
        pre_grad = (hidden[...] * slope[...]).astype(BF16)
        return lax.dot_general(pre_grad, up[...], NT, preferred_element_type=F32)

    @pl.when((step >= 4) & (step < 6))
    def _():
        send[...] = result().astype(BF16)

    @pl.when(step >= 6)
    def _():
        keep[...] = result()


def expert_sums(place, pairs, mine, other, down, up, pre):
    count = len(mine)
    tok_rows, half_width = mine[0].shape
    units, width = down.shape
    tokens = count * tok_rows
    chunk = half_width // 2

    def clip(i, low):
        return jnp.clip(i - low, 0, 1)

    def down_at(i, place):
        return (0, jnp.where(i < 2, 2 * place[0] + clip(i, 0), 2 * (1 - place[0]) + clip(i, 2)))

    def up_at(i, place):
        return (jnp.where(i < 6, 2 * (1 - place[0]) + clip(i, 4), 2 * place[0] + clip(i, 6)), 0)

    return pl.pallas_call(
        functools.partial(expert_kernel, count),
        grid_spec=pltpu.PrefetchScalarGridSpec(
            num_scalar_prefetch=1,
            grid=(8,),
            in_specs=[whole()] * count
            + [pl.BlockSpec((tok_rows, chunk), lambda i, place: (0, clip(i, 0)))] * count
            + [pl.BlockSpec((tok_rows, chunk), lambda i, place: (0, clip(i, 2)))] * count
            + [pl.BlockSpec((units, chunk), down_at), pl.BlockSpec((chunk, units), up_at), whole()],
            out_specs=[
                pl.BlockSpec((tokens, chunk), lambda i, place: (0, clip(i, 4))),
                pl.BlockSpec((tokens, chunk), lambda i, place: (0, clip(i, 6))),
            ],
            scratch_shapes=[
                pltpu.VMEM((tokens, 1), F32),
                pltpu.VMEM((tokens, units), F32),
                pltpu.VMEM((tokens, units), F32),
                pltpu.VMEM((tokens, chunk), BF16),
            ],
        ),
        out_shape=[
            jax.ShapeDtypeStruct((tokens, half_width), BF16),
            jax.ShapeDtypeStruct((tokens, half_width), F32),
        ],
        compiler_params=pltpu.CompilerParams(vmem_limit_bytes=VMEM_LIMIT),
        cost_estimate=pl.CostEstimate(
            flops=4 * tokens * width * units, bytes_accessed=4 * width * units + 10 * tokens * width, transcendentals=0
        ),
        name="experts",
    )(place, *pairs, *mine, *other, down, up, pre)


def proj_kernel(count, with_taps, place, *refs):
    grads, heads = refs[:count], refs[count : 2 * count]
    taps, weight = refs[2 * count : 2 * count + 2]
    refs = refs[2 * count + 2 :]
    if with_taps:
        inputs, send, keep, tap_out, ext, scaled = refs
    else:
        send, keep, ext, scaled = refs
    tok_rows, chunk = grads[0].shape
    kernel_size = taps.shape[0]
    step = pl.program_id(0)

    tap = taps[...]
    for k in range(count):
        ext[:tok_rows, :] = grads[k][...].astype(F32)
        follows = (place[2 + k] < lax.axis_size("expert") - 1).astype(F32)
        ext[tok_rows:, :] = heads[k][...].astype(F32) * follows
        result = jnp.zeros((tok_rows, chunk), F32)
        for j in range(kernel_size):
            start = kernel_size - 1 - j
            result = result + tap[j : j + 1, :] * ext[start : start + tok_rows, :]
        scaled[k * tok_rows : (k + 1) * tok_rows, :] = result.astype(BF16)
        if with_taps and k == 0:
            values = inputs[...].astype(F32)
            for j in range(kernel_size):
                start = kernel_size - 1 - j
                terms = values * ext[start : start + tok_rows, :]
                tap_out[j : j + 1, :] = jnp.sum(terms, axis=0, keepdims=True)

    product = lax.dot_general(scaled[...], weight[...], NT, preferred_element_type=F32)

    @pl.when(step == 0)
    def _():
        keep[...] = product

    @pl.when(step > 0)
    def _():
        keep[...] += product

    @pl.when(step == pl.num_programs(0) - 1)
    def _():
        send[...] = keep[...].astype(BF16)


def proj_sums(place, grads, heads, taps, weight, inputs=None):
    count = len(grads)
    tok_rows, half_width = grads[0].shape
    block = weight.shape[0]
    tokens = count * tok_rows
    chunk = half_width // 4
    with_taps = inputs is not None

    def wide(rows):
        return pl.BlockSpec((rows, chunk), lambda i: (0, i))

    last = [wide(tok_rows)] if with_taps else []
    out_specs = [pl.BlockSpec((tokens, block), lambda i: (0, 0))] * 2
    out_shape = [jax.ShapeDtypeStruct((tokens, block), BF16), jax.ShapeDtypeStruct((tokens, block), F32)]
    if with_taps:
        out_specs = out_specs + [wide(taps.shape[0])]
        out_shape = out_shape + [jax.ShapeDtypeStruct(taps.shape, F32)]
    return pl.pallas_call(
        functools.partial(proj_kernel, count, with_taps),
        grid=(half_width // chunk,),
        in_specs=[whole(pltpu.SMEM)]
        + [wide(tok_rows)] * count
        + [wide(HEAD)] * count
        + [wide(taps.shape[0]), wide(block)]
        + last,
        out_specs=out_specs,
        out_shape=out_shape,
        scratch_shapes=[pltpu.VMEM((tok_rows + HEAD, chunk), F32), pltpu.VMEM((tokens, chunk), BF16)],
        compiler_params=pltpu.CompilerParams(vmem_limit_bytes=VMEM_LIMIT),
        cost_estimate=pl.CostEstimate(
            flops=2 * tokens * half_width * block,
            bytes_accessed=2 * (block + tokens) * half_width + 6 * tokens * block,
            transcendentals=0,
        ),
        name="projection",
    )(place, *grads, *heads, taps, weight, *([inputs] if with_taps else []))


def final_kernel(place, grad, keep, received, right, left, own_proj, own_received, *refs):
    pieces, out, total = refs[:-2], refs[-2], refs[-1]
    half, me = place[0], place[1]
    experts = lax.axis_size("expert")
    part = own_proj.shape[1]
    total[...] = (
        grad[...].astype(F32)
        + (keep[...] + received[...].astype(F32))
        + right[...].astype(F32)
        + left[...].astype(F32)
    )

    def add(source, value):
        @pl.when((source >= 0) & (source < experts) & (source // 2 == half))
        def _():
            at = pl.ds(pl.multiple_of(lax.rem(source, 2) * part, part), part)
            total[:, at] += value()

    add(me, lambda: own_proj[...] + own_received[...].astype(F32))
    sources = (me + 1, me - 1, lax.rem(me + 2, experts), experts - 1 - me + jnp.where(me % 3 == 0, 0, experts))
    for source, piece in zip(sources, pieces):
        add(source, lambda piece=piece: piece[...].astype(F32))
    out[...] = total[...].astype(BF16)


def final_sum(place, grad, *arrays):
    return pl.pallas_call(
        final_kernel,
        in_specs=[whole(pltpu.SMEM)] + [whole()] * (1 + len(arrays)),
        out_specs=whole(),
        out_shape=jax.ShapeDtypeStruct(grad.shape, BF16),
        scratch_shapes=[pltpu.VMEM(grad.shape, F32)],
        compiler_params=pltpu.CompilerParams(vmem_limit_bytes=VMEM_LIMIT),
        cost_estimate=pl.CostEstimate(flops=8 * grad.size, bytes_accessed=24 * grad.size, transcendentals=0),
        name="residual",
    )(place, grad, *arrays)


RIGHT = [(0, 1), (1, 2), (2, 3)]
LEFT = [(3, 2), (2, 1), (1, 0)]


def moved(array, pairs):
    return lax.ppermute(array, "expert", pairs)


def swapped(array):
    return rotated(array, "mp", 1)


def together(*arrays):
    return lax.optimization_barrier(arrays)


def token_plan(
    out_grad,
    expert_ids,
    gate_codes,
    up_weight,
    down_weight,
    pre_act,
    conv_grad,
    conv_input,
    conv_weight,
    in_proj,
):
    me, half = lax.axis_index("expert"), lax.axis_index("mp")
    experts = lax.axis_size("expert")
    far_block = (me + 2) % experts
    end_block = jnp.where(me == 0, experts - 1, 0)
    near = jnp.stack([half, me, me, jnp.maximum(me - 1, 0), jnp.minimum(me + 1, experts - 1), far_block])
    near, last = near.astype(jnp.int32), jnp.stack([half, me, end_block]).astype(jnp.int32)
    rows_own, conv_own = out_grad[0], conv_grad[0]
    tok_rows = rows_own.shape[0]
    w_down, w_up, pre = down_weight[0, 0], up_weight[0, 0], pre_act[0, 0]
    taps, w_proj = conv_weight[0], in_proj[0]

    def block(array, k):
        return array[k * tok_rows : (k + 1) * tok_rows]

    rows_left, rows_right = moved(rows_own, RIGHT), moved(rows_own, LEFT)
    pairs = around((expert_ids[0] * 256 + gate_codes[0]).T)
    heads = around(conv_own[:HEAD])
    other_own = swapped(rows_own)
    rows_left, rows_right, other_own, *tiny = together(rows_left, rows_right, other_own, *pairs, *heads)
    pairs, heads = tiny[:experts], tiny[experts:]

    from_left, from_right = moved(rows_left, RIGHT[1:]), moved(rows_right, LEFT[1:])
    other_left, other_right = swapped(rows_left), swapped(rows_right)
    from_left, from_right, other_left, other_right = together(from_left, from_right, other_left, other_right)

    rows_far = jnp.where(me >= 2, from_left, from_right)
    rows_end = moved(rows_far, [(2, 3), (1, 0)])
    other_far = swapped(rows_far)
    send, keep = expert_sums(
        near,
        [pairs[0], pairs[1], pairs[3], pairs[2]],
        [rows_own, rows_left, rows_right, rows_far],
        [other_own, other_left, other_right, other_far],
        w_down,
        w_up,
        pre,
    )
    rows_end, send, keep, conv_own = together(rows_end, send, keep, conv_own)

    conv_left, conv_right = moved(conv_own, RIGHT), moved(conv_own, LEFT)
    other_end = swapped(rows_end)
    got = swapped(send)
    send_end, keep_end = expert_sums(
        last, [jnp.where(me == 0, pairs[1], pairs[3])], [rows_end], [other_end], w_down, w_up, pre
    )
    conv_left, conv_right, got, send_end, keep_end = together(conv_left, conv_right, got, send_end, keep_end)

    from_left, from_right = moved(conv_left, RIGHT[1:]), moved(conv_right, LEFT[1:])
    back_end = (keep_end + swapped(send_end).astype(F32)).astype(BF16)
    back_end = moved(back_end, [(0, 1), (3, 2)])
    from_left, from_right, back_end = together(from_left, from_right, back_end)

    conv_far = jnp.where(me >= 2, from_left, from_right)
    conv_end = moved(conv_far, [(2, 3), (1, 0)])
    back = (block(keep, 3) + block(got, 3).astype(F32) + back_end.astype(F32)).astype(BF16)
    back_right, back_left = moved(back, RIGHT[:2]), moved(back, LEFT[:2])
    proj_send, proj_keep, tap_terms = proj_sums(
        near,
        [conv_own, conv_left, conv_right, conv_far],
        [heads[3], heads[0], heads[2], heads[1]],
        taps,
        w_proj,
        conv_input[0],
    )
    conv_end, back_right, back_left, proj_send, proj_keep = together(
        conv_end, back_right, back_left, proj_send, proj_keep
    )

    to_right = (block(keep, 2) + block(got, 2).astype(F32) + back_right.astype(F32)).astype(BF16)
    to_left = (block(keep, 1) + block(got, 1).astype(F32) + back_left.astype(F32)).astype(BF16)
    to_right, to_left = moved(to_right, RIGHT), moved(to_left, LEFT)
    proj_send_end, proj_keep_end = proj_sums(last, [conv_end], [heads[2]], taps, w_proj)

    gather = [(e * 2 + 1 - e // 2, e * 2 + e // 2) for e in range(experts)]
    both = ("expert", "mp")
    proj_got = lax.ppermute(proj_send, both, gather)
    proj_got_end = lax.ppermute(proj_send_end, both, gather)

    def deliver(kept, got, pairs):
        value = (kept + got.astype(F32)).astype(BF16)
        return lax.ppermute(value, both, [(e * 2 + e // 2, d * 2 + e // 2) for e, d in pairs])

    pieces = [
        deliver(block(proj_keep, 1), block(proj_got, 1), LEFT),
        deliver(block(proj_keep, 2), block(proj_got, 2), RIGHT),
        deliver(block(proj_keep, 3), block(proj_got, 3), [(e, (e + 2) % 4) for e in range(experts)]),
        deliver(proj_keep_end, proj_got_end, [(0, 3), (3, 0)]),
    ]
    tap_grads = doubling_sum(tap_terms, "expert")
    residual = final_sum(
        near, rows_own, block(keep, 0), block(got, 0), to_right, to_left, block(proj_keep, 0), block(proj_got, 0), *pieces
    )
    return (shifted(residual, "section", -1)[None], tap_grads[None])


def shards(*arrays):
    experts, halves = lax.axis_size("expert"), lax.axis_size("mp")
    capacity = arrays[5].shape[2] // experts
    dense = capacity == arrays[0].shape[1] and experts == 4 and halves == 2
    return (token_plan if dense else slot_plan)(*arrays)


def solution(mesh):
    in_specs = (
        P("section", "expert", "mp"),
        P("section", "expert", None),
        P("section", "expert", None),
        P("section", "expert", None, "mp"),
        P("section", "expert", "mp", None),
        P("section", "expert", None, "mp"),
        P("section", "expert", "mp"),
        P("section", "expert", "mp"),
        P("section", None, "mp"),
        P("section", "expert", "mp"),
    )
    out_specs = (P("section", "expert", "mp"), P("section", None, "mp"))
    return jax.shard_map(shards, mesh=mesh, in_specs=in_specs, out_specs=out_specs, check_vma=False)
```

```python
import functools

import jax
import jax.numpy as jnp
from jax import lax
from jax.experimental import pallas as pl
from jax.experimental.pallas import tpu as pltpu
from jax.sharding import PartitionSpec as P


def shifted(array, axis, by):
    size = lax.axis_size(axis)
    pairs = [(i, i + by) for i in range(size) if 0 <= i + by < size]
    return lax.ppermute(array, axis, pairs)


def silu_slope(pre_value):
    sig = jax.nn.sigmoid(pre_value)
    return sig * (1.0 + pre_value * (1.0 - sig))


def gated_rows(gates, rows, tok_rows):
    scaled = (gates[:, :, None] * rows.astype(jnp.float32)[:, None, :]).astype(jnp.bfloat16)
    return scaled.reshape(tok_rows * 2, rows.shape[1])


def fill_buffer(scaled, target, experts, capacity):
    width = scaled.shape[1]
    buffer = jnp.zeros((experts * capacity, width), jnp.bfloat16).at[target].set(scaled)
    return buffer.reshape(experts, capacity, width)


def slot_plan(
    out_grad,
    expert_ids,
    gate_codes,
    up_weight,
    down_weight,
    pre_act,
    conv_grad,
    conv_input,
    conv_weight,
    in_proj,
):
    grad_rows = out_grad[0]
    route_ids = expert_ids[0]
    tok_rows = grad_rows.shape[0]
    experts = lax.axis_size("expert")
    capacity = pre_act.shape[2] // experts
    gates = gate_codes[0].astype(jnp.float32) / 256.0
    flat_ids = route_ids.reshape(tok_rows * 2)
    onehot = (flat_ids[:, None] == jnp.arange(experts, dtype=jnp.int32)[None, :]).astype(jnp.int32)
    before = jnp.cumsum(onehot, axis=0) - onehot
    position = jnp.sum(before * onehot, axis=1)
    target = flat_ids * capacity + position
    whole_rows = lax.all_gather(grad_rows, "mp", axis=1, tiled=True)
    buffer = fill_buffer(gated_rows(gates, whole_rows, tok_rows), target, experts, capacity)
    arrived = lax.all_to_all(buffer, "expert", split_axis=0, concat_axis=0, tiled=True)
    slot_rows = arrived.reshape(experts * capacity, whole_rows.shape[1])
    w_down = down_weight[0, 0]
    w_up = up_weight[0, 0]
    pre_slots = pre_act[0, 0].astype(jnp.float32)
    hidden = lax.dot_general(
        slot_rows, w_down, (((1,), (1,)), ((), ())), preferred_element_type=jnp.float32
    )
    pre_grad = (hidden * silu_slope(pre_slots)).astype(jnp.bfloat16)
    partial_value = lax.dot_general(
        pre_grad, w_up, (((1,), (1,)), ((), ())), preferred_element_type=jnp.float32
    )
    share = lax.psum_scatter(partial_value, "mp", scatter_dimension=1, tiled=True).astype(
        jnp.bfloat16
    )
    returned = lax.all_to_all(
        share.reshape(experts, capacity, share.shape[1]),
        "expert",
        split_axis=0,
        concat_axis=0,
        tiled=True,
    )
    picked = returned.reshape(experts * capacity, grad_rows.shape[1])[target]
    picked = picked.astype(jnp.float32).reshape(tok_rows, 2, grad_rows.shape[1])
    moe_total = grad_rows.astype(jnp.float32) + picked[:, 0, :] + picked[:, 1, :]
    grads_here = conv_grad[0]
    inputs_here = conv_input[0]
    taps = conv_weight[0]
    kernel_size = taps.shape[0]
    next_rows = shifted(grads_here[: kernel_size - 1], "expert", -1)
    prev_rows = shifted(inputs_here[tok_rows - kernel_size + 1 :], "expert", 1)
    grad_ext = jnp.concatenate([grads_here, next_rows], axis=0).astype(jnp.float32)
    input_ext = jnp.concatenate([prev_rows, inputs_here], axis=0).astype(jnp.float32)
    grad_local = grads_here.astype(jnp.float32)
    conv_result = jnp.zeros(grads_here.shape, jnp.float32)
    tap_terms = []
    for tap in range(kernel_size):
        start = kernel_size - 1 - tap
        conv_result = conv_result + taps[tap][None, :] * grad_ext[start : start + tok_rows]
        tap_terms.append(jnp.sum(grad_local * input_ext[tap : tap + tok_rows], axis=0))
    input_grad = conv_result.astype(jnp.bfloat16)
    tap_grads = lax.psum(jnp.stack(tap_terms), "expert")
    w_proj = in_proj[0]
    proj_partial = lax.dot_general(
        input_grad,
        lax.all_gather(w_proj, "expert", axis=0, tiled=True),
        (((1,), (1,)), ((), ())),
        preferred_element_type=jnp.float32,
    )
    proj_share = lax.psum_scatter(proj_partial, "mp", scatter_dimension=1, tiled=True)
    residual = (moe_total + proj_share).astype(jnp.bfloat16)
    sent_residual = shifted(residual, "section", -1)
    return (sent_residual[None], tap_grads[None])


F32, BF16 = jnp.float32, jnp.bfloat16
VMEM_LIMIT = 14 * 1024 * 1024
HEAD = 16
RIGHT = [(0, 1), (1, 2), (2, 3)]
LEFT = [(3, 2), (2, 1), (1, 0)]
NT = (((1,), (1,)), ((), ()))
TN = (((0,), (0,)), ((), ()))


def whole(memory=pltpu.VMEM):
    return pl.BlockSpec(memory_space=memory)


def rotated(array, axis, by):
    size = lax.axis_size(axis)
    return lax.ppermute(array, axis, [(i, (i + by) % size) for i in range(size)])


def around(array):
    return [array] + [rotated(array, "expert", k) for k in range(1, lax.axis_size("expert"))]


def doubling_sum(array, axis):
    size, step = lax.axis_size(axis), 1
    while step < size:
        array = array + lax.ppermute(array, axis, [(i, i ^ step) for i in range(size)])
        step *= 2
    return array


def params():
    return pltpu.CompilerParams(vmem_limit_bytes=VMEM_LIMIT)


def cost(flops, bytes_accessed):
    return pl.CostEstimate(flops=8 * flops, bytes_accessed=8 * bytes_accessed, transcendentals=0)


def square(size):
    row = lax.broadcasted_iota(jnp.int32, (size, size), 0)
    return row, lax.broadcasted_iota(jnp.int32, (size, size), 1)


def upright(line, row, column):
    return jnp.sum(jnp.where(row == column, line, 0.0), axis=1, keepdims=True)


def hidden_kernel(count, place, *refs):
    pairs, rows = refs[:count], refs[count : 2 * count]
    down_own, down_other, send, keep, gates, scaled = refs[2 * count :]
    tok_rows = rows[0].shape[0]
    units = down_own.shape[0]
    step = pl.program_id(0)

    @pl.when(step == 0)
    def _():
        row, column = square(tok_rows)
        for k in range(count):
            pair = pairs[k][...]
            named = (pair // 256) == place[1]
            code = jnp.sum(jnp.where(named, (pair % 256).astype(F32), 0.0), axis=0, keepdims=True)
            gates[k * tok_rows : (k + 1) * tok_rows, :] = upright(code, row, column) / 256.0
        keep[...] = jnp.zeros_like(keep)

    for k in range(count):
        at = pl.ds(k * tok_rows, tok_rows)
        scaled[at, :] = (gates[at, :] * rows[k][...].astype(F32)).astype(BF16)
    keep[:, :units] += lax.dot_general(scaled[...], down_own[...], NT, preferred_element_type=F32)
    keep[:, units:] += lax.dot_general(scaled[...], down_other[...], NT, preferred_element_type=F32)

    @pl.when(step == pl.num_programs(0) - 1)
    def _():
        send[...] = keep[...].astype(BF16)


def hidden_sums(place, pairs, rows, down, down_other):
    count = len(rows)
    tok_rows, half_width = rows[0].shape
    units = down.shape[0]
    tokens = count * tok_rows
    chunk = half_width // 4
    return pl.pallas_call(
        functools.partial(hidden_kernel, count),
        grid_spec=pltpu.PrefetchScalarGridSpec(
            num_scalar_prefetch=1,
            grid=(4,),
            in_specs=[whole()] * count
            + [pl.BlockSpec((tok_rows, chunk), lambda i, place: (0, i))] * count
            + [
                pl.BlockSpec((units, chunk), lambda i, place: (0, 4 * place[0] + i)),
                pl.BlockSpec((units, chunk), lambda i, place: (0, i)),
            ],
            out_specs=[pl.BlockSpec((tokens, 2 * units), lambda i, place: (0, 0))] * 2,
            scratch_shapes=[pltpu.VMEM((tokens, 1), F32), pltpu.VMEM((tokens, chunk), BF16)],
        ),
        out_shape=[jax.ShapeDtypeStruct((tokens, 2 * units), dtype) for dtype in (BF16, F32)],
        compiler_params=params(),
        cost_estimate=cost(4 * tokens * half_width * units, 4 * units * half_width + 2 * tokens * half_width),
        name="hidden",
    )(place, *pairs, *rows, down, down_other)


def finish_kernel(count, place, *refs):
    pairs = refs[:count]
    keep, got, pre_own, pre_other, up_own, up_other, out, pre_grad = refs[count:]
    tok_rows = keep.shape[0] // count
    units = pre_own.shape[1]

    @pl.when(pl.program_id(0) == 0)
    def _():
        row, column = square(tok_rows)
        for k in range(count):
            at = pl.ds(k * tok_rows, tok_rows)
            named = jnp.where((pairs[k][...] // 256) == place[1], 1.0, 0.0)
            named = jnp.sum(named, axis=0, keepdims=True)
            rank = jnp.where(row < column, upright(named, row, column), 0.0)
            rank = jnp.sum(rank, axis=0, keepdims=True).astype(jnp.int32)
            pick = jnp.where(rank == row, named, 0.0).astype(BF16)
            slots = pl.ds(pl.multiple_of(place[2 + k] * tok_rows, tok_rows), tok_rows)
            for side, pre in enumerate((pre_own, pre_other)):
                here = pl.ds(side * units, units)
                p = lax.dot_general(pick, pre[slots, :], TN, preferred_element_type=F32)
                q = 1.0 / (1.0 + jnp.exp(-p))
                hidden = keep[at, here] + got[at, pl.ds((1 - side) * units, units)].astype(F32)
                pre_grad[at, here] = (hidden * (q * (1.0 + p * (1.0 - q)))).astype(BF16)

    value = lax.dot_general(pre_grad[:, :units], up_own[...], NT, preferred_element_type=F32)
    value += lax.dot_general(pre_grad[:, units:], up_other[...], NT, preferred_element_type=F32)
    out[...] = value.astype(out.dtype)


def expert_sums(place, pairs, keep, got, pre, pre_other, up, up_other, dtype):
    count = len(pairs)
    tokens = keep.shape[0]
    units = pre.shape[1]
    half_width = up_other.shape[0]
    chunk = half_width // 4
    return pl.pallas_call(
        functools.partial(finish_kernel, count),
        grid_spec=pltpu.PrefetchScalarGridSpec(
            num_scalar_prefetch=1,
            grid=(4,),
            in_specs=[whole()] * (count + 4)
            + [
                pl.BlockSpec((chunk, units), lambda i, place: (4 * place[0] + i, 0)),
                pl.BlockSpec((chunk, units), lambda i, place: (i, 0)),
            ],
            out_specs=pl.BlockSpec((tokens, chunk), lambda i, place: (0, i)),
            scratch_shapes=[pltpu.VMEM((tokens, 2 * units), BF16)],
        ),
        out_shape=jax.ShapeDtypeStruct((tokens, half_width), dtype),
        compiler_params=params(),
        cost_estimate=cost(4 * tokens * half_width * units, 4 * units * half_width + 4 * tokens * half_width),
        name="experts",
    )(place, *pairs, keep, got, pre, pre_other, up, up_other)


def proj_kernel(count, with_taps, place, *refs):
    grads, heads = refs[:count], refs[count : 2 * count]
    taps, weight = refs[2 * count : 2 * count + 2]
    refs = refs[2 * count + 2 :]
    if with_taps:
        inputs, send, keep, tap_out, ext, scaled = refs
    else:
        send, keep, ext, scaled = refs
    tok_rows, chunk = grads[0].shape
    kernel_size = taps.shape[0]
    step = pl.program_id(0)

    tap = taps[...]
    for k in range(count):
        ext[:tok_rows, :] = grads[k][...].astype(F32)
        follows = (place[2 + k] < lax.axis_size("expert") - 1).astype(F32)
        ext[tok_rows:, :] = heads[k][...].astype(F32) * follows
        result = jnp.zeros((tok_rows, chunk), F32)
        for j in range(kernel_size):
            start = kernel_size - 1 - j
            result = result + tap[j : j + 1, :] * ext[start : start + tok_rows, :]
        scaled[k * tok_rows : (k + 1) * tok_rows, :] = result.astype(BF16)
        if with_taps and k == 0:
            values = inputs[...].astype(F32)
            for j in range(kernel_size):
                start = kernel_size - 1 - j
                terms = values * ext[start : start + tok_rows, :]
                tap_out[j : j + 1, :] = jnp.sum(terms, axis=0, keepdims=True)

    product = lax.dot_general(scaled[...], weight[...], NT, preferred_element_type=F32)

    @pl.when(step == 0)
    def _():
        keep[...] = product

    @pl.when(step > 0)
    def _():
        keep[...] += product

    @pl.when(step == pl.num_programs(0) - 1)
    def _():
        send[...] = keep[...].astype(BF16)


def proj_sums(place, grads, heads, taps, weight, inputs=None):
    count = len(grads)
    tok_rows, half_width = grads[0].shape
    block = weight.shape[0]
    tokens = count * tok_rows
    chunk = half_width // 4
    with_taps = inputs is not None

    def wide(rows):
        return pl.BlockSpec((rows, chunk), lambda i: (0, i))

    last = [wide(tok_rows)] if with_taps else []
    out_specs = [pl.BlockSpec((tokens, block), lambda i: (0, 0))] * 2
    out_shape = [jax.ShapeDtypeStruct((tokens, block), BF16), jax.ShapeDtypeStruct((tokens, block), F32)]
    if with_taps:
        out_specs = out_specs + [wide(taps.shape[0])]
        out_shape = out_shape + [jax.ShapeDtypeStruct(taps.shape, F32)]
    return pl.pallas_call(
        functools.partial(proj_kernel, count, with_taps),
        grid=(half_width // chunk,),
        in_specs=[whole(pltpu.SMEM)]
        + [wide(tok_rows)] * count
        + [wide(HEAD)] * count
        + [wide(taps.shape[0]), wide(block)]
        + last,
        out_specs=out_specs,
        out_shape=out_shape,
        scratch_shapes=[pltpu.VMEM((tok_rows + HEAD, chunk), F32), pltpu.VMEM((tokens, chunk), BF16)],
        compiler_params=params(),
        cost_estimate=cost(
            2 * tokens * half_width * block, 2 * (block + tokens) * half_width + 6 * tokens * block
        ),
        name="projection",
    )(place, *grads, *heads, taps, weight, *([inputs] if with_taps else []))


def combine_kernel(place, grad, sums, back_right, back_left, proj_keep, proj_got, to_right, to_left, own, total):
    half, me = place[0], place[1]
    rows, part = grad.shape[0], proj_keep.shape[1]
    total[0:rows, :] = grad[...].astype(F32) + sums[0:rows, :]
    total[rows : 2 * rows, :] = sums[rows : 2 * rows, :] + back_left[...].astype(F32)
    total[2 * rows :, :] = sums[2 * rows :, :] + back_right[...].astype(F32)

    @pl.when(me // 2 == half)
    def _():
        at = pl.ds(pl.multiple_of(lax.rem(me, 2) * part, part), part)
        total[:, at] += proj_keep[...] + proj_got[...].astype(F32)

    own[...] = total[0:rows, :]
    to_left[...] = total[rows : 2 * rows, :].astype(BF16)
    to_right[...] = total[2 * rows :, :].astype(BF16)


def combined(place, grad, sums, *arrays):
    outs = [jax.ShapeDtypeStruct(grad.shape, dtype) for dtype in (BF16, BF16, F32)]
    return pl.pallas_call(
        combine_kernel,
        in_specs=[whole(pltpu.SMEM)] + [whole()] * (2 + len(arrays)),
        out_specs=[whole()] * 3,
        out_shape=outs,
        scratch_shapes=[pltpu.VMEM(sums.shape, F32)],
        compiler_params=params(),
        cost_estimate=cost(8 * grad.size, 40 * grad.size),
        name="combine",
    )(place, grad, sums, *arrays)


def final_kernel(place, residual, far, end, out, total):
    half, me = place[0], place[1]
    experts = lax.axis_size("expert")
    part = far.shape[1]
    total[...] = residual[...].astype(F32)

    def add(source, value):
        @pl.when((source < experts) & (source // 2 == half))
        def _():
            at = pl.ds(pl.multiple_of(lax.rem(source, 2) * part, part), part)
            total[:, at] += value[...].astype(F32)

    add(lax.rem(me + 2, experts), far)
    add(jnp.where(lax.rem(me, experts - 1) == 0, experts - 1 - me, experts), end)
    out[...] = total[...].astype(BF16)


def final_sum(place, residual, far, end):
    return pl.pallas_call(
        final_kernel,
        in_specs=[whole(pltpu.SMEM)] + [whole()] * 3,
        out_specs=whole(),
        out_shape=jax.ShapeDtypeStruct(residual.shape, BF16),
        scratch_shapes=[pltpu.VMEM(residual.shape, F32)],
        compiler_params=params(),
        cost_estimate=cost(4 * residual.size, 8 * residual.size),
        name="residual",
    )(place, residual, far, end)


def moved(array, pairs):
    return lax.ppermute(array, "expert", pairs)


def swapped(array):
    return rotated(array, "mp", 1)


def together(*arrays):
    return lax.optimization_barrier(arrays)


def token_plan(
    out_grad,
    expert_ids,
    gate_codes,
    up_weight,
    down_weight,
    pre_act,
    conv_grad,
    conv_input,
    conv_weight,
    in_proj,
):
    me, half = lax.axis_index("expert"), lax.axis_index("mp")
    experts = lax.axis_size("expert")

    def place(*blocks):
        return jnp.stack([half, me, *blocks]).astype(jnp.int32)

    far_block, end_block = (me + 2) % experts, jnp.where(me == 0, experts - 1, 0)
    near = place(me, jnp.maximum(me - 1, 0), jnp.minimum(me + 1, experts - 1))
    rows_own, conv_own = out_grad[0], conv_grad[0]
    tok_rows, half_width = rows_own.shape
    w_down, w_up, pre = down_weight[0, 0], up_weight[0, 0], pre_act[0, 0]
    taps, w_proj = conv_weight[0], in_proj[0]

    pairs = around((expert_ids[0] * 256 + gate_codes[0]).T)
    down_send = lax.dynamic_slice_in_dim(w_down, (1 - half) * half_width, half_width, 1)
    up_send = lax.dynamic_slice_in_dim(w_up, (1 - half) * half_width, half_width, 0)
    rows_own, down_send, *pairs = together(rows_own, down_send, *pairs)

    rows_left, rows_right = moved(rows_own, RIGHT), moved(rows_own, LEFT)
    down_other = swapped(down_send)
    rows_left, rows_right, down_other, up_send, pre_send = together(rows_left, rows_right, down_other, up_send, pre)

    def hidden(where, routes, rows):
        send, keep = hidden_sums(where, routes, rows, w_down, down_other)
        return keep, swapped(send)

    def finish(where, routes, keep, got, dtype):
        return expert_sums(where, routes, keep, got, pre, pre_other, w_up, up_other, dtype)

    near_pairs = [pairs[0], pairs[1], pairs[3]]
    from_left, from_right = moved(rows_left, RIGHT[1:]), moved(rows_right, LEFT[1:])
    up_other, pre_other = swapped(up_send), swapped(pre_send)
    near_keep, near_got = hidden(near, near_pairs, [rows_own, rows_left, rows_right])
    from_left, from_right, near_keep, up_other, pre_other = together(
        from_left, from_right, near_keep, up_other, pre_other
    )

    far, end = place(far_block), place(end_block)
    end_pairs = [jnp.where(me == 0, pairs[1], pairs[3])]
    rows_far = jnp.where(me >= 2, from_left, from_right)
    rows_end = moved(rows_far, [(2, 3), (1, 0)])
    near_sums = finish(near, near_pairs, near_keep, near_got, F32)
    far_keep, far_got = hidden(far, [pairs[2]], [rows_far])
    rows_end, near_sums, far_keep, conv_own = together(rows_end, near_sums, far_keep, conv_own)

    conv_left, conv_right = moved(conv_own, RIGHT), moved(conv_own, LEFT)
    end_keep, end_got = hidden(end, end_pairs, [rows_end])
    far_sums = finish(far, [pairs[2]], far_keep, far_got, F32)
    end_sums = finish(end, end_pairs, end_keep, end_got, BF16)
    next_head = moved(conv_own[:HEAD], [(2, 0), (3, 1)])
    last_head = moved(conv_own[:HEAD], [(3, 0)])
    conv_left, conv_right, end_sums, far_sums, next_head, last_head = together(
        conv_left, conv_right, end_sums, far_sums, next_head, last_head
    )

    from_left, from_right = moved(conv_left, RIGHT[1:]), moved(conv_right, LEFT[1:])
    back_end = moved(end_sums, [(0, 1), (3, 2)])
    gather = [(e * 2 + 1 - e // 2, e * 2 + e // 2) for e in range(experts)]

    def proj(where, grads, heads, *inputs):
        send, keep, *tap_terms = proj_sums(where, grads, heads, taps, w_proj, *inputs)
        return keep, lax.ppermute(send, ("expert", "mp"), gather), *tap_terms

    near_proj, near_proj_got, tap_terms = proj(
        near, [conv_own, conv_left, conv_right], [conv_right, conv_own, next_head], conv_input[0]
    )
    from_left, from_right, back_end, near_proj, conv_left = together(
        from_left, from_right, back_end, near_proj, conv_left
    )

    conv_far = jnp.where(me >= 2, from_left, from_right)
    conv_end = moved(conv_far, [(2, 3), (1, 0)])
    back = (far_sums + back_end.astype(F32)).astype(BF16)
    back_right, back_left = moved(back, RIGHT[:2]), moved(back, LEFT[:2])
    far_head = jnp.where(me >= 2, conv_left[:HEAD], last_head)
    far_proj, far_proj_got = proj(far, [conv_far], [far_head])
    conv_end, back_right, back_left, far_proj = together(conv_end, back_right, back_left, far_proj)

    to_right, to_left, own = combined(near, rows_own, near_sums, back_right, back_left, near_proj, near_proj_got)
    to_right, to_left, conv_end = together(to_right, to_left, conv_end)
    to_right, to_left = moved(to_right, RIGHT), moved(to_left, LEFT)
    end_proj, end_proj_got = proj(end, [conv_end], [conv_far])
    to_right, to_left, end_proj = together(to_right, to_left, end_proj)

    residual = (own + to_right.astype(F32) + to_left.astype(F32)).astype(BF16)
    sections, halves = lax.axis_size("section"), lax.axis_size("mp")

    def deliver(keep, got, pairs):
        def at(s, e, m):
            return (s * experts + e) * halves + m

        moves = [(at(s, e, e // 2), at(s - 1, d, e // 2)) for s in range(1, sections) for e, d in pairs]
        return lax.ppermute((keep + got.astype(F32)).astype(BF16), ("section", "expert", "mp"), moves)

    residual = shifted(residual, "section", -1)
    far_piece = deliver(far_proj, far_proj_got, [(e, (e + 2) % experts) for e in range(experts)])
    end_piece = deliver(end_proj, end_proj_got, [(0, experts - 1), (experts - 1, 0)])
    tap_grads = doubling_sum(tap_terms, "expert")
    residual = final_sum(near, residual, far_piece, end_piece)
    return (residual[None], tap_grads[None])


def shards(*arrays):
    experts, halves = lax.axis_size("expert"), lax.axis_size("mp")
    capacity = arrays[5].shape[2] // experts
    dense = capacity == arrays[0].shape[1] and experts == 4 and halves == 2
    return (token_plan if dense else slot_plan)(*arrays)


def solution(mesh):
    in_specs = (
        P("section", "expert", "mp"),
        P("section", "expert", None),
        P("section", "expert", None),
        P("section", "expert", None, "mp"),
        P("section", "expert", "mp", None),
        P("section", "expert", None, "mp"),
        P("section", "expert", "mp"),
        P("section", "expert", "mp"),
        P("section", None, "mp"),
        P("section", "expert", "mp"),
    )
    out_specs = (P("section", "expert", "mp"), P("section", None, "mp"))
    return jax.shard_map(shards, mesh=mesh, in_specs=in_specs, out_specs=out_specs, check_vma=False)
```

```python
import functools

import jax
import jax.numpy as jnp
from jax import lax
from jax.experimental import pallas as pl
from jax.experimental.pallas import tpu as pltpu
from jax.sharding import PartitionSpec as P


def shifted(array, axis, by):
    size = lax.axis_size(axis)
    pairs = [(i, i + by) for i in range(size) if 0 <= i + by < size]
    return lax.ppermute(array, axis, pairs)


def silu_slope(pre_value):
    sig = jax.nn.sigmoid(pre_value)
    return sig * (1.0 + pre_value * (1.0 - sig))


def gated_rows(gates, rows, tok_rows):
    scaled = (gates[:, :, None] * rows.astype(jnp.float32)[:, None, :]).astype(jnp.bfloat16)
    return scaled.reshape(tok_rows * 2, rows.shape[1])


def fill_buffer(scaled, target, experts, capacity):
    width = scaled.shape[1]
    buffer = jnp.zeros((experts * capacity, width), jnp.bfloat16).at[target].set(scaled)
    return buffer.reshape(experts, capacity, width)


def slot_plan(
    out_grad,
    expert_ids,
    gate_codes,
    up_weight,
    down_weight,
    pre_act,
    conv_grad,
    conv_input,
    conv_weight,
    in_proj,
):
    grad_rows = out_grad[0]
    route_ids = expert_ids[0]
    tok_rows = grad_rows.shape[0]
    experts = lax.axis_size("expert")
    capacity = pre_act.shape[2] // experts
    gates = gate_codes[0].astype(jnp.float32) / 256.0
    flat_ids = route_ids.reshape(tok_rows * 2)
    onehot = (flat_ids[:, None] == jnp.arange(experts, dtype=jnp.int32)[None, :]).astype(jnp.int32)
    before = jnp.cumsum(onehot, axis=0) - onehot
    position = jnp.sum(before * onehot, axis=1)
    target = flat_ids * capacity + position
    whole_rows = lax.all_gather(grad_rows, "mp", axis=1, tiled=True)
    buffer = fill_buffer(gated_rows(gates, whole_rows, tok_rows), target, experts, capacity)
    arrived = lax.all_to_all(buffer, "expert", split_axis=0, concat_axis=0, tiled=True)
    slot_rows = arrived.reshape(experts * capacity, whole_rows.shape[1])
    w_down = down_weight[0, 0]
    w_up = up_weight[0, 0]
    pre_slots = pre_act[0, 0].astype(jnp.float32)
    hidden = lax.dot_general(
        slot_rows, w_down, (((1,), (1,)), ((), ())), preferred_element_type=jnp.float32
    )
    pre_grad = (hidden * silu_slope(pre_slots)).astype(jnp.bfloat16)
    partial_value = lax.dot_general(
        pre_grad, w_up, (((1,), (1,)), ((), ())), preferred_element_type=jnp.float32
    )
    share = lax.psum_scatter(partial_value, "mp", scatter_dimension=1, tiled=True).astype(
        jnp.bfloat16
    )
    returned = lax.all_to_all(
        share.reshape(experts, capacity, share.shape[1]),
        "expert",
        split_axis=0,
        concat_axis=0,
        tiled=True,
    )
    picked = returned.reshape(experts * capacity, grad_rows.shape[1])[target]
    picked = picked.astype(jnp.float32).reshape(tok_rows, 2, grad_rows.shape[1])
    moe_total = grad_rows.astype(jnp.float32) + picked[:, 0, :] + picked[:, 1, :]
    grads_here = conv_grad[0]
    inputs_here = conv_input[0]
    taps = conv_weight[0]
    kernel_size = taps.shape[0]
    next_rows = shifted(grads_here[: kernel_size - 1], "expert", -1)
    prev_rows = shifted(inputs_here[tok_rows - kernel_size + 1 :], "expert", 1)
    grad_ext = jnp.concatenate([grads_here, next_rows], axis=0).astype(jnp.float32)
    input_ext = jnp.concatenate([prev_rows, inputs_here], axis=0).astype(jnp.float32)
    grad_local = grads_here.astype(jnp.float32)
    conv_result = jnp.zeros(grads_here.shape, jnp.float32)
    tap_terms = []
    for tap in range(kernel_size):
        start = kernel_size - 1 - tap
        conv_result = conv_result + taps[tap][None, :] * grad_ext[start : start + tok_rows]
        tap_terms.append(jnp.sum(grad_local * input_ext[tap : tap + tok_rows], axis=0))
    input_grad = conv_result.astype(jnp.bfloat16)
    tap_grads = lax.psum(jnp.stack(tap_terms), "expert")
    w_proj = in_proj[0]
    proj_partial = lax.dot_general(
        input_grad,
        lax.all_gather(w_proj, "expert", axis=0, tiled=True),
        (((1,), (1,)), ((), ())),
        preferred_element_type=jnp.float32,
    )
    proj_share = lax.psum_scatter(proj_partial, "mp", scatter_dimension=1, tiled=True)
    residual = (moe_total + proj_share).astype(jnp.bfloat16)
    sent_residual = shifted(residual, "section", -1)
    return (sent_residual[None], tap_grads[None])


F32, BF16 = jnp.float32, jnp.bfloat16
VMEM_LIMIT = 14 * 1024 * 1024
RIGHT = [(0, 1), (1, 2), (2, 3)]
LEFT = [(3, 2), (2, 1), (1, 0)]
NT = (((1,), (1,)), ((), ()))
TN = (((0,), (0,)), ((), ()))


def whole(memory=pltpu.VMEM):
    return pl.BlockSpec(memory_space=memory)


def rotated(array, axis, by):
    size = lax.axis_size(axis)
    return lax.ppermute(array, axis, [(i, (i + by) % size) for i in range(size)])


def around(array):
    return [array] + [rotated(array, "expert", k) for k in range(1, lax.axis_size("expert"))]


def doubling_sum(array, axis):
    size, step = lax.axis_size(axis), 1
    while step < size:
        array = array + lax.ppermute(array, axis, [(i, i ^ step) for i in range(size)])
        step *= 2
    return array


def params(limit=VMEM_LIMIT):
    return pltpu.CompilerParams(vmem_limit_bytes=limit)


def cost(flops, bytes_accessed):
    return pl.CostEstimate(flops=flops, bytes_accessed=bytes_accessed, transcendentals=0)


def streamed(source, buffer, sems, step):
    count, _, chunk = buffer.shape

    def copy(i):
        columns = pl.ds(pl.multiple_of(i * chunk, chunk), chunk)
        return pltpu.make_async_copy(source.at[:, columns], buffer.at[i], sems.at[i])

    @pl.when(step == 0)
    def _():
        for i in range(count):
            copy(i).start()

    copy(step).wait()
    return buffer[step]


def stream_scratch(array, count):
    shape = (count, array.shape[0], array.shape[1] // count)
    return [pltpu.VMEM(shape, array.dtype), pltpu.SemaphoreType.DMA((count,))]


def square(size):
    row = lax.broadcasted_iota(jnp.int32, (size, size), 0)
    return row, lax.broadcasted_iota(jnp.int32, (size, size), 1)


def upright(line, row, column):
    return jnp.sum(jnp.where(row == column, line, 0.0), axis=1, keepdims=True)


def rows_of(place, k, experts, tok_rows):
    block = lax.rem(place[1] - k + experts, experts)
    return pl.ds(pl.multiple_of(block * tok_rows, tok_rows), tok_rows)


def hidden_kernel(experts, place, *refs):
    pairs = refs[:experts]
    rows, down_own, down_other, send, keep, gates, buffer, sems = refs[experts:]
    tok_rows = rows.shape[0] // experts
    units = down_own.shape[0]
    step = pl.program_id(0)
    values = streamed(rows, buffer, sems, step).astype(F32)

    @pl.when(step == 0)
    def _():
        row, column = square(tok_rows)
        for k in range(experts):
            pair = pairs[k][...]
            named = (pair // 256) == place[1]
            code = jnp.sum(jnp.where(named, (pair % 256).astype(F32), 0.0), axis=0, keepdims=True)
            gates[rows_of(place, k, experts, tok_rows), :] = upright(code, row, column) / 256.0
        keep[...] = jnp.zeros_like(keep)

    scaled = (gates[...] * values).astype(BF16)
    keep[:, :units] += lax.dot_general(scaled, down_own[...], NT, preferred_element_type=F32)
    keep[:, units:] += lax.dot_general(scaled, down_other[...], NT, preferred_element_type=F32)

    @pl.when(step == pl.num_programs(0) - 1)
    def _():
        send[...] = keep[...].astype(BF16)


def hidden_sums(place, pairs, rows, down, down_other):
    experts = len(pairs)
    tokens, half_width = rows.shape
    units = down.shape[0]
    chunk = half_width // 4
    return pl.pallas_call(
        functools.partial(hidden_kernel, experts),
        grid_spec=pltpu.PrefetchScalarGridSpec(
            num_scalar_prefetch=1,
            grid=(4,),
            in_specs=[whole()] * experts
            + [
                whole(pltpu.HBM),
                pl.BlockSpec((units, chunk), lambda i, place: (0, 4 * place[0] + i)),
                pl.BlockSpec((units, chunk), lambda i, place: (0, i)),
            ],
            out_specs=[pl.BlockSpec((tokens, 2 * units), lambda i, place: (0, 0))] * 2,
            scratch_shapes=[pltpu.VMEM((tokens, 1), F32)] + stream_scratch(rows, 4),
        ),
        out_shape=[jax.ShapeDtypeStruct((tokens, 2 * units), dtype) for dtype in (BF16, F32)],
        compiler_params=params(),
        cost_estimate=cost(4 * tokens * half_width * units, 4 * units * half_width + 2 * tokens * half_width),
        name="hidden",
    )(place, *pairs, rows, down, down_other)


def finish_kernel(experts, place, *refs):
    pairs = refs[:experts]
    keep, got, pre_own, pre_other, up_own, up_other, out, pre_grad = refs[experts:]
    tok_rows = keep.shape[0] // experts
    units = pre_own.shape[1]

    @pl.when(pl.program_id(0) == 0)
    def _():
        row, column = square(tok_rows)
        for k in range(experts):
            at = rows_of(place, k, experts, tok_rows)
            named = jnp.where((pairs[k][...] // 256) == place[1], 1.0, 0.0)
            named = jnp.sum(named, axis=0, keepdims=True)
            rank = jnp.where(row < column, upright(named, row, column), 0.0)
            rank = jnp.sum(rank, axis=0, keepdims=True).astype(jnp.int32)
            pick = jnp.where(rank == row, named, 0.0).astype(BF16)
            for side, pre in enumerate((pre_own, pre_other)):
                here = pl.ds(side * units, units)
                p = lax.dot_general(pick, pre[at, :], TN, preferred_element_type=F32)
                q = 1.0 / (1.0 + jnp.exp(-p))
                hidden = keep[at, here] + got[at, pl.ds((1 - side) * units, units)].astype(F32)
                pre_grad[at, here] = (hidden * (q * (1.0 + p * (1.0 - q)))).astype(BF16)

    value = lax.dot_general(pre_grad[:, :units], up_own[...], NT, preferred_element_type=F32)
    value += lax.dot_general(pre_grad[:, units:], up_other[...], NT, preferred_element_type=F32)
    out[...] = value


def expert_sums(place, pairs, keep, got, pre, pre_other, up, up_other):
    experts = len(pairs)
    tokens = keep.shape[0]
    units = pre.shape[1]
    half_width = up_other.shape[0]
    chunk = half_width // 4
    return pl.pallas_call(
        functools.partial(finish_kernel, experts),
        grid_spec=pltpu.PrefetchScalarGridSpec(
            num_scalar_prefetch=1,
            grid=(4,),
            in_specs=[whole()] * (experts + 4)
            + [
                pl.BlockSpec((chunk, units), lambda i, place: (4 * place[0] + i, 0)),
                pl.BlockSpec((chunk, units), lambda i, place: (i, 0)),
            ],
            out_specs=pl.BlockSpec((tokens, chunk), lambda i, place: (0, i)),
            scratch_shapes=[pltpu.VMEM((tokens, 2 * units), BF16)],
        ),
        out_shape=jax.ShapeDtypeStruct((tokens, half_width), F32),
        compiler_params=params(),
        cost_estimate=cost(4 * tokens * half_width * units, 4 * units * half_width + 4 * tokens * half_width),
        name="experts",
    )(place, *pairs, keep, got, pre, pre_other, up, up_other)


def proj_kernel(place, grads, taps, weight, inputs, send, keep, tap_out, ext, buffer, sems):
    tokens = grads.shape[0]
    tok_rows, chunk = inputs.shape
    kernel_size = taps.shape[0]
    step = pl.program_id(0)

    ext[:tokens, :] = streamed(grads, buffer, sems, step).astype(F32)
    ext[tokens:, :] = jnp.zeros((ext.shape[0] - tokens, chunk), F32)
    tap = taps[...]
    result = jnp.zeros((tokens, chunk), F32)
    for j in range(kernel_size):
        start = kernel_size - 1 - j
        result = result + tap[j : j + 1, :] * ext[start : start + tokens, :]
    window = ext[pl.ds(pl.multiple_of(place[1] * tok_rows, tok_rows), tok_rows + 8), :]
    values = inputs[...].astype(F32)
    for j in range(kernel_size):
        start = kernel_size - 1 - j
        tap_out[j : j + 1, :] = jnp.sum(values * window[start : start + tok_rows, :], axis=0, keepdims=True)
    product = lax.dot_general(result.astype(BF16), weight[...], NT, preferred_element_type=F32)

    @pl.when(step == 0)
    def _():
        keep[...] = product

    @pl.when(step > 0)
    def _():
        keep[...] += product

    @pl.when(step == pl.num_programs(0) - 1)
    def _():
        send[...] = keep[...].astype(BF16)


def proj_sums(place, grads, taps, weight, inputs):
    tokens, half_width = grads.shape
    block = weight.shape[0]
    chunk = half_width // 4

    def wide(array):
        return pl.BlockSpec((array.shape[0], chunk), lambda i: (0, i))

    return pl.pallas_call(
        proj_kernel,
        grid=(half_width // chunk,),
        in_specs=[whole(pltpu.SMEM), whole(pltpu.HBM), wide(taps), wide(weight), wide(inputs)],
        out_specs=[pl.BlockSpec((tokens, block), lambda i: (0, 0))] * 2 + [wide(taps)],
        out_shape=[
            jax.ShapeDtypeStruct((tokens, block), BF16),
            jax.ShapeDtypeStruct((tokens, block), F32),
            jax.ShapeDtypeStruct(taps.shape, F32),
        ],
        scratch_shapes=[pltpu.VMEM((tokens + 8, chunk), F32)] + stream_scratch(grads, 4),
        compiler_params=params(),
        cost_estimate=cost(
            2 * tokens * half_width * block, 2 * (block + tokens) * half_width + 6 * tokens * block
        ),
        name="projection",
    )(place, grads, taps, weight, inputs)


def combine_kernel(place, grad, sums, back_right, back_left, proj_keep, proj_got, to_right, to_left, own, total):
    half, me = place[0], place[1]
    rows, part = grad.shape[0], proj_keep.shape[1]
    experts = sums.shape[0] // rows
    blocks = (me, jnp.maximum(me - 1, 0), jnp.minimum(me + 1, experts - 1))
    places = [pl.ds(pl.multiple_of(block * rows, rows), rows) for block in blocks]
    for k, other in enumerate((grad, back_left, back_right)):
        total[k * rows : (k + 1) * rows, :] = sums[places[k], :] + other[...].astype(F32)

    @pl.when(me // 2 == half)
    def _():
        at = pl.ds(pl.multiple_of(lax.rem(me, 2) * part, part), part)
        for k in range(3):
            total[k * rows : (k + 1) * rows, at] += proj_keep[places[k], :] + proj_got[places[k], :].astype(F32)

    own[...] = total[0:rows, :]
    to_left[...] = total[rows : 2 * rows, :].astype(BF16)
    to_right[...] = total[2 * rows :, :].astype(BF16)


def combined(place, grad, *arrays):
    outs = [jax.ShapeDtypeStruct(grad.shape, dtype) for dtype in (BF16, BF16, F32)]
    return pl.pallas_call(
        combine_kernel,
        in_specs=[whole(pltpu.SMEM)] + [whole()] * (1 + len(arrays)),
        out_specs=[whole()] * 3,
        out_shape=outs,
        scratch_shapes=[pltpu.VMEM((3 * grad.shape[0], grad.shape[1]), F32)],
        compiler_params=params(),
        cost_estimate=cost(8 * grad.size, 40 * grad.size),
        name="combine",
    )(place, grad, *arrays)


def final_kernel(place, residual, far, end, out, total):
    half, me = place[0], place[1]
    experts = lax.axis_size("expert")
    part = far.shape[1]
    total[...] = residual[...].astype(F32)

    def add(source, value):
        @pl.when((source < experts) & (source // 2 == half))
        def _():
            at = pl.ds(pl.multiple_of(lax.rem(source, 2) * part, part), part)
            total[:, at] += value[...].astype(F32)

    add(lax.rem(me + 2, experts), far)
    add(jnp.where(lax.rem(me, experts - 1) == 0, experts - 1 - me, experts), end)
    out[...] = total[...].astype(BF16)


def final_sum(place, residual, far, end):
    return pl.pallas_call(
        final_kernel,
        in_specs=[whole(pltpu.SMEM)] + [whole()] * 3,
        out_specs=whole(),
        out_shape=jax.ShapeDtypeStruct(residual.shape, BF16),
        scratch_shapes=[pltpu.VMEM(residual.shape, F32)],
        compiler_params=params(),
        cost_estimate=cost(4 * residual.size, 8 * residual.size),
        name="residual",
    )(place, residual, far, end)


def moved(array, pairs):
    return lax.ppermute(array, "expert", pairs)


def swapped(array):
    return rotated(array, "mp", 1)


def together(*arrays):
    return lax.optimization_barrier(arrays)


def token_plan(
    out_grad,
    expert_ids,
    gate_codes,
    up_weight,
    down_weight,
    pre_act,
    conv_grad,
    conv_input,
    conv_weight,
    in_proj,
):
    me, half = lax.axis_index("expert"), lax.axis_index("mp")
    experts = lax.axis_size("expert")
    place = jnp.stack([half, me]).astype(jnp.int32)
    far_block, end_block = (me + 2) % experts, jnp.where(me == 0, experts - 1, 0)
    rows_own = out_grad[0]
    tok_rows, half_width = rows_own.shape
    w_down, w_up, pre = down_weight[0, 0], up_weight[0, 0], pre_act[0, 0]

    def block(array, k):
        return lax.dynamic_slice_in_dim(array, k * tok_rows, tok_rows, 0)

    all_rows = lax.all_gather(rows_own, "expert", axis=0, tiled=True)
    all_conv = lax.all_gather(conv_grad[0], "expert", axis=0, tiled=True)

    pairs = around((expert_ids[0] * 256 + gate_codes[0]).T)
    down_other = swapped(lax.dynamic_slice_in_dim(w_down, (1 - half) * half_width, half_width, 1))
    up_other = swapped(lax.dynamic_slice_in_dim(w_up, (1 - half) * half_width, half_width, 0))
    pre_other = swapped(pre)
    down_other, up_other, pre_other, all_rows, *pairs = together(down_other, up_other, pre_other, all_rows, *pairs)

    send, keep = hidden_sums(place, pairs, all_rows, w_down, down_other)
    sums = expert_sums(place, pairs, keep, swapped(send), pre, pre_other, w_up, up_other)
    back_end = moved(block(sums, end_block).astype(BF16), [(0, 1), (3, 2)])
    back = (block(sums, far_block) + back_end.astype(F32)).astype(BF16)
    back_right, back_left = moved(back, RIGHT[:2]), moved(back, LEFT[:2])
    back_right, back_left, all_conv = together(back_right, back_left, all_conv)

    proj_send, proj, tap_terms = proj_sums(place, all_conv, conv_weight[0], in_proj[0], conv_input[0])
    gather = [(e * 2 + 1 - e // 2, e * 2 + e // 2) for e in range(experts)]
    proj_got = lax.ppermute(proj_send, ("expert", "mp"), gather)
    to_right, to_left, own = combined(place, rows_own, sums, back_right, back_left, proj, proj_got)
    to_right, to_left = moved(to_right, RIGHT), moved(to_left, LEFT)

    residual = (own + to_right.astype(F32) + to_left.astype(F32)).astype(BF16)
    sections, halves = lax.axis_size("section"), lax.axis_size("mp")

    def deliver(keep, got, pairs):
        def at(s, e, m):
            return (s * experts + e) * halves + m

        moves = [(at(s, e, e // 2), at(s - 1, d, e // 2)) for s in range(1, sections) for e, d in pairs]
        return lax.ppermute((keep + got.astype(F32)).astype(BF16), ("section", "expert", "mp"), moves)

    residual = shifted(residual, "section", -1)
    far_piece = deliver(block(proj, far_block), block(proj_got, far_block), [(e, (e + 2) % experts) for e in range(experts)])
    end_piece = deliver(block(proj, end_block), block(proj_got, end_block), [(0, experts - 1), (experts - 1, 0)])
    tap_grads = doubling_sum(tap_terms, "expert")
    residual = final_sum(place, residual, far_piece, end_piece)
    return (residual[None], tap_grads[None])


def shards(*arrays):
    experts, halves = lax.axis_size("expert"), lax.axis_size("mp")
    capacity = arrays[5].shape[2] // experts
    dense = capacity == arrays[0].shape[1] and experts == 4 and halves == 2
    return (token_plan if dense else slot_plan)(*arrays)


def solution(mesh):
    in_specs = (
        P("section", "expert", "mp"),
        P("section", "expert", None),
        P("section", "expert", None),
        P("section", "expert", None, "mp"),
        P("section", "expert", "mp", None),
        P("section", "expert", None, "mp"),
        P("section", "expert", "mp"),
        P("section", "expert", "mp"),
        P("section", None, "mp"),
        P("section", "expert", "mp"),
    )
    out_specs = (P("section", "expert", "mp"), P("section", None, "mp"))
    return jax.shard_map(shards, mesh=mesh, in_specs=in_specs, out_specs=out_specs, check_vma=False)
```

```python
import functools

import jax
import jax.numpy as jnp
from jax import lax
from jax.experimental import pallas as pl
from jax.experimental.pallas import tpu as pltpu
from jax.sharding import PartitionSpec as P


def shifted(array, axis, by):
    size = lax.axis_size(axis)
    pairs = [(i, i + by) for i in range(size) if 0 <= i + by < size]
    return lax.ppermute(array, axis, pairs)


def silu_slope(pre_value):
    sig = jax.nn.sigmoid(pre_value)
    return sig * (1.0 + pre_value * (1.0 - sig))


def gated_rows(gates, rows, tok_rows):
    scaled = (gates[:, :, None] * rows.astype(jnp.float32)[:, None, :]).astype(jnp.bfloat16)
    return scaled.reshape(tok_rows * 2, rows.shape[1])


def fill_buffer(scaled, target, experts, capacity):
    width = scaled.shape[1]
    buffer = jnp.zeros((experts * capacity, width), jnp.bfloat16).at[target].set(scaled)
    return buffer.reshape(experts, capacity, width)


def slot_plan(
    out_grad,
    expert_ids,
    gate_codes,
    up_weight,
    down_weight,
    pre_act,
    conv_grad,
    conv_input,
    conv_weight,
    in_proj,
):
    grad_rows = out_grad[0]
    route_ids = expert_ids[0]
    tok_rows = grad_rows.shape[0]
    experts = lax.axis_size("expert")
    capacity = pre_act.shape[2] // experts
    gates = gate_codes[0].astype(jnp.float32) / 256.0
    flat_ids = route_ids.reshape(tok_rows * 2)
    onehot = (flat_ids[:, None] == jnp.arange(experts, dtype=jnp.int32)[None, :]).astype(jnp.int32)
    before = jnp.cumsum(onehot, axis=0) - onehot
    position = jnp.sum(before * onehot, axis=1)
    target = flat_ids * capacity + position
    whole_rows = lax.all_gather(grad_rows, "mp", axis=1, tiled=True)
    buffer = fill_buffer(gated_rows(gates, whole_rows, tok_rows), target, experts, capacity)
    arrived = lax.all_to_all(buffer, "expert", split_axis=0, concat_axis=0, tiled=True)
    slot_rows = arrived.reshape(experts * capacity, whole_rows.shape[1])
    w_down = down_weight[0, 0]
    w_up = up_weight[0, 0]
    pre_slots = pre_act[0, 0].astype(jnp.float32)
    hidden = lax.dot_general(
        slot_rows, w_down, (((1,), (1,)), ((), ())), preferred_element_type=jnp.float32
    )
    pre_grad = (hidden * silu_slope(pre_slots)).astype(jnp.bfloat16)
    partial_value = lax.dot_general(
        pre_grad, w_up, (((1,), (1,)), ((), ())), preferred_element_type=jnp.float32
    )
    share = lax.psum_scatter(partial_value, "mp", scatter_dimension=1, tiled=True).astype(
        jnp.bfloat16
    )
    returned = lax.all_to_all(
        share.reshape(experts, capacity, share.shape[1]),
        "expert",
        split_axis=0,
        concat_axis=0,
        tiled=True,
    )
    picked = returned.reshape(experts * capacity, grad_rows.shape[1])[target]
    picked = picked.astype(jnp.float32).reshape(tok_rows, 2, grad_rows.shape[1])
    moe_total = grad_rows.astype(jnp.float32) + picked[:, 0, :] + picked[:, 1, :]
    grads_here = conv_grad[0]
    inputs_here = conv_input[0]
    taps = conv_weight[0]
    kernel_size = taps.shape[0]
    next_rows = shifted(grads_here[: kernel_size - 1], "expert", -1)
    prev_rows = shifted(inputs_here[tok_rows - kernel_size + 1 :], "expert", 1)
    grad_ext = jnp.concatenate([grads_here, next_rows], axis=0).astype(jnp.float32)
    input_ext = jnp.concatenate([prev_rows, inputs_here], axis=0).astype(jnp.float32)
    grad_local = grads_here.astype(jnp.float32)
    conv_result = jnp.zeros(grads_here.shape, jnp.float32)
    tap_terms = []
    for tap in range(kernel_size):
        start = kernel_size - 1 - tap
        conv_result = conv_result + taps[tap][None, :] * grad_ext[start : start + tok_rows]
        tap_terms.append(jnp.sum(grad_local * input_ext[tap : tap + tok_rows], axis=0))
    input_grad = conv_result.astype(jnp.bfloat16)
    tap_grads = lax.psum(jnp.stack(tap_terms), "expert")
    w_proj = in_proj[0]
    proj_partial = lax.dot_general(
        input_grad,
        lax.all_gather(w_proj, "expert", axis=0, tiled=True),
        (((1,), (1,)), ((), ())),
        preferred_element_type=jnp.float32,
    )
    proj_share = lax.psum_scatter(proj_partial, "mp", scatter_dimension=1, tiled=True)
    residual = (moe_total + proj_share).astype(jnp.bfloat16)
    sent_residual = shifted(residual, "section", -1)
    return (sent_residual[None], tap_grads[None])


F32, BF16 = jnp.float32, jnp.bfloat16
VMEM_LIMIT = 14 * 1024 * 1024
HEAD = 16
LANES = 128
RIGHT = [(0, 1), (1, 2), (2, 3)]
LEFT = [(3, 2), (2, 1), (1, 0)]
NT = (((1,), (1,)), ((), ()))
TN = (((0,), (0,)), ((), ()))


def whole(memory=pltpu.VMEM):
    return pl.BlockSpec(memory_space=memory)


def rotated(array, axis, by):
    size = lax.axis_size(axis)
    return lax.ppermute(array, axis, [(i, (i + by) % size) for i in range(size)])


def around(array):
    return [array] + [rotated(array, "expert", k) for k in range(1, lax.axis_size("expert"))]


def doubling_sum(array, axis):
    size, step = lax.axis_size(axis), 1
    while step < size:
        array = array + lax.ppermute(array, axis, [(i, i ^ step) for i in range(size)])
        step *= 2
    return array


def params():
    return pltpu.CompilerParams(vmem_limit_bytes=VMEM_LIMIT)


def cost(flops, bytes_accessed):
    return pl.CostEstimate(flops=8 * flops, bytes_accessed=8 * bytes_accessed, transcendentals=0)


def square(size):
    row = lax.broadcasted_iota(jnp.int32, (size, size), 0)
    return row, lax.broadcasted_iota(jnp.int32, (size, size), 1)


def routing(columns, me):
    values = columns[...].astype(F32)
    named = jnp.where(values[:, 0:2] == me.astype(F32), 1.0, 0.0)
    gate = jnp.sum(named * values[:, 2:4], axis=1, keepdims=True) / 256.0
    return jnp.sum(named, axis=1, keepdims=True), gate


def hidden_kernel(count, place, *refs):
    routes, rows = refs[:count], refs[count : 2 * count]
    down_own, down_other, send, keep, gates, scaled = refs[2 * count :]
    tok_rows = rows[0].shape[0]
    units = down_own.shape[0]
    step = pl.program_id(0)

    @pl.when(step == 0)
    def _():
        for k in range(count):
            gates[k * tok_rows : (k + 1) * tok_rows, :] = routing(routes[k], place[1])[1]
        keep[...] = jnp.zeros_like(keep)

    for k in range(count):
        at = pl.ds(k * tok_rows, tok_rows)
        scaled[at, :] = (gates[at, :] * rows[k][...].astype(F32)).astype(BF16)
    keep[:, :units] += lax.dot_general(scaled[...], down_own[...], NT, preferred_element_type=F32)
    keep[:, units:] += lax.dot_general(scaled[...], down_other[...], NT, preferred_element_type=F32)

    @pl.when(step == pl.num_programs(0) - 1)
    def _():
        send[...] = keep[...].astype(BF16)


def route_columns(rows):
    tok_rows, width = rows.shape
    return pl.BlockSpec((tok_rows, LANES), lambda i, place: (0, width // LANES - 1))


def hidden_sums(place, rows, down, down_other):
    count = len(rows)
    tok_rows = rows[0].shape[0]
    units, half_width = down_other.shape
    tokens = count * tok_rows
    chunk = half_width // 4
    return pl.pallas_call(
        functools.partial(hidden_kernel, count),
        grid_spec=pltpu.PrefetchScalarGridSpec(
            num_scalar_prefetch=1,
            grid=(4,),
            in_specs=[route_columns(rows[0])] * count
            + [pl.BlockSpec((tok_rows, chunk), lambda i, place: (0, i))] * count
            + [
                pl.BlockSpec((units, chunk), lambda i, place: (0, 4 * place[0] + i)),
                pl.BlockSpec((units, chunk), lambda i, place: (0, i)),
            ],
            out_specs=[pl.BlockSpec((tokens, 2 * units), lambda i, place: (0, 0))] * 2,
            scratch_shapes=[pltpu.VMEM((tokens, 1), F32), pltpu.VMEM((tokens, chunk), BF16)],
        ),
        out_shape=[jax.ShapeDtypeStruct((tokens, 2 * units), dtype) for dtype in (BF16, F32)],
        compiler_params=params(),
        cost_estimate=cost(4 * tokens * half_width * units, 4 * units * half_width + 2 * tokens * half_width),
        name="hidden",
    )(place, *rows, *rows, down, down_other)


def finish_kernel(count, place, *refs):
    routes = refs[:count]
    keep, got, pre_own, pre_other, up_own, up_other, out, pre_grad = refs[count:]
    tok_rows = keep.shape[0] // count
    units = pre_own.shape[1]

    @pl.when(pl.program_id(0) == 0)
    def _():
        row, column = square(tok_rows)
        for k in range(count):
            at = pl.ds(k * tok_rows, tok_rows)
            named, _ = routing(routes[k], place[1])
            rank = jnp.sum(jnp.where(row < column, named, 0.0), axis=0, keepdims=True).astype(jnp.int32)
            named = jnp.sum(jnp.where(row == column, named, 0.0), axis=0, keepdims=True)
            pick = jnp.where(rank == row, named, 0.0).astype(BF16)
            slots = pl.ds(pl.multiple_of(place[2 + k] * tok_rows, tok_rows), tok_rows)
            for side, pre in enumerate((pre_own, pre_other)):
                here = pl.ds(side * units, units)
                p = lax.dot_general(pick, pre[slots, :], TN, preferred_element_type=F32)
                q = 1.0 / (1.0 + jnp.exp(-p))
                hidden = keep[at, here] + got[at, pl.ds((1 - side) * units, units)].astype(F32)
                pre_grad[at, here] = (hidden * (q * (1.0 + p * (1.0 - q)))).astype(BF16)

    value = lax.dot_general(pre_grad[:, :units], up_own[...], NT, preferred_element_type=F32)
    value += lax.dot_general(pre_grad[:, units:], up_other[...], NT, preferred_element_type=F32)
    out[...] = value.astype(out.dtype)


def expert_sums(place, rows, keep, got, pre, pre_other, up, up_other, dtype):
    count = len(rows)
    tokens = keep.shape[0]
    units = pre.shape[1]
    half_width = up_other.shape[0]
    chunk = half_width // 4
    return pl.pallas_call(
        functools.partial(finish_kernel, count),
        grid_spec=pltpu.PrefetchScalarGridSpec(
            num_scalar_prefetch=1,
            grid=(4,),
            in_specs=[route_columns(rows[0])] * count
            + [whole()] * 4
            + [
                pl.BlockSpec((chunk, units), lambda i, place: (4 * place[0] + i, 0)),
                pl.BlockSpec((chunk, units), lambda i, place: (i, 0)),
            ],
            out_specs=pl.BlockSpec((tokens, chunk), lambda i, place: (0, i)),
            scratch_shapes=[pltpu.VMEM((tokens, 2 * units), BF16)],
        ),
        out_shape=jax.ShapeDtypeStruct((tokens, half_width), dtype),
        compiler_params=params(),
        cost_estimate=cost(4 * tokens * half_width * units, 4 * units * half_width + 4 * tokens * half_width),
        name="experts",
    )(place, *rows, keep, got, pre, pre_other, up, up_other)


def proj_kernel(count, with_taps, place, *refs):
    grads, heads = refs[:count], refs[count : 2 * count]
    taps, weight = refs[2 * count : 2 * count + 2]
    refs = refs[2 * count + 2 :]
    if with_taps:
        inputs, send, keep, tap_out, ext, scaled = refs
    else:
        send, keep, ext, scaled = refs
    tok_rows, chunk = grads[0].shape
    kernel_size = taps.shape[0]
    step = pl.program_id(0)

    tap = taps[...]
    for k in range(count):
        ext[:tok_rows, :] = grads[k][...].astype(F32)
        follows = (place[2 + k] < lax.axis_size("expert") - 1).astype(F32)
        ext[tok_rows:, :] = heads[k][...].astype(F32) * follows
        result = jnp.zeros((tok_rows, chunk), F32)
        for j in range(kernel_size):
            start = kernel_size - 1 - j
            result = result + tap[j : j + 1, :] * ext[start : start + tok_rows, :]
        scaled[k * tok_rows : (k + 1) * tok_rows, :] = result.astype(BF16)
        if with_taps and k == 0:
            values = inputs[...].astype(F32)
            for j in range(kernel_size):
                start = kernel_size - 1 - j
                terms = values * ext[start : start + tok_rows, :]
                tap_out[j : j + 1, :] = jnp.sum(terms, axis=0, keepdims=True)

    product = lax.dot_general(scaled[...], weight[...], NT, preferred_element_type=F32)

    @pl.when(step == 0)
    def _():
        keep[...] = product

    @pl.when(step > 0)
    def _():
        keep[...] += product

    @pl.when(step == pl.num_programs(0) - 1)
    def _():
        send[...] = keep[...].astype(BF16)


def proj_sums(place, grads, heads, taps, weight, inputs=None):
    count = len(grads)
    tok_rows, half_width = grads[0].shape
    block = weight.shape[0]
    tokens = count * tok_rows
    chunk = half_width // 4
    with_taps = inputs is not None

    def wide(rows):
        return pl.BlockSpec((rows, chunk), lambda i: (0, i))

    last = [wide(tok_rows)] if with_taps else []
    out_specs = [pl.BlockSpec((tokens, block), lambda i: (0, 0))] * 2
    out_shape = [jax.ShapeDtypeStruct((tokens, block), BF16), jax.ShapeDtypeStruct((tokens, block), F32)]
    if with_taps:
        out_specs = out_specs + [wide(taps.shape[0])]
        out_shape = out_shape + [jax.ShapeDtypeStruct(taps.shape, F32)]
    return pl.pallas_call(
        functools.partial(proj_kernel, count, with_taps),
        grid=(half_width // chunk,),
        in_specs=[whole(pltpu.SMEM)]
        + [wide(tok_rows)] * count
        + [wide(HEAD)] * count
        + [wide(taps.shape[0]), wide(block)]
        + last,
        out_specs=out_specs,
        out_shape=out_shape,
        scratch_shapes=[pltpu.VMEM((tok_rows + HEAD, chunk), F32), pltpu.VMEM((tokens, chunk), BF16)],
        compiler_params=params(),
        cost_estimate=cost(
            2 * tokens * half_width * block, 2 * (block + tokens) * half_width + 6 * tokens * block
        ),
        name="projection",
    )(place, *grads, *heads, taps, weight, *([inputs] if with_taps else []))


def combine_kernel(place, grad, sums, back_right, back_left, proj_keep, proj_got, to_right, to_left, own, total):
    half, me = place[0], place[1]
    rows, part = grad.shape[0], proj_keep.shape[1]
    total[0:rows, :] = grad[...].astype(F32) + sums[0:rows, :]
    total[rows : 2 * rows, :] = sums[rows : 2 * rows, :] + back_left[...].astype(F32)
    total[2 * rows :, :] = sums[2 * rows :, :] + back_right[...].astype(F32)

    @pl.when(me // 2 == half)
    def _():
        at = pl.ds(pl.multiple_of(lax.rem(me, 2) * part, part), part)
        total[:, at] += proj_keep[...] + proj_got[...].astype(F32)

    own[...] = total[0:rows, :]
    to_left[...] = total[rows : 2 * rows, :].astype(BF16)
    to_right[...] = total[2 * rows :, :].astype(BF16)


def combined(place, grad, sums, *arrays):
    outs = [jax.ShapeDtypeStruct(grad.shape, dtype) for dtype in (BF16, BF16, F32)]
    return pl.pallas_call(
        combine_kernel,
        in_specs=[whole(pltpu.SMEM)] + [whole()] * (2 + len(arrays)),
        out_specs=[whole()] * 3,
        out_shape=outs,
        scratch_shapes=[pltpu.VMEM(sums.shape, F32)],
        compiler_params=params(),
        cost_estimate=cost(8 * grad.size, 40 * grad.size),
        name="combine",
    )(place, grad, sums, *arrays)


def final_kernel(place, residual, far, end, out, total):
    half, me = place[0], place[1]
    experts = lax.axis_size("expert")
    part = far.shape[1]
    total[...] = residual[...].astype(F32)

    def add(source, value):
        @pl.when((source < experts) & (source // 2 == half))
        def _():
            at = pl.ds(pl.multiple_of(lax.rem(source, 2) * part, part), part)
            total[:, at] += value[...].astype(F32)

    add(lax.rem(me + 2, experts), far)
    add(jnp.where(lax.rem(me, experts - 1) == 0, experts - 1 - me, experts), end)
    out[...] = total[...].astype(BF16)


def final_sum(place, residual, far, end):
    return pl.pallas_call(
        final_kernel,
        in_specs=[whole(pltpu.SMEM)] + [whole()] * 3,
        out_specs=whole(),
        out_shape=jax.ShapeDtypeStruct(residual.shape, BF16),
        scratch_shapes=[pltpu.VMEM(residual.shape, F32)],
        compiler_params=params(),
        cost_estimate=cost(4 * residual.size, 8 * residual.size),
        name="residual",
    )(place, residual, far, end)


def moved(array, pairs):
    return lax.ppermute(array, "expert", pairs)


def swapped(array):
    return rotated(array, "mp", 1)


def together(*arrays):
    return lax.optimization_barrier(arrays)


def token_plan(
    out_grad,
    expert_ids,
    gate_codes,
    up_weight,
    down_weight,
    pre_act,
    conv_grad,
    conv_input,
    conv_weight,
    in_proj,
):
    me, half = lax.axis_index("expert"), lax.axis_index("mp")
    experts = lax.axis_size("expert")

    def place(*blocks):
        return jnp.stack([half, me, *blocks]).astype(jnp.int32)

    far_block, end_block = (me + 2) % experts, jnp.where(me == 0, experts - 1, 0)
    near = place(me, jnp.maximum(me - 1, 0), jnp.minimum(me + 1, experts - 1))
    rows_own, conv_own = out_grad[0], conv_grad[0]
    tok_rows, half_width = rows_own.shape
    w_down, w_up, pre = down_weight[0, 0], up_weight[0, 0], pre_act[0, 0]
    taps, w_proj = conv_weight[0], in_proj[0]

    routes = jnp.concatenate([expert_ids[0], gate_codes[0]], axis=1).astype(BF16)
    rows_own = jnp.concatenate([rows_own, jnp.pad(routes, ((0, 0), (0, LANES - routes.shape[1])))], axis=1)
    down_send = lax.dynamic_slice_in_dim(w_down, (1 - half) * half_width, half_width, 1)
    rows_left, rows_right = moved(rows_own, RIGHT), moved(rows_own, LEFT)
    down_other = swapped(down_send)
    up_send = lax.dynamic_slice_in_dim(w_up, (1 - half) * half_width, half_width, 0)
    rows_left, rows_right, down_other, up_send = together(rows_left, rows_right, down_other, up_send)

    def hidden(where, rows):
        send, keep = hidden_sums(where, rows, w_down, down_other)
        return keep, swapped(send)

    def finish(where, rows, keep, got, dtype):
        return expert_sums(where, rows, keep, got, pre, pre_other, w_up, up_other, dtype)

    near_rows = [rows_own, rows_left, rows_right]
    from_left, from_right = moved(rows_left, RIGHT[1:]), moved(rows_right, LEFT[1:])
    near_keep, near_got = hidden(near, near_rows)
    from_left, from_right, near_keep, up_send, pre_send = together(from_left, from_right, near_keep, up_send, pre)

    far, end = place(far_block), place(end_block)
    rows_far = jnp.where(me >= 2, from_left, from_right)
    rows_end = moved(rows_far, [(2, 3), (1, 0)])
    up_other, pre_other = swapped(up_send), swapped(pre_send)
    far_keep, far_got = hidden(far, [rows_far])
    next_head = moved(conv_own[:HEAD], [(2, 0), (3, 1)])
    last_head = moved(conv_own[:HEAD], [(3, 0)])
    rows_end, far_keep, up_other, pre_other, next_head, last_head, conv_own = together(
        rows_end, far_keep, up_other, pre_other, next_head, last_head, conv_own
    )

    conv_left, conv_right = moved(conv_own, RIGHT), moved(conv_own, LEFT)
    end_keep, end_got = hidden(end, [rows_end])
    far_sums = finish(far, [rows_far], far_keep, far_got, F32)
    end_sums = finish(end, [rows_end], end_keep, end_got, BF16)
    conv_left, conv_right, end_sums, far_sums = together(conv_left, conv_right, end_sums, far_sums)

    from_left, from_right = moved(conv_left, RIGHT[1:]), moved(conv_right, LEFT[1:])
    back_end = moved(end_sums, [(0, 1), (3, 2)])
    gather = [(e * 2 + 1 - e // 2, e * 2 + e // 2) for e in range(experts)]

    def proj(where, grads, heads, *inputs):
        send, keep, *tap_terms = proj_sums(where, grads, heads, taps, w_proj, *inputs)
        return keep, lax.ppermute(send, ("expert", "mp"), gather), *tap_terms

    near_proj, near_proj_got, tap_terms = proj(
        near, [conv_own, conv_left, conv_right], [conv_right, conv_own, next_head], conv_input[0]
    )
    from_left, from_right, near_proj, conv_left, near_keep = together(
        from_left, from_right, near_proj, conv_left, near_keep
    )

    conv_far = jnp.where(me >= 2, from_left, from_right)
    conv_far, back_end = together(conv_far, back_end)
    conv_end = moved(conv_far, [(2, 3), (1, 0)])
    back = (far_sums + back_end.astype(F32)).astype(BF16)
    back_right, back_left = moved(back, RIGHT[:2]), moved(back, LEFT[:2])
    far_head = jnp.where(me >= 2, conv_left[:HEAD], last_head)
    near_sums = finish(near, near_rows, near_keep, near_got, F32)
    near_sums, conv_far = together(near_sums, conv_far)
    far_proj, far_proj_got = proj(far, [conv_far], [far_head])
    conv_end, back_right, back_left, far_proj, near_sums = together(
        conv_end, back_right, back_left, far_proj, near_sums
    )

    to_right, to_left, own = combined(near, out_grad[0], near_sums, back_right, back_left, near_proj, near_proj_got)
    to_right, to_left, conv_end = together(to_right, to_left, conv_end)
    to_right, to_left = moved(to_right, RIGHT), moved(to_left, LEFT)
    end_proj, end_proj_got = proj(end, [conv_end], [conv_far])
    to_right, to_left, end_proj = together(to_right, to_left, end_proj)

    residual = (own + to_right.astype(F32) + to_left.astype(F32)).astype(BF16)
    sections, cores = lax.axis_size("section"), lax.axis_size("mp")

    def deliver(keep, got, pairs):
        def at(s, e, m):
            return (s * experts + e) * cores + m

        moves = [(at(s, e, e // 2), at(s - 1, d, e // 2)) for s in range(1, sections) for e, d in pairs]
        return lax.ppermute((keep + got.astype(F32)).astype(BF16), ("section", "expert", "mp"), moves)

    residual = shifted(residual, "section", -1)
    far_piece = deliver(far_proj, far_proj_got, [(e, (e + 2) % experts) for e in range(experts)])
    end_piece = deliver(end_proj, end_proj_got, [(0, experts - 1), (experts - 1, 0)])
    tap_grads = doubling_sum(tap_terms, "expert")
    residual = final_sum(near, residual, far_piece, end_piece)
    return (residual[None], tap_grads[None])


def shards(*arrays):
    experts, halves = lax.axis_size("expert"), lax.axis_size("mp")
    capacity = arrays[5].shape[2] // experts
    dense = capacity == arrays[0].shape[1] and experts == 4 and halves == 2
    return (token_plan if dense else slot_plan)(*arrays)


def solution(mesh):
    in_specs = (
        P("section", "expert", "mp"),
        P("section", "expert", None),
        P("section", "expert", None),
        P("section", "expert", None, "mp"),
        P("section", "expert", "mp", None),
        P("section", "expert", None, "mp"),
        P("section", "expert", "mp"),
        P("section", "expert", "mp"),
        P("section", None, "mp"),
        P("section", "expert", "mp"),
    )
    out_specs = (P("section", "expert", "mp"), P("section", None, "mp"))
    return jax.shard_map(shards, mesh=mesh, in_specs=in_specs, out_specs=out_specs, check_vma=False)
```

```python
import functools

import jax
import jax.numpy as jnp
from jax import lax
from jax.experimental import pallas as pl
from jax.experimental.pallas import tpu as pltpu
from jax.sharding import PartitionSpec as P


def shifted(array, axis, by):
    size = lax.axis_size(axis)
    pairs = [(i, i + by) for i in range(size) if 0 <= i + by < size]
    return lax.ppermute(array, axis, pairs)


def silu_slope(pre_value):
    sig = jax.nn.sigmoid(pre_value)
    return sig * (1.0 + pre_value * (1.0 - sig))


def gated_rows(gates, rows, tok_rows):
    scaled = (gates[:, :, None] * rows.astype(jnp.float32)[:, None, :]).astype(jnp.bfloat16)
    return scaled.reshape(tok_rows * 2, rows.shape[1])


def fill_buffer(scaled, target, experts, capacity):
    width = scaled.shape[1]
    buffer = jnp.zeros((experts * capacity, width), jnp.bfloat16).at[target].set(scaled)
    return buffer.reshape(experts, capacity, width)


def slot_plan(
    out_grad,
    expert_ids,
    gate_codes,
    up_weight,
    down_weight,
    pre_act,
    conv_grad,
    conv_input,
    conv_weight,
    in_proj,
):
    grad_rows = out_grad[0]
    route_ids = expert_ids[0]
    tok_rows = grad_rows.shape[0]
    experts = lax.axis_size("expert")
    capacity = pre_act.shape[2] // experts
    gates = gate_codes[0].astype(jnp.float32) / 256.0
    flat_ids = route_ids.reshape(tok_rows * 2)
    onehot = (flat_ids[:, None] == jnp.arange(experts, dtype=jnp.int32)[None, :]).astype(jnp.int32)
    before = jnp.cumsum(onehot, axis=0) - onehot
    position = jnp.sum(before * onehot, axis=1)
    target = flat_ids * capacity + position
    whole_rows = lax.all_gather(grad_rows, "mp", axis=1, tiled=True)
    buffer = fill_buffer(gated_rows(gates, whole_rows, tok_rows), target, experts, capacity)
    arrived = lax.all_to_all(buffer, "expert", split_axis=0, concat_axis=0, tiled=True)
    slot_rows = arrived.reshape(experts * capacity, whole_rows.shape[1])
    w_down = down_weight[0, 0]
    w_up = up_weight[0, 0]
    pre_slots = pre_act[0, 0].astype(jnp.float32)
    hidden = lax.dot_general(
        slot_rows, w_down, (((1,), (1,)), ((), ())), preferred_element_type=jnp.float32
    )
    pre_grad = (hidden * silu_slope(pre_slots)).astype(jnp.bfloat16)
    partial_value = lax.dot_general(
        pre_grad, w_up, (((1,), (1,)), ((), ())), preferred_element_type=jnp.float32
    )
    share = lax.psum_scatter(partial_value, "mp", scatter_dimension=1, tiled=True).astype(
        jnp.bfloat16
    )
    returned = lax.all_to_all(
        share.reshape(experts, capacity, share.shape[1]),
        "expert",
        split_axis=0,
        concat_axis=0,
        tiled=True,
    )
    picked = returned.reshape(experts * capacity, grad_rows.shape[1])[target]
    picked = picked.astype(jnp.float32).reshape(tok_rows, 2, grad_rows.shape[1])
    moe_total = grad_rows.astype(jnp.float32) + picked[:, 0, :] + picked[:, 1, :]
    grads_here = conv_grad[0]
    inputs_here = conv_input[0]
    taps = conv_weight[0]
    kernel_size = taps.shape[0]
    next_rows = shifted(grads_here[: kernel_size - 1], "expert", -1)
    prev_rows = shifted(inputs_here[tok_rows - kernel_size + 1 :], "expert", 1)
    grad_ext = jnp.concatenate([grads_here, next_rows], axis=0).astype(jnp.float32)
    input_ext = jnp.concatenate([prev_rows, inputs_here], axis=0).astype(jnp.float32)
    grad_local = grads_here.astype(jnp.float32)
    conv_result = jnp.zeros(grads_here.shape, jnp.float32)
    tap_terms = []
    for tap in range(kernel_size):
        start = kernel_size - 1 - tap
        conv_result = conv_result + taps[tap][None, :] * grad_ext[start : start + tok_rows]
        tap_terms.append(jnp.sum(grad_local * input_ext[tap : tap + tok_rows], axis=0))
    input_grad = conv_result.astype(jnp.bfloat16)
    tap_grads = lax.psum(jnp.stack(tap_terms), "expert")
    w_proj = in_proj[0]
    proj_partial = lax.dot_general(
        input_grad,
        lax.all_gather(w_proj, "expert", axis=0, tiled=True),
        (((1,), (1,)), ((), ())),
        preferred_element_type=jnp.float32,
    )
    proj_share = lax.psum_scatter(proj_partial, "mp", scatter_dimension=1, tiled=True)
    residual = (moe_total + proj_share).astype(jnp.bfloat16)
    sent_residual = shifted(residual, "section", -1)
    return (sent_residual[None], tap_grads[None])


F32, BF16 = jnp.float32, jnp.bfloat16
VMEM_LIMIT = 14 * 1024 * 1024
HEAD = 16
LANES = 128
RIGHT = [(0, 1), (1, 2), (2, 3)]
LEFT = [(3, 2), (2, 1), (1, 0)]
NT = (((1,), (1,)), ((), ()))
TN = (((0,), (0,)), ((), ()))


def whole(memory=pltpu.VMEM):
    return pl.BlockSpec(memory_space=memory)


def rotated(array, axis, by):
    size = lax.axis_size(axis)
    return lax.ppermute(array, axis, [(i, (i + by) % size) for i in range(size)])


def around(array):
    return [array] + [rotated(array, "expert", k) for k in range(1, lax.axis_size("expert"))]


def doubling_sum(array, axis):
    size, step = lax.axis_size(axis), 1
    while step < size:
        array = array + lax.ppermute(array, axis, [(i, i ^ step) for i in range(size)])
        step *= 2
    return array


def params():
    return pltpu.CompilerParams(vmem_limit_bytes=VMEM_LIMIT)


def cost(flops, bytes_accessed):
    return pl.CostEstimate(flops=8 * flops, bytes_accessed=8 * bytes_accessed, transcendentals=0)


def square(size):
    row = lax.broadcasted_iota(jnp.int32, (size, size), 0)
    return row, lax.broadcasted_iota(jnp.int32, (size, size), 1)


def routing(columns, me):
    values = columns[...].astype(F32)
    named = jnp.where(values[:, 0:2] == me.astype(F32), 1.0, 0.0)
    gate = jnp.sum(named * values[:, 2:4], axis=1, keepdims=True) / 256.0
    return jnp.sum(named, axis=1, keepdims=True), gate


def hidden_kernel(count, place, *refs):
    routes, rows = refs[:count], refs[count : 2 * count]
    down_own, down_other, send, keep, gates, scaled = refs[2 * count :]
    tok_rows = rows[0].shape[0]
    units = down_own.shape[0]
    step = pl.program_id(0)

    @pl.when(step == 0)
    def _():
        for k in range(count):
            gates[k * tok_rows : (k + 1) * tok_rows, :] = routing(routes[k], place[1])[1]
        keep[...] = jnp.zeros_like(keep)

    for k in range(count):
        at = pl.ds(k * tok_rows, tok_rows)
        scaled[at, :] = (gates[at, :] * rows[k][...].astype(F32)).astype(BF16)
    keep[:, :units] += lax.dot_general(scaled[...], down_own[...], NT, preferred_element_type=F32)
    keep[:, units:] += lax.dot_general(scaled[...], down_other[...], NT, preferred_element_type=F32)

    @pl.when(step == pl.num_programs(0) - 1)
    def _():
        send[...] = keep[...].astype(BF16)


def route_columns(rows):
    tok_rows, width = rows.shape
    return pl.BlockSpec((tok_rows, LANES), lambda i, place: (0, width // LANES - 1))


def hidden_sums(place, rows, down, down_other):
    count = len(rows)
    tok_rows = rows[0].shape[0]
    units, half_width = down_other.shape
    tokens = count * tok_rows
    chunk = half_width // 4
    return pl.pallas_call(
        functools.partial(hidden_kernel, count),
        grid_spec=pltpu.PrefetchScalarGridSpec(
            num_scalar_prefetch=1,
            grid=(4,),
            in_specs=[route_columns(rows[0])] * count
            + [pl.BlockSpec((tok_rows, chunk), lambda i, place: (0, i))] * count
            + [
                pl.BlockSpec((units, chunk), lambda i, place: (0, 4 * place[0] + i)),
                pl.BlockSpec((units, chunk), lambda i, place: (0, i)),
            ],
            out_specs=[pl.BlockSpec((tokens, 2 * units), lambda i, place: (0, 0))] * 2,
            scratch_shapes=[pltpu.VMEM((tokens, 1), F32), pltpu.VMEM((tokens, chunk), BF16)],
        ),
        out_shape=[jax.ShapeDtypeStruct((tokens, 2 * units), dtype) for dtype in (BF16, F32)],
        compiler_params=params(),
        cost_estimate=cost(4 * tokens * half_width * units, 4 * units * half_width + 2 * tokens * half_width),
        name="hidden",
    )(place, *rows, *rows, down, down_other)


def finish_kernel(count, place, *refs):
    routes = refs[:count]
    keep, got, pre_own, pre_other, up_own, up_other, out, pre_grad = refs[count:]
    tok_rows = pre_grad.shape[0] // count
    units = pre_own.shape[1]

    @pl.when(pl.program_id(0) == 0)
    def _():
        row, column = square(tok_rows)
        for k in range(count):
            at = pl.ds(k * tok_rows, tok_rows)
            named, _ = routing(routes[k], place[1])
            rank = jnp.sum(jnp.where(row < column, named, 0.0), axis=0, keepdims=True).astype(jnp.int32)
            named = jnp.sum(jnp.where(row == column, named, 0.0), axis=0, keepdims=True)
            pick = jnp.where(rank == row, named, 0.0).astype(BF16)
            slots = pl.ds(pl.multiple_of(place[2 + k] * tok_rows, tok_rows), tok_rows)
            for side, pre in enumerate((pre_own, pre_other)):
                here = pl.ds(side * units, units)
                p = lax.dot_general(pick, pre[slots, :], TN, preferred_element_type=F32)
                q = 1.0 / (1.0 + jnp.exp(-p))
                hidden = keep[at, here] + got[at, pl.ds((1 - side) * units, units)].astype(F32)
                pre_grad[at, here] = (hidden * (q * (1.0 + p * (1.0 - q)))).astype(BF16)

    value = lax.dot_general(pre_grad[:, :units], up_own[...], NT, preferred_element_type=F32)
    value += lax.dot_general(pre_grad[:, units:], up_other[...], NT, preferred_element_type=F32)
    out[...] = value.astype(out.dtype)


def expert_sums(place, rows, keep, got, pre, pre_other, up, up_other, dtype):
    count = len(rows)
    tokens = count * rows[0].shape[0]
    units = pre.shape[1]
    half_width = up_other.shape[0]
    chunk = half_width // 4
    return pl.pallas_call(
        functools.partial(finish_kernel, count),
        grid_spec=pltpu.PrefetchScalarGridSpec(
            num_scalar_prefetch=1,
            grid=(4,),
            in_specs=[route_columns(rows[0])] * count
            + [whole()] * 4
            + [
                pl.BlockSpec((chunk, units), lambda i, place: (4 * place[0] + i, 0)),
                pl.BlockSpec((chunk, units), lambda i, place: (i, 0)),
            ],
            out_specs=pl.BlockSpec((tokens, chunk), lambda i, place: (0, i)),
            scratch_shapes=[pltpu.VMEM((tokens, 2 * units), BF16)],
        ),
        out_shape=jax.ShapeDtypeStruct((tokens, half_width), dtype),
        compiler_params=params(),
        cost_estimate=cost(4 * tokens * half_width * units, 4 * units * half_width + 4 * tokens * half_width),
        name="experts",
    )(place, *rows, keep, got, pre, pre_other, up, up_other)


def proj_kernel(count, with_taps, place, *refs):
    grads, heads = refs[:count], refs[count : 2 * count]
    taps, weight = refs[2 * count : 2 * count + 2]
    refs = refs[2 * count + 2 :]
    if with_taps:
        inputs, send, keep, tap_out, ext, scaled = refs
    else:
        send, keep, ext, scaled = refs
    tok_rows, chunk = grads[0].shape
    kernel_size = taps.shape[0]
    step = pl.program_id(0)

    tap = taps[...]
    for k in range(count):
        ext[:tok_rows, :] = grads[k][...].astype(F32)
        follows = (place[2 + k] < lax.axis_size("expert") - 1).astype(F32)
        ext[tok_rows:, :] = heads[k][...].astype(F32) * follows
        result = jnp.zeros((tok_rows, chunk), F32)
        for j in range(kernel_size):
            start = kernel_size - 1 - j
            result = result + tap[j : j + 1, :] * ext[start : start + tok_rows, :]
        scaled[k * tok_rows : (k + 1) * tok_rows, :] = result.astype(BF16)
        if with_taps and k == 0:
            values = inputs[...].astype(F32)
            for j in range(kernel_size):
                start = kernel_size - 1 - j
                terms = values * ext[start : start + tok_rows, :]
                tap_out[j : j + 1, :] = jnp.sum(terms, axis=0, keepdims=True)

    product = lax.dot_general(scaled[...], weight[...], NT, preferred_element_type=F32)

    @pl.when(step == 0)
    def _():
        keep[...] = product

    @pl.when(step > 0)
    def _():
        keep[...] += product

    @pl.when(step == pl.num_programs(0) - 1)
    def _():
        send[...] = keep[...].astype(BF16)


def proj_sums(place, grads, heads, taps, weight, inputs=None):
    count = len(grads)
    tok_rows, half_width = grads[0].shape
    block = weight.shape[0]
    tokens = count * tok_rows
    chunk = half_width // 4
    with_taps = inputs is not None

    def wide(rows):
        return pl.BlockSpec((rows, chunk), lambda i: (0, i))

    last = [wide(tok_rows)] if with_taps else []
    out_specs = [pl.BlockSpec((tokens, block), lambda i: (0, 0))] * 2
    out_shape = [jax.ShapeDtypeStruct((tokens, block), BF16), jax.ShapeDtypeStruct((tokens, block), F32)]
    if with_taps:
        out_specs = out_specs + [wide(taps.shape[0])]
        out_shape = out_shape + [jax.ShapeDtypeStruct(taps.shape, F32)]
    return pl.pallas_call(
        functools.partial(proj_kernel, count, with_taps),
        grid=(half_width // chunk,),
        in_specs=[whole(pltpu.SMEM)]
        + [wide(tok_rows)] * count
        + [wide(HEAD)] * count
        + [wide(taps.shape[0]), wide(block)]
        + last,
        out_specs=out_specs,
        out_shape=out_shape,
        scratch_shapes=[pltpu.VMEM((tok_rows + HEAD, chunk), F32), pltpu.VMEM((tokens, chunk), BF16)],
        compiler_params=params(),
        cost_estimate=cost(
            2 * tokens * half_width * block, 2 * (block + tokens) * half_width + 6 * tokens * block
        ),
        name="projection",
    )(place, *grads, *heads, taps, weight, *([inputs] if with_taps else []))


def combine_kernel(place, grad, sums, back_right, back_left, proj_keep, proj_got, to_right, to_left, own, total):
    half, me = place[0], place[1]
    rows, part = grad.shape[0], proj_keep.shape[1]
    total[0:rows, :] = grad[...].astype(F32) + sums[0:rows, :]
    total[rows : 2 * rows, :] = sums[rows : 2 * rows, :] + back_left[...].astype(F32)
    total[2 * rows :, :] = sums[2 * rows :, :] + back_right[...].astype(F32)

    @pl.when(me // 2 == half)
    def _():
        at = pl.ds(pl.multiple_of(lax.rem(me, 2) * part, part), part)
        total[:, at] += proj_keep[...] + proj_got[...].astype(F32)

    own[...] = total[0:rows, :]
    to_left[...] = total[rows : 2 * rows, :].astype(BF16)
    to_right[...] = total[2 * rows :, :].astype(BF16)


def combined(place, grad, sums, *arrays):
    outs = [jax.ShapeDtypeStruct(grad.shape, dtype) for dtype in (BF16, BF16, F32)]
    return pl.pallas_call(
        combine_kernel,
        in_specs=[whole(pltpu.SMEM)] + [whole()] * (2 + len(arrays)),
        out_specs=[whole()] * 3,
        out_shape=outs,
        scratch_shapes=[pltpu.VMEM(sums.shape, F32)],
        compiler_params=params(),
        cost_estimate=cost(8 * grad.size, 40 * grad.size),
        name="combine",
    )(place, grad, sums, *arrays)


def final_kernel(place, residual, far, end, out, total):
    half, me = place[0], place[1]
    experts = lax.axis_size("expert")
    part = far.shape[1]
    total[...] = residual[...].astype(F32)

    def add(source, value):
        @pl.when((source < experts) & (source // 2 == half))
        def _():
            at = pl.ds(pl.multiple_of(lax.rem(source, 2) * part, part), part)
            total[:, at] += value[...].astype(F32)

    add(lax.rem(me + 2, experts), far)
    add(jnp.where(lax.rem(me, experts - 1) == 0, experts - 1 - me, experts), end)
    out[...] = total[...].astype(BF16)


def final_sum(place, residual, far, end):
    return pl.pallas_call(
        final_kernel,
        in_specs=[whole(pltpu.SMEM)] + [whole()] * 3,
        out_specs=whole(),
        out_shape=jax.ShapeDtypeStruct(residual.shape, BF16),
        scratch_shapes=[pltpu.VMEM(residual.shape, F32)],
        compiler_params=params(),
        cost_estimate=cost(4 * residual.size, 8 * residual.size),
        name="residual",
    )(place, residual, far, end)


def moved(array, pairs):
    return lax.ppermute(array, "expert", pairs)


def swapped(array):
    return rotated(array, "mp", 1)


def together(*arrays):
    return lax.optimization_barrier(arrays)


def token_plan(
    out_grad,
    expert_ids,
    gate_codes,
    up_weight,
    down_weight,
    pre_act,
    conv_grad,
    conv_input,
    conv_weight,
    in_proj,
):
    me, half = lax.axis_index("expert"), lax.axis_index("mp")
    experts = lax.axis_size("expert")

    def place(*blocks):
        return jnp.stack([half, me, *blocks]).astype(jnp.int32)

    far_block, end_block = (me + 2) % experts, jnp.where(me == 0, experts - 1, 0)
    near = place(me, jnp.maximum(me - 1, 0), jnp.minimum(me + 1, experts - 1))
    rows_own, conv_own = out_grad[0], conv_grad[0]
    tok_rows, half_width = rows_own.shape
    w_down, w_up, pre = down_weight[0, 0], up_weight[0, 0], pre_act[0, 0]
    taps, w_proj = conv_weight[0], in_proj[0]

    routes = jnp.concatenate([expert_ids[0], gate_codes[0]], axis=1).astype(BF16)
    rows_own = jnp.concatenate([rows_own, jnp.pad(routes, ((0, 0), (0, LANES - routes.shape[1])))], axis=1)
    rows_left, rows_right = moved(rows_own, RIGHT), moved(rows_own, LEFT)
    down_send = lax.dynamic_slice_in_dim(w_down, (1 - half) * half_width, half_width, 1)
    up_send = lax.dynamic_slice_in_dim(w_up, (1 - half) * half_width, half_width, 0)
    rows_left, rows_right, down_send, up_send, pre_send, head = together(
        rows_left, rows_right, down_send, up_send, pre, conv_own[:HEAD]
    )

    from_left, from_right = moved(rows_left, RIGHT[1:]), moved(rows_right, LEFT[1:])
    down_other, pre_other = swapped(down_send), swapped(pre_send)
    next_head = moved(head, [(2, 0), (3, 1)])
    from_left, from_right, down_other, pre_other, up_send, next_head = together(
        from_left, from_right, down_other, pre_other, up_send, next_head
    )

    def hidden(where, rows):
        send, keep = hidden_sums(where, rows, w_down, down_other)
        return keep, swapped(send)

    def finish(where, rows, sums, dtype):
        return expert_sums(where, rows, *sums, pre, pre_other, w_up, up_other, dtype)

    far, end = place(far_block), place(end_block)
    rows_far = jnp.where(me >= 2, from_left, from_right)
    rows_end = moved(rows_far, [(2, 3), (1, 0)])
    up_other = swapped(up_send)
    near_rows = [rows_own, rows_left, rows_right]
    keep, got = hidden(near, near_rows)
    rows_end, rows_far, keep, up_other, conv_own = together(rows_end, rows_far, keep, up_other, conv_own)

    conv_left, conv_right = moved(conv_own, RIGHT), moved(conv_own, LEFT)
    end_hidden = hidden(end, [rows_end])
    far_keep, far_got = hidden(far, [rows_far])
    end_sums = finish(end, [rows_end], end_hidden, BF16)
    conv_left, conv_right, end_sums, keep, far_keep = together(conv_left, conv_right, end_sums, keep, far_keep)

    from_left, from_right = moved(conv_left, RIGHT[1:]), moved(conv_right, LEFT[1:])
    back_end = moved(end_sums, [(0, 1), (3, 2)])
    gather = [(e * 2 + 1 - e // 2, e * 2 + e // 2) for e in range(experts)]

    def proj(where, grads, heads, *inputs):
        send, keep, *tap_terms = proj_sums(where, grads, heads, taps, w_proj, *inputs)
        return keep, lax.ppermute(send, ("expert", "mp"), gather), *tap_terms

    near_proj, near_proj_got, tap_terms = proj(
        near, [conv_own, conv_left, conv_right], [conv_right, conv_own, next_head], conv_input[0]
    )
    far_sums = finish(far, [rows_far], (far_keep, far_got), F32)
    from_left, from_right, near_proj, conv_left, keep, far_sums = together(
        from_left, from_right, near_proj, conv_left, keep, far_sums
    )

    conv_far = jnp.where(me >= 2, from_left, from_right)
    conv_far, back_end = together(conv_far, back_end)
    conv_end = moved(conv_far, [(2, 3), (1, 0)])
    back = (far_sums + back_end.astype(F32)).astype(BF16)
    back_right, back_left = moved(back, RIGHT[:2]), moved(back, LEFT[:2])
    near_sums = finish(near, near_rows, (keep, got), F32)
    conv_end, back_right, back_left, near_sums = together(conv_end, back_right, back_left, near_sums)

    to_right, to_left, own = combined(near, out_grad[0], near_sums, back_right, back_left, near_proj, near_proj_got)
    to_right, to_left, conv_end = together(to_right, to_left, conv_end)
    to_right, to_left = moved(to_right, RIGHT), moved(to_left, LEFT)
    far_head = jnp.where(me >= 2, conv_left[:HEAD], conv_end[:HEAD])
    proj_keep, proj_got = proj(place(far_block, end_block), [conv_far, conv_end], [far_head, conv_far])
    to_right, to_left, proj_keep = together(to_right, to_left, proj_keep)

    residual = (own + to_right.astype(F32) + to_left.astype(F32)).astype(BF16)
    sections, cores = lax.axis_size("section"), lax.axis_size("mp")

    def deliver(keep, got, pairs):
        def at(s, e, m):
            return (s * experts + e) * cores + m

        moves = [(at(s, e, e // 2), at(s - 1, d, e // 2)) for s in range(1, sections) for e, d in pairs]
        return lax.ppermute((keep + got.astype(F32)).astype(BF16), ("section", "expert", "mp"), moves)

    residual = shifted(residual, "section", -1)
    far_piece = deliver(proj_keep[:tok_rows], proj_got[:tok_rows], [(e, (e + 2) % experts) for e in range(experts)])
    end_piece = deliver(proj_keep[tok_rows:], proj_got[tok_rows:], [(0, experts - 1), (experts - 1, 0)])
    tap_grads = doubling_sum(tap_terms, "expert")
    residual = final_sum(near, residual, far_piece, end_piece)
    return (residual[None], tap_grads[None])


def shards(*arrays):
    experts, halves = lax.axis_size("expert"), lax.axis_size("mp")
    capacity = arrays[5].shape[2] // experts
    dense = capacity == arrays[0].shape[1] and experts == 4 and halves == 2
    return (token_plan if dense else slot_plan)(*arrays)


def solution(mesh):
    in_specs = (
        P("section", "expert", "mp"),
        P("section", "expert", None),
        P("section", "expert", None),
        P("section", "expert", None, "mp"),
        P("section", "expert", "mp", None),
        P("section", "expert", None, "mp"),
        P("section", "expert", "mp"),
        P("section", "expert", "mp"),
        P("section", None, "mp"),
        P("section", "expert", "mp"),
    )
    out_specs = (P("section", "expert", "mp"), P("section", None, "mp"))
    return jax.shard_map(shards, mesh=mesh, in_specs=in_specs, out_specs=out_specs, check_vma=False)
```

```python
import functools

import jax
import jax.numpy as jnp
from jax import lax
from jax.experimental import pallas as pl
from jax.experimental.pallas import tpu as pltpu
from jax.sharding import PartitionSpec as P


def shifted(array, axis, by):
    size = lax.axis_size(axis)
    pairs = [(i, i + by) for i in range(size) if 0 <= i + by < size]
    return lax.ppermute(array, axis, pairs)


def silu_slope(pre_value):
    sig = jax.nn.sigmoid(pre_value)
    return sig * (1.0 + pre_value * (1.0 - sig))


def gated_rows(gates, rows, tok_rows):
    scaled = (gates[:, :, None] * rows.astype(jnp.float32)[:, None, :]).astype(jnp.bfloat16)
    return scaled.reshape(tok_rows * 2, rows.shape[1])


def fill_buffer(scaled, target, experts, capacity):
    width = scaled.shape[1]
    buffer = jnp.zeros((experts * capacity, width), jnp.bfloat16).at[target].set(scaled)
    return buffer.reshape(experts, capacity, width)


def slot_plan(
    out_grad,
    expert_ids,
    gate_codes,
    up_weight,
    down_weight,
    pre_act,
    conv_grad,
    conv_input,
    conv_weight,
    in_proj,
):
    grad_rows = out_grad[0]
    route_ids = expert_ids[0]
    tok_rows = grad_rows.shape[0]
    experts = lax.axis_size("expert")
    capacity = pre_act.shape[2] // experts
    gates = gate_codes[0].astype(jnp.float32) / 256.0
    flat_ids = route_ids.reshape(tok_rows * 2)
    onehot = (flat_ids[:, None] == jnp.arange(experts, dtype=jnp.int32)[None, :]).astype(jnp.int32)
    before = jnp.cumsum(onehot, axis=0) - onehot
    position = jnp.sum(before * onehot, axis=1)
    target = flat_ids * capacity + position
    whole_rows = lax.all_gather(grad_rows, "mp", axis=1, tiled=True)
    buffer = fill_buffer(gated_rows(gates, whole_rows, tok_rows), target, experts, capacity)
    arrived = lax.all_to_all(buffer, "expert", split_axis=0, concat_axis=0, tiled=True)
    slot_rows = arrived.reshape(experts * capacity, whole_rows.shape[1])
    w_down = down_weight[0, 0]
    w_up = up_weight[0, 0]
    pre_slots = pre_act[0, 0].astype(jnp.float32)
    hidden = lax.dot_general(
        slot_rows, w_down, (((1,), (1,)), ((), ())), preferred_element_type=jnp.float32
    )
    pre_grad = (hidden * silu_slope(pre_slots)).astype(jnp.bfloat16)
    partial_value = lax.dot_general(
        pre_grad, w_up, (((1,), (1,)), ((), ())), preferred_element_type=jnp.float32
    )
    share = lax.psum_scatter(partial_value, "mp", scatter_dimension=1, tiled=True).astype(
        jnp.bfloat16
    )
    returned = lax.all_to_all(
        share.reshape(experts, capacity, share.shape[1]),
        "expert",
        split_axis=0,
        concat_axis=0,
        tiled=True,
    )
    picked = returned.reshape(experts * capacity, grad_rows.shape[1])[target]
    picked = picked.astype(jnp.float32).reshape(tok_rows, 2, grad_rows.shape[1])
    moe_total = grad_rows.astype(jnp.float32) + picked[:, 0, :] + picked[:, 1, :]
    grads_here = conv_grad[0]
    inputs_here = conv_input[0]
    taps = conv_weight[0]
    kernel_size = taps.shape[0]
    next_rows = shifted(grads_here[: kernel_size - 1], "expert", -1)
    prev_rows = shifted(inputs_here[tok_rows - kernel_size + 1 :], "expert", 1)
    grad_ext = jnp.concatenate([grads_here, next_rows], axis=0).astype(jnp.float32)
    input_ext = jnp.concatenate([prev_rows, inputs_here], axis=0).astype(jnp.float32)
    grad_local = grads_here.astype(jnp.float32)
    conv_result = jnp.zeros(grads_here.shape, jnp.float32)
    tap_terms = []
    for tap in range(kernel_size):
        start = kernel_size - 1 - tap
        conv_result = conv_result + taps[tap][None, :] * grad_ext[start : start + tok_rows]
        tap_terms.append(jnp.sum(grad_local * input_ext[tap : tap + tok_rows], axis=0))
    input_grad = conv_result.astype(jnp.bfloat16)
    tap_grads = lax.psum(jnp.stack(tap_terms), "expert")
    w_proj = in_proj[0]
    proj_partial = lax.dot_general(
        input_grad,
        lax.all_gather(w_proj, "expert", axis=0, tiled=True),
        (((1,), (1,)), ((), ())),
        preferred_element_type=jnp.float32,
    )
    proj_share = lax.psum_scatter(proj_partial, "mp", scatter_dimension=1, tiled=True)
    residual = (moe_total + proj_share).astype(jnp.bfloat16)
    sent_residual = shifted(residual, "section", -1)
    return (sent_residual[None], tap_grads[None])


F32, BF16 = jnp.float32, jnp.bfloat16
VMEM_LIMIT = 14 * 1024 * 1024
HEAD = 16
LANES = 128
RIGHT = [(0, 1), (1, 2), (2, 3)]
LEFT = [(3, 2), (2, 1), (1, 0)]
NT = (((1,), (1,)), ((), ()))
TN = (((0,), (0,)), ((), ()))


def whole(memory=pltpu.VMEM):
    return pl.BlockSpec(memory_space=memory)


def rotated(array, axis, by):
    size = lax.axis_size(axis)
    return lax.ppermute(array, axis, [(i, (i + by) % size) for i in range(size)])


def around(array):
    return [array] + [rotated(array, "expert", k) for k in range(1, lax.axis_size("expert"))]


def doubling_sum(array, axis):
    size, step = lax.axis_size(axis), 1
    while step < size:
        array = array + lax.ppermute(array, axis, [(i, i ^ step) for i in range(size)])
        step *= 2
    return array


def params():
    return pltpu.CompilerParams(vmem_limit_bytes=VMEM_LIMIT)


def cost(flops, bytes_accessed):
    return pl.CostEstimate(flops=8 * flops, bytes_accessed=8 * bytes_accessed, transcendentals=0)


def square(size):
    row = lax.broadcasted_iota(jnp.int32, (size, size), 0)
    return row, lax.broadcasted_iota(jnp.int32, (size, size), 1)


def routing(columns, me):
    values = columns.astype(F32)
    named = jnp.where(values[:, 0:2] == me.astype(F32), 1.0, 0.0)
    gate = jnp.sum(named * values[:, 2:4], axis=1, keepdims=True) / 256.0
    return jnp.sum(named, axis=1, keepdims=True), gate


def hidden_kernel(count, place, *refs):
    routes, rows = refs[:count], refs[count : 2 * count]
    down_own, down_other, send, keep, handed, gates, scaled = refs[2 * count :]
    tok_rows = rows[0].shape[0]
    units = down_own.shape[0]
    step = pl.program_id(0)

    @pl.when(step == 0)
    def _():
        for k in range(count):
            at = pl.ds(k * tok_rows, tok_rows)
            gates[at, :] = routing(routes[k][...], place[1])[1]
            handed[at, :] = routes[k][...]
        keep[...] = jnp.zeros_like(keep)

    for k in range(count):
        at = pl.ds(k * tok_rows, tok_rows)
        scaled[at, :] = (gates[at, :] * rows[k][...].astype(F32)).astype(BF16)
    keep[:, :units] += lax.dot_general(scaled[...], down_own[...], NT, preferred_element_type=F32)
    keep[:, units:] += lax.dot_general(scaled[...], down_other[...], NT, preferred_element_type=F32)

    @pl.when(step == pl.num_programs(0) - 1)
    def _():
        send[...] = keep[...].astype(BF16)


def route_columns(rows):
    tok_rows, width = rows.shape
    return pl.BlockSpec((tok_rows, LANES), lambda i, place: (0, width // LANES - 1))


def hidden_sums(place, rows, down, down_other):
    count = len(rows)
    tok_rows = rows[0].shape[0]
    units, half_width = down_other.shape
    tokens = count * tok_rows
    chunk = half_width // 4
    return pl.pallas_call(
        functools.partial(hidden_kernel, count),
        grid_spec=pltpu.PrefetchScalarGridSpec(
            num_scalar_prefetch=1,
            grid=(4,),
            in_specs=[route_columns(rows[0])] * count
            + [pl.BlockSpec((tok_rows, chunk), lambda i, place: (0, i))] * count
            + [
                pl.BlockSpec((units, chunk), lambda i, place: (0, 4 * place[0] + i)),
                pl.BlockSpec((units, chunk), lambda i, place: (0, i)),
            ],
            out_specs=[pl.BlockSpec((tokens, 2 * units), lambda i, place: (0, 0))] * 2
            + [pl.BlockSpec((tokens, LANES), lambda i, place: (0, 0))],
            scratch_shapes=[pltpu.VMEM((tokens, 1), F32), pltpu.VMEM((tokens, chunk), BF16)],
        ),
        out_shape=[jax.ShapeDtypeStruct((tokens, 2 * units), dtype) for dtype in (BF16, F32)]
        + [jax.ShapeDtypeStruct((tokens, LANES), BF16)],
        compiler_params=params(),
        cost_estimate=cost(4 * tokens * half_width * units, 4 * units * half_width + 2 * tokens * half_width),
        name="hidden",
    )(place, *rows, *rows, down, down_other)


def finish_kernel(count, place, routes, keep, got, pre_own, pre_other, up_own, up_other, out, pre_grad):
    tok_rows = pre_grad.shape[0] // count
    units = pre_own.shape[1]

    @pl.when(pl.program_id(0) == 0)
    def _():
        row, column = square(tok_rows)
        for k in range(count):
            at = pl.ds(k * tok_rows, tok_rows)
            named, _ = routing(routes[at, :], place[1])
            rank = jnp.sum(jnp.where(row < column, named, 0.0), axis=0, keepdims=True).astype(jnp.int32)
            named = jnp.sum(jnp.where(row == column, named, 0.0), axis=0, keepdims=True)
            pick = jnp.where(rank == row, named, 0.0).astype(BF16)
            slots = pl.ds(pl.multiple_of(place[2 + k] * tok_rows, tok_rows), tok_rows)
            for side, pre in enumerate((pre_own, pre_other)):
                here = pl.ds(side * units, units)
                p = lax.dot_general(pick, pre[slots, :], TN, preferred_element_type=F32)
                q = 1.0 / (1.0 + jnp.exp(-p))
                hidden = keep[at, here] + got[at, pl.ds((1 - side) * units, units)].astype(F32)
                pre_grad[at, here] = (hidden * (q * (1.0 + p * (1.0 - q)))).astype(BF16)

    value = lax.dot_general(pre_grad[:, :units], up_own[...], NT, preferred_element_type=F32)
    value += lax.dot_general(pre_grad[:, units:], up_other[...], NT, preferred_element_type=F32)
    out[...] = value.astype(out.dtype)


def expert_sums(place, routes, keep, got, pre, pre_other, up, up_other, dtype):
    tokens = keep.shape[0]
    count = place.shape[0] - 2
    units = pre.shape[1]
    half_width = up_other.shape[0]
    chunk = half_width // 4
    return pl.pallas_call(
        functools.partial(finish_kernel, count),
        grid_spec=pltpu.PrefetchScalarGridSpec(
            num_scalar_prefetch=1,
            grid=(4,),
            in_specs=[whole()] * 5
            + [
                pl.BlockSpec((chunk, units), lambda i, place: (4 * place[0] + i, 0)),
                pl.BlockSpec((chunk, units), lambda i, place: (i, 0)),
            ],
            out_specs=pl.BlockSpec((tokens, chunk), lambda i, place: (0, i)),
            scratch_shapes=[pltpu.VMEM((tokens, 2 * units), BF16)],
        ),
        out_shape=jax.ShapeDtypeStruct((tokens, half_width), dtype),
        compiler_params=params(),
        cost_estimate=cost(4 * tokens * half_width * units, 4 * units * half_width + 4 * tokens * half_width),
        name="experts",
    )(place, routes, keep, got, pre, pre_other, up, up_other)


def proj_kernel(count, with_taps, place, *refs):
    grads, heads = refs[:count], refs[count : 2 * count]
    taps, weight = refs[2 * count : 2 * count + 2]
    refs = refs[2 * count + 2 :]
    if with_taps:
        inputs, send, keep, tap_out, ext, scaled = refs
    else:
        send, keep, ext, scaled = refs
    tok_rows, chunk = grads[0].shape
    kernel_size = taps.shape[0]
    step = pl.program_id(0)

    tap = taps[...]
    for k in range(count):
        ext[:tok_rows, :] = grads[k][...].astype(F32)
        follows = (place[2 + k] < lax.axis_size("expert") - 1).astype(F32)
        ext[tok_rows:, :] = heads[k][...].astype(F32) * follows
        result = jnp.zeros((tok_rows, chunk), F32)
        for j in range(kernel_size):
            start = kernel_size - 1 - j
            result = result + tap[j : j + 1, :] * ext[start : start + tok_rows, :]
        scaled[k * tok_rows : (k + 1) * tok_rows, :] = result.astype(BF16)
        if with_taps and k == 0:
            values = inputs[...].astype(F32)
            for j in range(kernel_size):
                start = kernel_size - 1 - j
                terms = values * ext[start : start + tok_rows, :]
                tap_out[j : j + 1, :] = jnp.sum(terms, axis=0, keepdims=True)

    product = lax.dot_general(scaled[...], weight[...], NT, preferred_element_type=F32)

    @pl.when(step == 0)
    def _():
        keep[...] = product

    @pl.when(step > 0)
    def _():
        keep[...] += product

    @pl.when(step == pl.num_programs(0) - 1)
    def _():
        send[...] = keep[...].astype(BF16)


def proj_sums(place, grads, heads, taps, weight, inputs=None):
    count = len(grads)
    tok_rows, half_width = grads[0].shape
    block = weight.shape[0]
    tokens = count * tok_rows
    chunk = half_width // 4
    with_taps = inputs is not None

    def wide(rows):
        return pl.BlockSpec((rows, chunk), lambda i: (0, i))

    last = [wide(tok_rows)] if with_taps else []
    out_specs = [pl.BlockSpec((tokens, block), lambda i: (0, 0))] * 2
    out_shape = [jax.ShapeDtypeStruct((tokens, block), BF16), jax.ShapeDtypeStruct((tokens, block), F32)]
    if with_taps:
        out_specs = out_specs + [wide(taps.shape[0])]
        out_shape = out_shape + [jax.ShapeDtypeStruct(taps.shape, F32)]
    return pl.pallas_call(
        functools.partial(proj_kernel, count, with_taps),
        grid=(half_width // chunk,),
        in_specs=[whole(pltpu.SMEM)]
        + [wide(tok_rows)] * count
        + [wide(HEAD)] * count
        + [wide(taps.shape[0]), wide(block)]
        + last,
        out_specs=out_specs,
        out_shape=out_shape,
        scratch_shapes=[pltpu.VMEM((tok_rows + HEAD, chunk), F32), pltpu.VMEM((tokens, chunk), BF16)],
        compiler_params=params(),
        cost_estimate=cost(
            2 * tokens * half_width * block, 2 * (block + tokens) * half_width + 6 * tokens * block
        ),
        name="projection",
    )(place, *grads, *heads, taps, weight, *([inputs] if with_taps else []))


def combine_kernel(place, grad, sums, back_right, back_left, proj_keep, proj_got, to_right, to_left, own, total):
    half, me = place[0], place[1]
    rows, part = grad.shape[0], proj_keep.shape[1]
    total[0:rows, :] = grad[...].astype(F32) + sums[0:rows, :]
    total[rows : 2 * rows, :] = sums[rows : 2 * rows, :] + back_left[...].astype(F32)
    total[2 * rows :, :] = sums[2 * rows :, :] + back_right[...].astype(F32)

    @pl.when(me // 2 == half)
    def _():
        at = pl.ds(pl.multiple_of(lax.rem(me, 2) * part, part), part)
        total[:, at] += proj_keep[...] + proj_got[...].astype(F32)

    own[...] = total[0:rows, :]
    to_left[...] = total[rows : 2 * rows, :].astype(BF16)
    to_right[...] = total[2 * rows :, :].astype(BF16)


def combined(place, grad, sums, *arrays):
    outs = [jax.ShapeDtypeStruct(grad.shape, dtype) for dtype in (BF16, BF16, F32)]
    return pl.pallas_call(
        combine_kernel,
        in_specs=[whole(pltpu.SMEM)] + [whole()] * (2 + len(arrays)),
        out_specs=[whole()] * 3,
        out_shape=outs,
        scratch_shapes=[pltpu.VMEM(sums.shape, F32)],
        compiler_params=params(),
        cost_estimate=cost(8 * grad.size, 40 * grad.size),
        name="combine",
    )(place, grad, sums, *arrays)


def final_kernel(place, residual, far, end, out, total):
    half, me = place[0], place[1]
    experts = lax.axis_size("expert")
    part = far.shape[1]
    total[...] = residual[...].astype(F32)

    def add(source, value):
        @pl.when((source < experts) & (source // 2 == half))
        def _():
            at = pl.ds(pl.multiple_of(lax.rem(source, 2) * part, part), part)
            total[:, at] += value[...].astype(F32)

    add(lax.rem(me + 2, experts), far)
    add(jnp.where(lax.rem(me, experts - 1) == 0, experts - 1 - me, experts), end)
    out[...] = total[...].astype(BF16)


def final_sum(place, residual, far, end):
    return pl.pallas_call(
        final_kernel,
        in_specs=[whole(pltpu.SMEM)] + [whole()] * 3,
        out_specs=whole(),
        out_shape=jax.ShapeDtypeStruct(residual.shape, BF16),
        scratch_shapes=[pltpu.VMEM(residual.shape, F32)],
        compiler_params=params(),
        cost_estimate=cost(4 * residual.size, 8 * residual.size),
        name="residual",
    )(place, residual, far, end)


def moved(array, pairs):
    return lax.ppermute(array, "expert", pairs)


def swapped(array):
    return rotated(array, "mp", 1)


def together(*arrays):
    return lax.optimization_barrier(arrays)


def token_plan(
    out_grad,
    expert_ids,
    gate_codes,
    up_weight,
    down_weight,
    pre_act,
    conv_grad,
    conv_input,
    conv_weight,
    in_proj,
):
    me, half = lax.axis_index("expert"), lax.axis_index("mp")
    experts = lax.axis_size("expert")

    def place(*blocks):
        return jnp.stack([half, me, *blocks]).astype(jnp.int32)

    far_block, end_block = (me + 2) % experts, jnp.where(me == 0, experts - 1, 0)
    near = place(me, jnp.maximum(me - 1, 0), jnp.minimum(me + 1, experts - 1))
    rows_own, conv_own = out_grad[0], conv_grad[0]
    tok_rows, half_width = rows_own.shape
    w_down, w_up, pre = down_weight[0, 0], up_weight[0, 0], pre_act[0, 0]
    taps, w_proj = conv_weight[0], in_proj[0]

    routes = jnp.concatenate([expert_ids[0], gate_codes[0]], axis=1).astype(BF16)
    rows_own = jnp.concatenate([rows_own, jnp.pad(routes, ((0, 0), (0, LANES - routes.shape[1])))], axis=1)
    rows_left, rows_right = moved(rows_own, RIGHT), moved(rows_own, LEFT)
    down_send = lax.dynamic_slice_in_dim(w_down, (1 - half) * half_width, half_width, 1)
    up_send = lax.dynamic_slice_in_dim(w_up, (1 - half) * half_width, half_width, 0)
    rows_left, rows_right, down_send, up_send, pre_send, head = together(
        rows_left, rows_right, down_send, up_send, pre, conv_own[:HEAD]
    )

    from_left, from_right = moved(rows_left, RIGHT[1:]), moved(rows_right, LEFT[1:])
    down_other, pre_other = swapped(down_send), swapped(pre_send)
    from_left, from_right, down_other, pre_other, up_send, head = together(
        from_left, from_right, down_other, pre_other, up_send, head
    )

    def hidden(where, rows):
        send, keep, routes = hidden_sums(where, rows, w_down, down_other)
        return routes, keep, swapped(send)

    def finish(where, sums, dtype):
        return expert_sums(where, *sums, pre, pre_other, w_up, up_other, dtype)

    far, end = place(far_block), place(end_block)
    rows_far = jnp.where(me >= 2, from_left, from_right)
    rows_end = moved(rows_far, [(2, 3), (1, 0)])
    up_other = swapped(up_send)
    routes, keep, got = hidden(near, [rows_own, rows_left, rows_right])
    next_head = moved(head, LEFT[:2])
    rows_end, rows_far, keep, up_other, conv_own, next_head = together(
        rows_end, rows_far, keep, up_other, conv_own, next_head
    )

    conv_left, conv_right = moved(conv_own, RIGHT), moved(conv_own, LEFT)
    end_hidden = hidden(end, [rows_end])
    far_routes, far_keep, far_got = hidden(far, [rows_far])
    end_sums = finish(end, end_hidden, BF16)
    next_head = moved(next_head, LEFT[1:])
    conv_left, conv_right, end_sums, keep, far_keep, next_head = together(
        conv_left, conv_right, end_sums, keep, far_keep, next_head
    )

    from_left, from_right = moved(conv_left, RIGHT[1:]), moved(conv_right, LEFT[1:])
    back_end = moved(end_sums, [(0, 1), (3, 2)])
    gather = [(e * 2 + 1 - e // 2, e * 2 + e // 2) for e in range(experts)]

    def proj(where, grads, heads, *inputs):
        send, keep, *tap_terms = proj_sums(where, grads, heads, taps, w_proj, *inputs)
        return keep, lax.ppermute(send, ("expert", "mp"), gather), *tap_terms

    near_proj, near_proj_got, tap_terms = proj(
        near, [conv_own, conv_left, conv_right], [conv_right, conv_own, next_head], conv_input[0]
    )
    far_sums = finish(far, (far_routes, far_keep, far_got), F32)
    from_left, from_right, near_proj, conv_left, keep, far_sums = together(
        from_left, from_right, near_proj, conv_left, keep, far_sums
    )

    conv_far = jnp.where(me >= 2, from_left, from_right)
    conv_far, back_end = together(conv_far, back_end)
    conv_end = moved(conv_far, [(2, 3), (1, 0)])
    back = (far_sums + back_end.astype(F32)).astype(BF16)
    back_right, back_left = moved(back, RIGHT[:2]), moved(back, LEFT[:2])
    near_sums = finish(near, (routes, keep, got), F32)
    conv_end, back_right, back_left, near_sums = together(conv_end, back_right, back_left, near_sums)

    to_right, to_left, own = combined(near, out_grad[0], near_sums, back_right, back_left, near_proj, near_proj_got)
    to_right, to_left, conv_end = together(to_right, to_left, conv_end)
    to_right, to_left = moved(to_right, RIGHT), moved(to_left, LEFT)
    far_head = jnp.where(me >= 2, conv_left[:HEAD], conv_end[:HEAD])
    proj_keep, proj_got = proj(place(far_block, end_block), [conv_far, conv_end], [far_head, conv_far])
    to_right, to_left, proj_keep = together(to_right, to_left, proj_keep)

    residual = (own + to_right.astype(F32) + to_left.astype(F32)).astype(BF16)
    sections, cores = lax.axis_size("section"), lax.axis_size("mp")

    def deliver(keep, got, pairs):
        def at(s, e, m):
            return (s * experts + e) * cores + m

        moves = [(at(s, e, e // 2), at(s - 1, d, e // 2)) for s in range(1, sections) for e, d in pairs]
        return lax.ppermute((keep + got.astype(F32)).astype(BF16), ("section", "expert", "mp"), moves)

    residual = shifted(residual, "section", -1)
    far_piece = deliver(proj_keep[:tok_rows], proj_got[:tok_rows], [(e, (e + 2) % experts) for e in range(experts)])
    end_piece = deliver(proj_keep[tok_rows:], proj_got[tok_rows:], [(0, experts - 1), (experts - 1, 0)])
    tap_grads = doubling_sum(tap_terms, "expert")
    residual = final_sum(near, residual, far_piece, end_piece)
    return (residual[None], tap_grads[None])


def shards(*arrays):
    experts, halves = lax.axis_size("expert"), lax.axis_size("mp")
    capacity = arrays[5].shape[2] // experts
    dense = capacity == arrays[0].shape[1] and experts == 4 and halves == 2
    return (token_plan if dense else slot_plan)(*arrays)


def solution(mesh):
    in_specs = (
        P("section", "expert", "mp"),
        P("section", "expert", None),
        P("section", "expert", None),
        P("section", "expert", None, "mp"),
        P("section", "expert", "mp", None),
        P("section", "expert", None, "mp"),
        P("section", "expert", "mp"),
        P("section", "expert", "mp"),
        P("section", None, "mp"),
        P("section", "expert", "mp"),
    )
    out_specs = (P("section", "expert", "mp"), P("section", None, "mp"))
    return jax.shard_map(shards, mesh=mesh, in_specs=in_specs, out_specs=out_specs, check_vma=False)
```

```python
import functools

import jax
import jax.numpy as jnp
from jax import lax
from jax.experimental import pallas as pl
from jax.experimental.pallas import tpu as pltpu
from jax.sharding import PartitionSpec as P


def shifted(array, axis, by):
    size = lax.axis_size(axis)
    pairs = [(i, i + by) for i in range(size) if 0 <= i + by < size]
    return lax.ppermute(array, axis, pairs)


def silu_slope(pre_value):
    sig = jax.nn.sigmoid(pre_value)
    return sig * (1.0 + pre_value * (1.0 - sig))


def gated_rows(gates, rows, tok_rows):
    scaled = (gates[:, :, None] * rows.astype(jnp.float32)[:, None, :]).astype(jnp.bfloat16)
    return scaled.reshape(tok_rows * 2, rows.shape[1])


def fill_buffer(scaled, target, experts, capacity):
    width = scaled.shape[1]
    buffer = jnp.zeros((experts * capacity, width), jnp.bfloat16).at[target].set(scaled)
    return buffer.reshape(experts, capacity, width)


def slot_plan(
    out_grad,
    expert_ids,
    gate_codes,
    up_weight,
    down_weight,
    pre_act,
    conv_grad,
    conv_input,
    conv_weight,
    in_proj,
):
    grad_rows = out_grad[0]
    route_ids = expert_ids[0]
    tok_rows = grad_rows.shape[0]
    experts = lax.axis_size("expert")
    capacity = pre_act.shape[2] // experts
    gates = gate_codes[0].astype(jnp.float32) / 256.0
    flat_ids = route_ids.reshape(tok_rows * 2)
    onehot = (flat_ids[:, None] == jnp.arange(experts, dtype=jnp.int32)[None, :]).astype(jnp.int32)
    before = jnp.cumsum(onehot, axis=0) - onehot
    position = jnp.sum(before * onehot, axis=1)
    target = flat_ids * capacity + position
    whole_rows = lax.all_gather(grad_rows, "mp", axis=1, tiled=True)
    buffer = fill_buffer(gated_rows(gates, whole_rows, tok_rows), target, experts, capacity)
    arrived = lax.all_to_all(buffer, "expert", split_axis=0, concat_axis=0, tiled=True)
    slot_rows = arrived.reshape(experts * capacity, whole_rows.shape[1])
    w_down = down_weight[0, 0]
    w_up = up_weight[0, 0]
    pre_slots = pre_act[0, 0].astype(jnp.float32)
    hidden = lax.dot_general(
        slot_rows, w_down, (((1,), (1,)), ((), ())), preferred_element_type=jnp.float32
    )
    pre_grad = (hidden * silu_slope(pre_slots)).astype(jnp.bfloat16)
    partial_value = lax.dot_general(
        pre_grad, w_up, (((1,), (1,)), ((), ())), preferred_element_type=jnp.float32
    )
    share = lax.psum_scatter(partial_value, "mp", scatter_dimension=1, tiled=True).astype(
        jnp.bfloat16
    )
    returned = lax.all_to_all(
        share.reshape(experts, capacity, share.shape[1]),
        "expert",
        split_axis=0,
        concat_axis=0,
        tiled=True,
    )
    picked = returned.reshape(experts * capacity, grad_rows.shape[1])[target]
    picked = picked.astype(jnp.float32).reshape(tok_rows, 2, grad_rows.shape[1])
    moe_total = grad_rows.astype(jnp.float32) + picked[:, 0, :] + picked[:, 1, :]
    grads_here = conv_grad[0]
    inputs_here = conv_input[0]
    taps = conv_weight[0]
    kernel_size = taps.shape[0]
    next_rows = shifted(grads_here[: kernel_size - 1], "expert", -1)
    prev_rows = shifted(inputs_here[tok_rows - kernel_size + 1 :], "expert", 1)
    grad_ext = jnp.concatenate([grads_here, next_rows], axis=0).astype(jnp.float32)
    input_ext = jnp.concatenate([prev_rows, inputs_here], axis=0).astype(jnp.float32)
    grad_local = grads_here.astype(jnp.float32)
    conv_result = jnp.zeros(grads_here.shape, jnp.float32)
    tap_terms = []
    for tap in range(kernel_size):
        start = kernel_size - 1 - tap
        conv_result = conv_result + taps[tap][None, :] * grad_ext[start : start + tok_rows]
        tap_terms.append(jnp.sum(grad_local * input_ext[tap : tap + tok_rows], axis=0))
    input_grad = conv_result.astype(jnp.bfloat16)
    tap_grads = lax.psum(jnp.stack(tap_terms), "expert")
    w_proj = in_proj[0]
    proj_partial = lax.dot_general(
        input_grad,
        lax.all_gather(w_proj, "expert", axis=0, tiled=True),
        (((1,), (1,)), ((), ())),
        preferred_element_type=jnp.float32,
    )
    proj_share = lax.psum_scatter(proj_partial, "mp", scatter_dimension=1, tiled=True)
    residual = (moe_total + proj_share).astype(jnp.bfloat16)
    sent_residual = shifted(residual, "section", -1)
    return (sent_residual[None], tap_grads[None])


F32, BF16 = jnp.float32, jnp.bfloat16
VMEM_LIMIT = 14 * 1024 * 1024
HEAD = 16
LANES = 128
RIGHT = [(0, 1), (1, 2), (2, 3)]
LEFT = [(3, 2), (2, 1), (1, 0)]
NT = (((1,), (1,)), ((), ()))
TN = (((0,), (0,)), ((), ()))


def whole(memory=pltpu.VMEM):
    return pl.BlockSpec(memory_space=memory)


def rotated(array, axis, by):
    size = lax.axis_size(axis)
    return lax.ppermute(array, axis, [(i, (i + by) % size) for i in range(size)])


def around(array):
    return [array] + [rotated(array, "expert", k) for k in range(1, lax.axis_size("expert"))]


def doubling_sum(array, axis):
    size, step = lax.axis_size(axis), 1
    while step < size:
        array = array + lax.ppermute(array, axis, [(i, i ^ step) for i in range(size)])
        step *= 2
    return array


def params():
    return pltpu.CompilerParams(vmem_limit_bytes=VMEM_LIMIT)


def cost(flops, bytes_accessed):
    return pl.CostEstimate(flops=8 * flops, bytes_accessed=8 * bytes_accessed, transcendentals=0)


def square(size):
    row = lax.broadcasted_iota(jnp.int32, (size, size), 0)
    return row, lax.broadcasted_iota(jnp.int32, (size, size), 1)


def routing(columns, me):
    values = columns.astype(F32)
    named = jnp.where(values[:, 0:2] == me.astype(F32), 1.0, 0.0)
    gate = jnp.sum(named * values[:, 2:4], axis=1, keepdims=True) / 256.0
    return jnp.sum(named, axis=1, keepdims=True), gate


def hidden_kernel(count, place, *refs):
    routes, rows = refs[:count], refs[count : 2 * count]
    down_own, down_other, send, keep, handed, gates, scaled = refs[2 * count :]
    tok_rows = rows[0].shape[0]
    units = down_own.shape[0]
    step = pl.program_id(0)

    @pl.when(step == 0)
    def _():
        for k in range(count):
            at = pl.ds(k * tok_rows, tok_rows)
            gates[at, :] = routing(routes[k][...], place[1])[1]
            handed[at, :] = routes[k][...]
        keep[...] = jnp.zeros_like(keep)

    for k in range(count):
        at = pl.ds(k * tok_rows, tok_rows)
        scaled[at, :] = (gates[at, :] * rows[k][...].astype(F32)).astype(BF16)
    keep[:, :units] += lax.dot_general(scaled[...], down_own[...], NT, preferred_element_type=F32)
    keep[:, units:] += lax.dot_general(scaled[...], down_other[...], NT, preferred_element_type=F32)

    @pl.when(step == pl.num_programs(0) - 1)
    def _():
        send[...] = keep[...].astype(BF16)


def route_columns(rows):
    tok_rows, width = rows.shape
    return pl.BlockSpec((tok_rows, LANES), lambda i, place: (0, width // LANES - 1))


def hidden_sums(place, rows, down, down_other):
    count = len(rows)
    tok_rows = rows[0].shape[0]
    units, half_width = down_other.shape
    tokens = count * tok_rows
    chunk = half_width // 4
    return pl.pallas_call(
        functools.partial(hidden_kernel, count),
        grid_spec=pltpu.PrefetchScalarGridSpec(
            num_scalar_prefetch=1,
            grid=(4,),
            in_specs=[route_columns(rows[0])] * count
            + [pl.BlockSpec((tok_rows, chunk), lambda i, place: (0, i))] * count
            + [
                pl.BlockSpec((units, chunk), lambda i, place: (0, 4 * place[0] + i)),
                pl.BlockSpec((units, chunk), lambda i, place: (0, i)),
            ],
            out_specs=[pl.BlockSpec((tokens, 2 * units), lambda i, place: (0, 0))] * 2
            + [pl.BlockSpec((tokens, LANES), lambda i, place: (0, 0))],
            scratch_shapes=[pltpu.VMEM((tokens, 1), F32), pltpu.VMEM((tokens, chunk), BF16)],
        ),
        out_shape=[jax.ShapeDtypeStruct((tokens, 2 * units), dtype) for dtype in (BF16, F32)]
        + [jax.ShapeDtypeStruct((tokens, LANES), BF16)],
        compiler_params=params(),
        cost_estimate=cost(4 * tokens * half_width * units, 4 * units * half_width + 2 * tokens * half_width),
        name="hidden",
    )(place, *rows, *rows, down, down_other)


def finish_kernel(count, place, routes, keep, got, pre_own, pre_other, up_own, up_other, out, pre_grad):
    tok_rows = pre_grad.shape[0] // count
    units = pre_own.shape[1]

    @pl.when(pl.program_id(0) == 0)
    def _():
        row, column = square(tok_rows)
        for k in range(count):
            at = pl.ds(k * tok_rows, tok_rows)
            named, _ = routing(routes[at, :], place[1])
            rank = jnp.sum(jnp.where(row < column, named, 0.0), axis=0, keepdims=True).astype(jnp.int32)
            named = jnp.sum(jnp.where(row == column, named, 0.0), axis=0, keepdims=True)
            pick = jnp.where(rank == row, named, 0.0).astype(BF16)
            slots = pl.ds(pl.multiple_of(place[2 + k] * tok_rows, tok_rows), tok_rows)
            for side, pre in enumerate((pre_own, pre_other)):
                here = pl.ds(side * units, units)
                p = lax.dot_general(pick, pre[slots, :], TN, preferred_element_type=F32)
                q = 1.0 / (1.0 + jnp.exp(-p))
                hidden = keep[at, here] + got[at, pl.ds((1 - side) * units, units)].astype(F32)
                pre_grad[at, here] = (hidden * (q * (1.0 + p * (1.0 - q)))).astype(BF16)

    value = lax.dot_general(pre_grad[:, :units], up_own[...], NT, preferred_element_type=F32)
    value += lax.dot_general(pre_grad[:, units:], up_other[...], NT, preferred_element_type=F32)
    out[...] = value.astype(out.dtype)


def expert_sums(place, routes, keep, got, pre, pre_other, up, up_other, dtype):
    tokens = keep.shape[0]
    count = place.shape[0] - 2
    units = pre.shape[1]
    half_width = up_other.shape[0]
    chunk = half_width // 4
    return pl.pallas_call(
        functools.partial(finish_kernel, count),
        grid_spec=pltpu.PrefetchScalarGridSpec(
            num_scalar_prefetch=1,
            grid=(4,),
            in_specs=[whole()] * 5
            + [
                pl.BlockSpec((chunk, units), lambda i, place: (4 * place[0] + i, 0)),
                pl.BlockSpec((chunk, units), lambda i, place: (i, 0)),
            ],
            out_specs=pl.BlockSpec((tokens, chunk), lambda i, place: (0, i)),
            scratch_shapes=[pltpu.VMEM((tokens, 2 * units), BF16)],
        ),
        out_shape=jax.ShapeDtypeStruct((tokens, half_width), dtype),
        compiler_params=params(),
        cost_estimate=cost(4 * tokens * half_width * units, 4 * units * half_width + 4 * tokens * half_width),
        name="experts",
    )(place, routes, keep, got, pre, pre_other, up, up_other)


def proj_kernel(count, with_taps, place, *refs):
    grads, heads = refs[:count], refs[count : 2 * count]
    taps, weight = refs[2 * count : 2 * count + 2]
    refs = refs[2 * count + 2 :]
    if with_taps:
        inputs, send, keep, tap_out, ext, scaled = refs
    else:
        send, keep, ext, scaled = refs
    tok_rows, chunk = grads[0].shape
    kernel_size = taps.shape[0]
    step = pl.program_id(0)

    tap = taps[...]
    for k in range(count):
        ext[:tok_rows, :] = grads[k][...].astype(F32)
        follows = (place[2 + k] < lax.axis_size("expert") - 1).astype(F32)
        ext[tok_rows:, :] = heads[k][...].astype(F32) * follows
        result = jnp.zeros((tok_rows, chunk), F32)
        for j in range(kernel_size):
            start = kernel_size - 1 - j
            result = result + tap[j : j + 1, :] * ext[start : start + tok_rows, :]
        scaled[k * tok_rows : (k + 1) * tok_rows, :] = result.astype(BF16)
        if with_taps and k == 0:
            values = inputs[...].astype(F32)
            for j in range(kernel_size):
                start = kernel_size - 1 - j
                terms = values * ext[start : start + tok_rows, :]
                tap_out[j : j + 1, :] = jnp.sum(terms, axis=0, keepdims=True)

    product = lax.dot_general(scaled[...], weight[...], NT, preferred_element_type=F32)

    @pl.when(step == 0)
    def _():
        keep[...] = product

    @pl.when(step > 0)
    def _():
        keep[...] += product

    @pl.when(step == pl.num_programs(0) - 1)
    def _():
        send[...] = keep[...].astype(BF16)


def proj_sums(place, grads, heads, taps, weight, inputs=None):
    count = len(grads)
    tok_rows, half_width = grads[0].shape
    block = weight.shape[0]
    tokens = count * tok_rows
    chunk = half_width // 4
    with_taps = inputs is not None

    def wide(rows):
        return pl.BlockSpec((rows, chunk), lambda i: (0, i))

    last = [wide(tok_rows)] if with_taps else []
    out_specs = [pl.BlockSpec((tokens, block), lambda i: (0, 0))] * 2
    out_shape = [jax.ShapeDtypeStruct((tokens, block), BF16), jax.ShapeDtypeStruct((tokens, block), F32)]
    if with_taps:
        out_specs = out_specs + [wide(taps.shape[0])]
        out_shape = out_shape + [jax.ShapeDtypeStruct(taps.shape, F32)]
    return pl.pallas_call(
        functools.partial(proj_kernel, count, with_taps),
        grid=(half_width // chunk,),
        in_specs=[whole(pltpu.SMEM)]
        + [wide(tok_rows)] * count
        + [wide(HEAD)] * count
        + [wide(taps.shape[0]), wide(block)]
        + last,
        out_specs=out_specs,
        out_shape=out_shape,
        scratch_shapes=[pltpu.VMEM((tok_rows + HEAD, chunk), F32), pltpu.VMEM((tokens, chunk), BF16)],
        compiler_params=params(),
        cost_estimate=cost(
            2 * tokens * half_width * block, 2 * (block + tokens) * half_width + 6 * tokens * block
        ),
        name="projection",
    )(place, *grads, *heads, taps, weight, *([inputs] if with_taps else []))


def combine_kernel(place, grad, sums, back_right, back_left, proj_keep, proj_got, to_right, to_left, own, total):
    half, me = place[0], place[1]
    rows, part = grad.shape[0], proj_keep.shape[1]
    total[0:rows, :] = grad[...].astype(F32) + sums[0:rows, :]
    total[rows : 2 * rows, :] = sums[rows : 2 * rows, :] + back_left[...].astype(F32)
    total[2 * rows :, :] = sums[2 * rows :, :] + back_right[...].astype(F32)

    @pl.when(me // 2 == half)
    def _():
        at = pl.ds(pl.multiple_of(lax.rem(me, 2) * part, part), part)
        total[:, at] += proj_keep[...] + proj_got[...].astype(F32)

    own[...] = total[0:rows, :]
    to_left[...] = total[rows : 2 * rows, :].astype(BF16)
    to_right[...] = total[2 * rows :, :].astype(BF16)


def combined(place, grad, sums, *arrays):
    outs = [jax.ShapeDtypeStruct(grad.shape, dtype) for dtype in (BF16, BF16, F32)]
    return pl.pallas_call(
        combine_kernel,
        in_specs=[whole(pltpu.SMEM)] + [whole()] * (2 + len(arrays)),
        out_specs=[whole()] * 3,
        out_shape=outs,
        scratch_shapes=[pltpu.VMEM(sums.shape, F32)],
        compiler_params=params(),
        cost_estimate=cost(8 * grad.size, 40 * grad.size),
        name="combine",
    )(place, grad, sums, *arrays)


def final_kernel(place, residual, far, end, out, total):
    half, me = place[0], place[1]
    experts = lax.axis_size("expert")
    part = far.shape[1]
    total[...] = residual[...].astype(F32)

    def add(source, value):
        @pl.when((source < experts) & (source // 2 == half))
        def _():
            at = pl.ds(pl.multiple_of(lax.rem(source, 2) * part, part), part)
            total[:, at] += value[...].astype(F32)

    add(lax.rem(me + 2, experts), far)
    add(jnp.where(lax.rem(me, experts - 1) == 0, experts - 1 - me, experts), end)
    out[...] = total[...].astype(BF16)


def final_sum(place, residual, far, end):
    return pl.pallas_call(
        final_kernel,
        in_specs=[whole(pltpu.SMEM)] + [whole()] * 3,
        out_specs=whole(),
        out_shape=jax.ShapeDtypeStruct(residual.shape, BF16),
        scratch_shapes=[pltpu.VMEM(residual.shape, F32)],
        compiler_params=params(),
        cost_estimate=cost(4 * residual.size, 8 * residual.size),
        name="residual",
    )(place, residual, far, end)


def moved(array, pairs):
    return lax.ppermute(array, "expert", pairs)


def swapped(array):
    return rotated(array, "mp", 1)


def together(*arrays):
    return lax.optimization_barrier(arrays)


def token_plan(
    out_grad,
    expert_ids,
    gate_codes,
    up_weight,
    down_weight,
    pre_act,
    conv_grad,
    conv_input,
    conv_weight,
    in_proj,
):
    me, half = lax.axis_index("expert"), lax.axis_index("mp")
    experts = lax.axis_size("expert")

    def place(*blocks):
        return jnp.stack([half, me, *blocks]).astype(jnp.int32)

    far_block, end_block = (me + 2) % experts, jnp.where(me == 0, experts - 1, 0)
    near = place(me, jnp.maximum(me - 1, 0), jnp.minimum(me + 1, experts - 1))
    rows_own, conv_own = out_grad[0], conv_grad[0]
    tok_rows, half_width = rows_own.shape
    w_down, w_up, pre = down_weight[0, 0], up_weight[0, 0], pre_act[0, 0]
    taps, w_proj = conv_weight[0], in_proj[0]

    routes = jnp.concatenate([expert_ids[0], gate_codes[0]], axis=1).astype(BF16)
    rows_own = jnp.concatenate([rows_own, jnp.pad(routes, ((0, 0), (0, LANES - routes.shape[1])))], axis=1)
    rows_left, rows_right = moved(rows_own, RIGHT), moved(rows_own, LEFT)
    down_send = lax.dynamic_slice_in_dim(w_down, (1 - half) * half_width, half_width, 1)
    up_send = lax.dynamic_slice_in_dim(w_up, (1 - half) * half_width, half_width, 0)
    rows_left, rows_right, down_send, up_send, pre_send, head = together(
        rows_left, rows_right, down_send, up_send, pre, conv_own[:HEAD]
    )

    from_left, from_right = moved(rows_left, RIGHT[1:]), moved(rows_right, LEFT[1:])
    down_other, pre_other = swapped(down_send), swapped(pre_send)
    from_left, from_right, down_other, pre_other, up_send, head = together(
        from_left, from_right, down_other, pre_other, up_send, head
    )

    def hidden(where, rows):
        send, keep, routes = hidden_sums(where, rows, w_down, down_other)
        return routes, keep, swapped(send)

    def finish(where, sums, dtype):
        return expert_sums(where, *sums, pre, pre_other, w_up, up_other, dtype)

    far, end = place(far_block), place(end_block)
    rows_far = jnp.where(me >= 2, from_left, from_right)
    rows_end = moved(rows_far, [(2, 3), (1, 0)])
    up_other = swapped(up_send)
    routes, keep, got = hidden(near, [rows_own, rows_left, rows_right])
    next_head = moved(head, LEFT[:2])
    rows_end, rows_far, keep, up_other, conv_own, next_head = together(
        rows_end, rows_far, keep, up_other, conv_own, next_head
    )

    conv_left, conv_right = moved(conv_own, RIGHT), moved(conv_own, LEFT)
    end_hidden = hidden(end, [rows_end])
    far_routes, far_keep, far_got = hidden(far, [rows_far])
    end_sums = finish(end, end_hidden, BF16)
    next_head = moved(next_head, LEFT[1:])
    conv_right, end_sums, keep, far_keep, next_head = together(conv_right, end_sums, keep, far_keep, next_head)

    from_left, from_right = moved(conv_left, RIGHT[1:]), moved(conv_right, LEFT[1:])
    back_end = moved(end_sums, [(0, 1), (3, 2)])
    gather = [(e * 2 + 1 - e // 2, e * 2 + e // 2) for e in range(experts)]

    def proj(where, grads, heads, *inputs):
        send, keep, *tap_terms = proj_sums(where, grads, heads, taps, w_proj, *inputs)
        return keep, lax.ppermute(send, ("expert", "mp"), gather), *tap_terms

    near_proj, near_proj_got, tap_terms = proj(
        near, [conv_own, conv_left, conv_right], [conv_right, conv_own, next_head], conv_input[0]
    )
    far_sums = finish(far, (far_routes, far_keep, far_got), F32)
    from_left, from_right, near_proj, conv_left, keep, far_sums = together(
        from_left, from_right, near_proj, conv_left, keep, far_sums
    )

    conv_far = jnp.where(me >= 2, from_left, from_right)
    conv_far, back_end = together(conv_far, back_end)
    conv_end = moved(conv_far, [(2, 3), (1, 0)])
    back = (far_sums + back_end.astype(F32)).astype(BF16)
    back_right, back_left = moved(back, RIGHT[:2]), moved(back, LEFT[:2])
    near_sums = finish(near, (routes, keep, got), F32)
    conv_end, back_right, back_left, near_sums = together(conv_end, back_right, back_left, near_sums)

    to_right, to_left, own = combined(near, out_grad[0], near_sums, back_right, back_left, near_proj, near_proj_got)
    to_right, to_left, conv_end = together(to_right, to_left, conv_end)
    to_right, to_left = moved(to_right, RIGHT), moved(to_left, LEFT)
    far_head = jnp.where(me >= 2, conv_left[:HEAD], conv_end[:HEAD])
    proj_keep, proj_got = proj(place(far_block, end_block), [conv_far, conv_end], [far_head, conv_far])
    to_right, to_left, proj_keep = together(to_right, to_left, proj_keep)

    residual = (own + to_right.astype(F32) + to_left.astype(F32)).astype(BF16)
    sections, cores = lax.axis_size("section"), lax.axis_size("mp")

    def deliver(keep, got, pairs):
        def at(s, e, m):
            return (s * experts + e) * cores + m

        moves = [(at(s, e, e // 2), at(s - 1, d, e // 2)) for s in range(1, sections) for e, d in pairs]
        return lax.ppermute((keep + got.astype(F32)).astype(BF16), ("section", "expert", "mp"), moves)

    residual = shifted(residual, "section", -1)
    far_piece = deliver(proj_keep[:tok_rows], proj_got[:tok_rows], [(e, (e + 2) % experts) for e in range(experts)])
    end_piece = deliver(proj_keep[tok_rows:], proj_got[tok_rows:], [(0, experts - 1), (experts - 1, 0)])
    tap_grads = doubling_sum(tap_terms, "expert")
    residual = final_sum(near, residual, far_piece, end_piece)
    return (residual[None], tap_grads[None])


def shards(*arrays):
    experts, halves = lax.axis_size("expert"), lax.axis_size("mp")
    capacity = arrays[5].shape[2] // experts
    dense = capacity == arrays[0].shape[1] and experts == 4 and halves == 2
    return (token_plan if dense else slot_plan)(*arrays)


def solution(mesh):
    in_specs = (
        P("section", "expert", "mp"),
        P("section", "expert", None),
        P("section", "expert", None),
        P("section", "expert", None, "mp"),
        P("section", "expert", "mp", None),
        P("section", "expert", None, "mp"),
        P("section", "expert", "mp"),
        P("section", "expert", "mp"),
        P("section", None, "mp"),
        P("section", "expert", "mp"),
    )
    out_specs = (P("section", "expert", "mp"), P("section", None, "mp"))
    return jax.shard_map(shards, mesh=mesh, in_specs=in_specs, out_specs=out_specs, check_vma=False)
```

```python
import functools

import jax
import jax.numpy as jnp
from jax import lax
from jax.experimental import pallas as pl
from jax.experimental.pallas import tpu as pltpu
from jax.sharding import PartitionSpec as P


def shifted(array, axis, by):
    size = lax.axis_size(axis)
    pairs = [(i, i + by) for i in range(size) if 0 <= i + by < size]
    return lax.ppermute(array, axis, pairs)


def silu_slope(pre_value):
    sig = jax.nn.sigmoid(pre_value)
    return sig * (1.0 + pre_value * (1.0 - sig))


def gated_rows(gates, rows, tok_rows):
    scaled = (gates[:, :, None] * rows.astype(jnp.float32)[:, None, :]).astype(jnp.bfloat16)
    return scaled.reshape(tok_rows * 2, rows.shape[1])


def fill_buffer(scaled, target, experts, capacity):
    width = scaled.shape[1]
    buffer = jnp.zeros((experts * capacity, width), jnp.bfloat16).at[target].set(scaled)
    return buffer.reshape(experts, capacity, width)


def slot_plan(
    out_grad,
    expert_ids,
    gate_codes,
    up_weight,
    down_weight,
    pre_act,
    conv_grad,
    conv_input,
    conv_weight,
    in_proj,
):
    grad_rows = out_grad[0]
    route_ids = expert_ids[0]
    tok_rows = grad_rows.shape[0]
    experts = lax.axis_size("expert")
    capacity = pre_act.shape[2] // experts
    gates = gate_codes[0].astype(jnp.float32) / 256.0
    flat_ids = route_ids.reshape(tok_rows * 2)
    onehot = (flat_ids[:, None] == jnp.arange(experts, dtype=jnp.int32)[None, :]).astype(jnp.int32)
    before = jnp.cumsum(onehot, axis=0) - onehot
    position = jnp.sum(before * onehot, axis=1)
    target = flat_ids * capacity + position
    whole_rows = lax.all_gather(grad_rows, "mp", axis=1, tiled=True)
    buffer = fill_buffer(gated_rows(gates, whole_rows, tok_rows), target, experts, capacity)
    arrived = lax.all_to_all(buffer, "expert", split_axis=0, concat_axis=0, tiled=True)
    slot_rows = arrived.reshape(experts * capacity, whole_rows.shape[1])
    w_down = down_weight[0, 0]
    w_up = up_weight[0, 0]
    pre_slots = pre_act[0, 0].astype(jnp.float32)
    hidden = lax.dot_general(
        slot_rows, w_down, (((1,), (1,)), ((), ())), preferred_element_type=jnp.float32
    )
    pre_grad = (hidden * silu_slope(pre_slots)).astype(jnp.bfloat16)
    partial_value = lax.dot_general(
        pre_grad, w_up, (((1,), (1,)), ((), ())), preferred_element_type=jnp.float32
    )
    share = lax.psum_scatter(partial_value, "mp", scatter_dimension=1, tiled=True).astype(
        jnp.bfloat16
    )
    returned = lax.all_to_all(
        share.reshape(experts, capacity, share.shape[1]),
        "expert",
        split_axis=0,
        concat_axis=0,
        tiled=True,
    )
    picked = returned.reshape(experts * capacity, grad_rows.shape[1])[target]
    picked = picked.astype(jnp.float32).reshape(tok_rows, 2, grad_rows.shape[1])
    moe_total = grad_rows.astype(jnp.float32) + picked[:, 0, :] + picked[:, 1, :]
    grads_here = conv_grad[0]
    inputs_here = conv_input[0]
    taps = conv_weight[0]
    kernel_size = taps.shape[0]
    next_rows = shifted(grads_here[: kernel_size - 1], "expert", -1)
    prev_rows = shifted(inputs_here[tok_rows - kernel_size + 1 :], "expert", 1)
    grad_ext = jnp.concatenate([grads_here, next_rows], axis=0).astype(jnp.float32)
    input_ext = jnp.concatenate([prev_rows, inputs_here], axis=0).astype(jnp.float32)
    grad_local = grads_here.astype(jnp.float32)
    conv_result = jnp.zeros(grads_here.shape, jnp.float32)
    tap_terms = []
    for tap in range(kernel_size):
        start = kernel_size - 1 - tap
        conv_result = conv_result + taps[tap][None, :] * grad_ext[start : start + tok_rows]
        tap_terms.append(jnp.sum(grad_local * input_ext[tap : tap + tok_rows], axis=0))
    input_grad = conv_result.astype(jnp.bfloat16)
    tap_grads = lax.psum(jnp.stack(tap_terms), "expert")
    w_proj = in_proj[0]
    proj_partial = lax.dot_general(
        input_grad,
        lax.all_gather(w_proj, "expert", axis=0, tiled=True),
        (((1,), (1,)), ((), ())),
        preferred_element_type=jnp.float32,
    )
    proj_share = lax.psum_scatter(proj_partial, "mp", scatter_dimension=1, tiled=True)
    residual = (moe_total + proj_share).astype(jnp.bfloat16)
    sent_residual = shifted(residual, "section", -1)
    return (sent_residual[None], tap_grads[None])


F32, BF16 = jnp.float32, jnp.bfloat16
VMEM_LIMIT = 14 * 1024 * 1024
HEAD = 16
LANES = 128
RIGHT = [(0, 1), (1, 2), (2, 3)]
LEFT = [(3, 2), (2, 1), (1, 0)]
NT = (((1,), (1,)), ((), ()))
TN = (((0,), (0,)), ((), ()))


def whole(memory=pltpu.VMEM):
    return pl.BlockSpec(memory_space=memory)


def rotated(array, axis, by):
    size = lax.axis_size(axis)
    return lax.ppermute(array, axis, [(i, (i + by) % size) for i in range(size)])


def around(array):
    return [array] + [rotated(array, "expert", k) for k in range(1, lax.axis_size("expert"))]


def doubling_sum(array, axis):
    size, step = lax.axis_size(axis), 1
    while step < size:
        array = array + lax.ppermute(array, axis, [(i, i ^ step) for i in range(size)])
        step *= 2
    return array


def params():
    return pltpu.CompilerParams(vmem_limit_bytes=VMEM_LIMIT)


def cost(flops, bytes_accessed):
    return pl.CostEstimate(flops=8 * flops, bytes_accessed=8 * bytes_accessed, transcendentals=0)


def square(size):
    row = lax.broadcasted_iota(jnp.int32, (size, size), 0)
    return row, lax.broadcasted_iota(jnp.int32, (size, size), 1)


def routing(columns, me):
    values = columns.astype(F32)
    named = jnp.where(values[:, 0:2] == me.astype(F32), 1.0, 0.0)
    gate = jnp.sum(named * values[:, 2:4], axis=1, keepdims=True) / 256.0
    return jnp.sum(named, axis=1, keepdims=True), gate


def hidden_kernel(count, place, *refs):
    routes, rows = refs[:count], refs[count : 2 * count]
    down_own, down_other, send, keep, handed, gates, scaled = refs[2 * count :]
    tok_rows = rows[0].shape[0]
    units = down_own.shape[0]
    step = pl.program_id(0)

    @pl.when(step == 0)
    def _():
        for k in range(count):
            at = pl.ds(k * tok_rows, tok_rows)
            gates[at, :] = routing(routes[k][...], place[1])[1]
            handed[at, :] = routes[k][...]
        keep[...] = jnp.zeros_like(keep)

    for k in range(count):
        at = pl.ds(k * tok_rows, tok_rows)
        scaled[at, :] = (gates[at, :] * rows[k][...].astype(F32)).astype(BF16)
    keep[:, :units] += lax.dot_general(scaled[...], down_own[...], NT, preferred_element_type=F32)
    keep[:, units:] += lax.dot_general(scaled[...], down_other[...], NT, preferred_element_type=F32)

    @pl.when(step == pl.num_programs(0) - 1)
    def _():
        send[...] = keep[...].astype(BF16)


def route_columns(rows):
    tok_rows, width = rows.shape
    return pl.BlockSpec((tok_rows, LANES), lambda i, place: (0, width // LANES - 1))


def hidden_sums(place, rows, down, down_other):
    count = len(rows)
    tok_rows = rows[0].shape[0]
    units, half_width = down_other.shape
    tokens = count * tok_rows
    chunk = half_width // 4
    return pl.pallas_call(
        functools.partial(hidden_kernel, count),
        grid_spec=pltpu.PrefetchScalarGridSpec(
            num_scalar_prefetch=1,
            grid=(4,),
            in_specs=[route_columns(rows[0])] * count
            + [pl.BlockSpec((tok_rows, chunk), lambda i, place: (0, i))] * count
            + [
                pl.BlockSpec((units, chunk), lambda i, place: (0, 4 * place[0] + i)),
                pl.BlockSpec((units, chunk), lambda i, place: (0, i)),
            ],
            out_specs=[pl.BlockSpec((tokens, 2 * units), lambda i, place: (0, 0))] * 2
            + [pl.BlockSpec((tokens, LANES), lambda i, place: (0, 0))],
            scratch_shapes=[pltpu.VMEM((tokens, 1), F32), pltpu.VMEM((tokens, chunk), BF16)],
        ),
        out_shape=[jax.ShapeDtypeStruct((tokens, 2 * units), dtype) for dtype in (BF16, F32)]
        + [jax.ShapeDtypeStruct((tokens, LANES), BF16)],
        compiler_params=params(),
        cost_estimate=cost(4 * tokens * half_width * units, 4 * units * half_width + 2 * tokens * half_width),
        name="hidden",
    )(place, *rows, *rows, down, down_other)


def finish_kernel(count, place, routes, keep, got, pre_own, pre_other, up_own, up_other, out, pre_grad):
    tok_rows = pre_grad.shape[0] // count
    units = pre_own.shape[1]

    @pl.when(pl.program_id(0) == 0)
    def _():
        row, column = square(tok_rows)
        for k in range(count):
            at = pl.ds(k * tok_rows, tok_rows)
            named, _ = routing(routes[at, :], place[1])
            rank = jnp.sum(jnp.where(row < column, named, 0.0), axis=0, keepdims=True).astype(jnp.int32)
            named = jnp.sum(jnp.where(row == column, named, 0.0), axis=0, keepdims=True)
            pick = jnp.where(rank == row, named, 0.0).astype(BF16)
            slots = pl.ds(pl.multiple_of(place[2 + k] * tok_rows, tok_rows), tok_rows)
            for side, pre in enumerate((pre_own, pre_other)):
                here = pl.ds(side * units, units)
                p = lax.dot_general(pick, pre[slots, :], TN, preferred_element_type=F32)
                q = 1.0 / (1.0 + jnp.exp(-p))
                hidden = keep[at, here] + got[at, pl.ds((1 - side) * units, units)].astype(F32)
                pre_grad[at, here] = (hidden * (q * (1.0 + p * (1.0 - q)))).astype(BF16)

    value = lax.dot_general(pre_grad[:, :units], up_own[...], NT, preferred_element_type=F32)
    value += lax.dot_general(pre_grad[:, units:], up_other[...], NT, preferred_element_type=F32)
    out[...] = value.astype(out.dtype)


def expert_sums(place, routes, keep, got, pre, pre_other, up, up_other, dtype):
    tokens = keep.shape[0]
    count = place.shape[0] - 2
    units = pre.shape[1]
    half_width = up_other.shape[0]
    chunk = half_width // 4
    return pl.pallas_call(
        functools.partial(finish_kernel, count),
        grid_spec=pltpu.PrefetchScalarGridSpec(
            num_scalar_prefetch=1,
            grid=(4,),
            in_specs=[whole()] * 5
            + [
                pl.BlockSpec((chunk, units), lambda i, place: (4 * place[0] + i, 0)),
                pl.BlockSpec((chunk, units), lambda i, place: (i, 0)),
            ],
            out_specs=pl.BlockSpec((tokens, chunk), lambda i, place: (0, i)),
            scratch_shapes=[pltpu.VMEM((tokens, 2 * units), BF16)],
        ),
        out_shape=jax.ShapeDtypeStruct((tokens, half_width), dtype),
        compiler_params=params(),
        cost_estimate=cost(4 * tokens * half_width * units, 4 * units * half_width + 4 * tokens * half_width),
        name="experts",
    )(place, routes, keep, got, pre, pre_other, up, up_other)


def proj_kernel(count, with_taps, place, *refs):
    grads, heads = refs[:count], refs[count : 2 * count]
    taps, weight = refs[2 * count : 2 * count + 2]
    refs = refs[2 * count + 2 :]
    if with_taps:
        inputs, send, keep, tap_out, ext, scaled = refs
    else:
        send, keep, ext, scaled = refs
    tok_rows, chunk = grads[0].shape
    kernel_size = taps.shape[0]
    step = pl.program_id(0)

    tap = taps[...]
    for k in range(count):
        ext[:tok_rows, :] = grads[k][...].astype(F32)
        follows = (place[2 + k] < lax.axis_size("expert") - 1).astype(F32)
        ext[tok_rows:, :] = heads[k][...].astype(F32) * follows
        result = jnp.zeros((tok_rows, chunk), F32)
        for j in range(kernel_size):
            start = kernel_size - 1 - j
            result = result + tap[j : j + 1, :] * ext[start : start + tok_rows, :]
        scaled[k * tok_rows : (k + 1) * tok_rows, :] = result.astype(BF16)
        if with_taps and k == 0:
            values = inputs[...].astype(F32)
            for j in range(kernel_size):
                start = kernel_size - 1 - j
                terms = values * ext[start : start + tok_rows, :]
                tap_out[j : j + 1, :] = jnp.sum(terms, axis=0, keepdims=True)

    product = lax.dot_general(scaled[...], weight[...], NT, preferred_element_type=F32)

    @pl.when(step == 0)
    def _():
        keep[...] = product

    @pl.when(step > 0)
    def _():
        keep[...] += product

    @pl.when(step == pl.num_programs(0) - 1)
    def _():
        send[...] = keep[...].astype(BF16)


def proj_sums(place, grads, heads, taps, weight, inputs=None):
    count = len(grads)
    tok_rows, half_width = grads[0].shape
    block = weight.shape[0]
    tokens = count * tok_rows
    chunk = half_width // 4
    with_taps = inputs is not None

    def wide(rows):
        return pl.BlockSpec((rows, chunk), lambda i: (0, i))

    last = [wide(tok_rows)] if with_taps else []
    out_specs = [pl.BlockSpec((tokens, block), lambda i: (0, 0))] * 2
    out_shape = [jax.ShapeDtypeStruct((tokens, block), BF16), jax.ShapeDtypeStruct((tokens, block), F32)]
    if with_taps:
        out_specs = out_specs + [wide(taps.shape[0])]
        out_shape = out_shape + [jax.ShapeDtypeStruct(taps.shape, F32)]
    return pl.pallas_call(
        functools.partial(proj_kernel, count, with_taps),
        grid=(half_width // chunk,),
        in_specs=[whole(pltpu.SMEM)]
        + [wide(tok_rows)] * count
        + [wide(HEAD)] * count
        + [wide(taps.shape[0]), wide(block)]
        + last,
        out_specs=out_specs,
        out_shape=out_shape,
        scratch_shapes=[pltpu.VMEM((tok_rows + HEAD, chunk), F32), pltpu.VMEM((tokens, chunk), BF16)],
        compiler_params=params(),
        cost_estimate=cost(
            2 * tokens * half_width * block, 2 * (block + tokens) * half_width + 6 * tokens * block
        ),
        name="projection",
    )(place, *grads, *heads, taps, weight, *([inputs] if with_taps else []))


def combine_kernel(place, grad, sums, back_right, back_left, proj_keep, proj_got, to_right, to_left, own, total):
    half, me = place[0], place[1]
    rows, part = grad.shape[0], proj_keep.shape[1]
    total[0:rows, :] = grad[...].astype(F32) + sums[0:rows, :]
    total[rows : 2 * rows, :] = sums[rows : 2 * rows, :] + back_left[...].astype(F32)
    total[2 * rows :, :] = sums[2 * rows :, :] + back_right[...].astype(F32)

    @pl.when(me // 2 == half)
    def _():
        at = pl.ds(pl.multiple_of(lax.rem(me, 2) * part, part), part)
        total[:, at] += proj_keep[...] + proj_got[...].astype(F32)

    own[...] = total[0:rows, :]
    to_left[...] = total[rows : 2 * rows, :].astype(BF16)
    to_right[...] = total[2 * rows :, :].astype(BF16)


def combined(place, grad, sums, *arrays):
    outs = [jax.ShapeDtypeStruct(grad.shape, dtype) for dtype in (BF16, BF16, F32)]
    return pl.pallas_call(
        combine_kernel,
        in_specs=[whole(pltpu.SMEM)] + [whole()] * (2 + len(arrays)),
        out_specs=[whole()] * 3,
        out_shape=outs,
        scratch_shapes=[pltpu.VMEM(sums.shape, F32)],
        compiler_params=params(),
        cost_estimate=cost(8 * grad.size, 40 * grad.size),
        name="combine",
    )(place, grad, sums, *arrays)


def final_kernel(place, residual, far, end, out, total):
    half, me = place[0], place[1]
    experts = lax.axis_size("expert")
    part = far.shape[1]
    total[...] = residual[...].astype(F32)

    def add(source, value):
        @pl.when((source < experts) & (source // 2 == half))
        def _():
            at = pl.ds(pl.multiple_of(lax.rem(source, 2) * part, part), part)
            total[:, at] += value[...].astype(F32)

    add(lax.rem(me + 2, experts), far)
    add(jnp.where(lax.rem(me, experts - 1) == 0, experts - 1 - me, experts), end)
    out[...] = total[...].astype(BF16)


def final_sum(place, residual, far, end):
    return pl.pallas_call(
        final_kernel,
        in_specs=[whole(pltpu.SMEM)] + [whole()] * 3,
        out_specs=whole(),
        out_shape=jax.ShapeDtypeStruct(residual.shape, BF16),
        scratch_shapes=[pltpu.VMEM(residual.shape, F32)],
        compiler_params=params(),
        cost_estimate=cost(4 * residual.size, 8 * residual.size),
        name="residual",
    )(place, residual, far, end)


def moved(array, pairs):
    return lax.ppermute(array, "expert", pairs)


def swapped(array):
    return rotated(array, "mp", 1)


def together(*arrays):
    return lax.optimization_barrier(arrays)


def token_plan(
    out_grad,
    expert_ids,
    gate_codes,
    up_weight,
    down_weight,
    pre_act,
    conv_grad,
    conv_input,
    conv_weight,
    in_proj,
):
    me, half = lax.axis_index("expert"), lax.axis_index("mp")
    experts = lax.axis_size("expert")

    def place(*blocks):
        return jnp.stack([half, me, *blocks]).astype(jnp.int32)

    far_block, end_block = (me + 2) % experts, jnp.where(me == 0, experts - 1, 0)
    near = place(me, jnp.maximum(me - 1, 0), jnp.minimum(me + 1, experts - 1))
    rows_own, conv_own = out_grad[0], conv_grad[0]
    tok_rows, half_width = rows_own.shape
    w_down, w_up, pre = down_weight[0, 0], up_weight[0, 0], pre_act[0, 0]
    taps, w_proj = conv_weight[0], in_proj[0]

    routes = jnp.concatenate([expert_ids[0], gate_codes[0]], axis=1).astype(BF16)
    rows_own = jnp.concatenate([rows_own, jnp.pad(routes, ((0, 0), (0, LANES - routes.shape[1])))], axis=1)
    rows_left, rows_right = moved(rows_own, RIGHT), moved(rows_own, LEFT)
    down_send = lax.dynamic_slice_in_dim(w_down, (1 - half) * half_width, half_width, 1)
    up_send = lax.dynamic_slice_in_dim(w_up, (1 - half) * half_width, half_width, 0)
    rows_left, rows_right, down_send, up_send, pre_send, head = together(
        rows_left, rows_right, down_send, up_send, pre, conv_own[:HEAD]
    )

    from_left, from_right = moved(rows_left, RIGHT[1:]), moved(rows_right, LEFT[1:])
    down_other, pre_other = swapped(down_send), swapped(pre_send)
    from_left, from_right, down_other, pre_other, up_send, head = together(
        from_left, from_right, down_other, pre_other, up_send, head
    )

    def hidden(where, rows):
        send, keep, routes = hidden_sums(where, rows, w_down, down_other)
        return routes, keep, swapped(send)

    def finish(where, sums, dtype):
        return expert_sums(where, *sums, pre, pre_other, w_up, up_other, dtype)

    far, end = place(far_block), place(end_block)
    rows_far = jnp.where(me >= 2, from_left, from_right)
    rows_end = moved(rows_far, [(2, 3), (1, 0)])
    up_other = swapped(up_send)
    routes, keep, got = hidden(near, [rows_own, rows_left, rows_right])
    next_head = moved(head, LEFT[:2])
    rows_end, rows_far, keep, up_other, conv_own, next_head = together(
        rows_end, rows_far, keep, up_other, conv_own, next_head
    )

    conv_left, conv_right = moved(conv_own, RIGHT), moved(conv_own, LEFT)
    end_hidden = hidden(end, [rows_end])
    far_routes, far_keep, far_got = hidden(far, [rows_far])
    end_sums = finish(end, end_hidden, BF16)
    next_head = moved(next_head, LEFT[1:])
    conv_right, end_sums, keep, far_keep, next_head = together(conv_right, end_sums, keep, far_keep, next_head)

    from_left, from_right = moved(conv_left, RIGHT[1:]), moved(conv_right, LEFT[1:])
    back_end = moved(end_sums, [(0, 1), (3, 2)])
    gather = [(e * 2 + 1 - e // 2, e * 2 + e // 2) for e in range(experts)]

    def proj(where, grads, heads, *inputs):
        send, keep, *tap_terms = proj_sums(where, grads, heads, taps, w_proj, *inputs)
        return keep, lax.ppermute(send, ("expert", "mp"), gather), *tap_terms

    near_proj, near_proj_got, tap_terms = proj(
        near, [conv_own, conv_left, conv_right], [conv_right, conv_own, next_head], conv_input[0]
    )
    far_sums = finish(far, (far_routes, far_keep, far_got), F32)
    from_left, from_right, near_proj, conv_left, keep, far_sums = together(
        from_left, from_right, near_proj, conv_left, keep, far_sums
    )

    conv_far = jnp.where(me >= 2, from_left, from_right)
    conv_far, back_end = together(conv_far, back_end)
    conv_end = moved(conv_far, [(2, 3), (1, 0)])
    back = (far_sums + back_end.astype(F32)).astype(BF16)
    back_right, back_left = moved(back, RIGHT[:2]), moved(back, LEFT[:2])
    near_sums = finish(near, (routes, keep, got), F32)
    back_right, back_left, near_sums = together(back_right, back_left, near_sums)

    to_right, to_left, own = combined(near, out_grad[0], near_sums, back_right, back_left, near_proj, near_proj_got)
    to_right, to_left, conv_far = together(to_right, to_left, conv_far)
    to_right, to_left = moved(to_right, RIGHT), moved(to_left, LEFT)
    far_head = jnp.where(me >= 2, conv_left[:HEAD], conv_end[:HEAD])
    proj_keep, proj_got = proj(place(far_block, end_block), [conv_far, conv_end], [far_head, conv_far])
    to_right, to_left, proj_keep = together(to_right, to_left, proj_keep)

    residual = (own + to_right.astype(F32) + to_left.astype(F32)).astype(BF16)
    sections, cores = lax.axis_size("section"), lax.axis_size("mp")

    def deliver(keep, got, pairs):
        def at(s, e, m):
            return (s * experts + e) * cores + m

        moves = [(at(s, e, e // 2), at(s - 1, d, e // 2)) for s in range(1, sections) for e, d in pairs]
        return lax.ppermute((keep + got.astype(F32)).astype(BF16), ("section", "expert", "mp"), moves)

    residual = shifted(residual, "section", -1)
    far_piece = deliver(proj_keep[:tok_rows], proj_got[:tok_rows], [(e, (e + 2) % experts) for e in range(experts)])
    end_piece = deliver(proj_keep[tok_rows:], proj_got[tok_rows:], [(0, experts - 1), (experts - 1, 0)])
    tap_grads = doubling_sum(tap_terms, "expert")
    residual = final_sum(near, residual, far_piece, end_piece)
    return (residual[None], tap_grads[None])


def shards(*arrays):
    experts, halves = lax.axis_size("expert"), lax.axis_size("mp")
    capacity = arrays[5].shape[2] // experts
    dense = capacity == arrays[0].shape[1] and experts == 4 and halves == 2
    return (token_plan if dense else slot_plan)(*arrays)


def solution(mesh):
    in_specs = (
        P("section", "expert", "mp"),
        P("section", "expert", None),
        P("section", "expert", None),
        P("section", "expert", None, "mp"),
        P("section", "expert", "mp", None),
        P("section", "expert", None, "mp"),
        P("section", "expert", "mp"),
        P("section", "expert", "mp"),
        P("section", None, "mp"),
        P("section", "expert", "mp"),
    )
    out_specs = (P("section", "expert", "mp"), P("section", None, "mp"))
    return jax.shard_map(shards, mesh=mesh, in_specs=in_specs, out_specs=out_specs, check_vma=False)
```
